256 devices in a mesh: ctx: 32 (over z, y_lo, core), resp: 8 (over x, y_hi).
Axes of the slice: x: 4, y: 4 (y_hi: 2, y_lo: 2; y = y_hi * 2 + y_lo), z: 8, core: 2. Of those that a mesh axis runs over, the one named last changes fastest.
Arguments:
- prompt_q: bfloat16 [4096, 8192], P('ctx', 'resp'), may hold values from -4.5 to 4.5
- prompt_k: bfloat16 [4096, 1024], P('ctx', 'resp'), may hold values from -4.5 to 4.5
- prompt_v: bfloat16 [4096, 1024], P('ctx', 'resp'), may hold values from -6 to 6
- prompt_out: bfloat16 [4096, 8192], P('ctx', 'resp'), may hold values from -3 to 3
- prompt_dout: bfloat16 [4096, 8192], P('ctx', 'resp'), may hold values from -1.5 to 1.5
- resp_q: bfloat16 [4096, 8192], P(('ctx', 'resp')), may hold values from -4.5 to 4.5
- resp_k: bfloat16 [4096, 1024], P(('ctx', 'resp')), may hold values from -6 to 6
- resp_v: bfloat16 [4096, 1024], P(('ctx', 'resp')), may hold values from -6 to 6
- resp_out: bfloat16 [4096, 8192], P(('ctx', 'resp')), may hold values from -3 to 3
- resp_dout: bfloat16 [4096, 8192], P(('ctx', 'resp')), may hold values from -1.5 to 1.5
- lengths: int32 [16], replicated, may hold values from 1 to 128, as said below
- resp_row: int32 [16], replicated, may hold values from 0 to 31
- block_index: int32 [32], replicated, may hold values from 0 to 31, each once
Outputs:
- prompt_dq: bfloat16 [4096, 8192], P('ctx', 'resp')
- prompt_dk: bfloat16 [4096, 1024], P('ctx', 'resp')
- prompt_dv: bfloat16 [4096, 1024], P('ctx', 'resp')
- resp_dq: bfloat16 [4096, 8192], P(('ctx', 'resp'))
- resp_dk: bfloat16 [4096, 1024], P(('ctx', 'resp'))
- resp_dv: bfloat16 [4096, 1024], P(('ctx', 'resp'))
The draws below stay inside these ranges and needn't reach their ends.
Inputs may be any that keep to these rules, and one draw needn't show every extreme that they name: `lengths`: the responses named to one index of ctx lie in its 128 slots one after another in order of their number from its first slot, and together fill exactly 128 slots; an index named by no response holds none.
All inputs are finite; a program needn't handle non-finite values.
Results may differ from the reference program's by a relative error of at most 0.005.
Values may be sent and summed in bfloat16 or wider, within the bound.
A program may use at most 64 MiB of HBM per device.

```python
import math
import jax
import jax.numpy as jnp
from jax import lax

HEAD_DIM = 128
Q_HEADS = 64
KV_HEADS = 8
BLOCK = 128
ROW_TOK = 128
RESPONSES = 16
PROMPT = 4096
SLOTS = 4096
N_CTX = 32


def response_layout(key):
    key = jax.random.fold_in(key, 101)
    key_rows, key_weights = jax.random.split(key, 2)
    number = jnp.arange(RESPONSES, dtype=jnp.int32)
    drawn_rows = jax.random.randint(key_rows, (RESPONSES,), 0, N_CTX - 1, dtype=jnp.int32)
    chosen_rows = jnp.where(number == 0, N_CTX - 1, jnp.where(number <= 2, 0, drawn_rows)).astype(jnp.int32)
    drawn_weights = jax.random.randint(key_weights, (RESPONSES,), 1, 9, dtype=jnp.int32)
    weights = jnp.where(number == 2, 0, drawn_weights).astype(jnp.int32)
    same_row = chosen_rows[:, None] == chosen_rows[None, :]
    weight_total = jnp.sum(jnp.where(same_row, weights[None, :], 0), axis=1).astype(jnp.int32)
    row_count = jnp.sum(same_row.astype(jnp.int32), axis=1).astype(jnp.int32)
    base_len = (1 + weights * (ROW_TOK - row_count) // jnp.maximum(weight_total, 1)).astype(jnp.int32)
    filled = jnp.sum(jnp.where(same_row, base_len[None, :], 0), axis=1).astype(jnp.int32)
    leading = jnp.sum((same_row & (number[None, :] < number[:, None])).astype(jnp.int32), axis=1) == 0
    lengths = (base_len + jnp.where(leading, ROW_TOK - filled, 0)).astype(jnp.int32)
    return (lengths, chosen_rows)


def draw_lengths(key, part):
    return response_layout(key)[0]


def draw_resp_row(key, part):
    return response_layout(key)[1]


def draw_prompt_q(key, part):
    key = jax.random.fold_in(key, 1)
    base_draw = jnp.clip(jax.random.normal(key, (PROMPT, Q_HEADS * HEAD_DIM), jnp.float32), -4.5, 4.5)
    return base_draw.astype(jnp.bfloat16)


def draw_prompt_k(key, part):
    key = jax.random.fold_in(key, 2)
    base_draw = jnp.clip(jax.random.normal(key, (PROMPT, KV_HEADS * HEAD_DIM), jnp.float32), -4.5, 4.5)
    return base_draw.astype(jnp.bfloat16)


def draw_resp_q(key, part):
    key = jax.random.fold_in(key, 3)
    base_draw = jnp.clip(jax.random.normal(key, (SLOTS, Q_HEADS * HEAD_DIM), jnp.float32), -4.5, 4.5)
    return base_draw.astype(jnp.bfloat16)


def levels(key, dims, cuts, low, top_value):
    def one(axis_at, shards_of):
        steps = jax.random.uniform(jax.random.fold_in(jax.random.fold_in(key, 6), axis_at), (shards_of,), jnp.float32, low / len(cuts), top_value / len(cuts))
        return jnp.repeat(jnp.exp(steps), dims[axis_at] // shards_of).reshape((-1,) + (1,) * (len(dims) - axis_at - 1))

    gain = one(*cuts[0])
    for cut in cuts[1:]:
        gain = gain * one(*cut)
    return gain


def centred(stream_key, extent, scale, limit, pieces=(), kind=jnp.bfloat16):
    values = jax.random.normal(stream_key, extent, jnp.float32) * scale
    if len(pieces) > 0:
        values = levels(stream_key, extent, pieces, -0.22, 0.18) * values
    return jnp.clip(values, min=-limit, max=limit).astype(kind)


def setup_inputs(seed: int = 0) -> dict:
    key_of = jax.random.split(jax.random.key(seed), 14)
    prompt_q = draw_prompt_q(jax.random.fold_in(key_of[13], 71), 0)
    prompt_k = draw_prompt_k(jax.random.fold_in(key_of[13], 71), 0)
    prompt_v = centred(key_of[2], (PROMPT, KV_HEADS * HEAD_DIM), 1.0, 6.0, ((0, 32), (1, 8)))
    prompt_out = centred(key_of[3], (PROMPT, Q_HEADS * HEAD_DIM), 0.3, 3.0, ((0, 32), (1, 8)))
    prompt_dout = centred(key_of[4], (PROMPT, Q_HEADS * HEAD_DIM), 0.25, 1.5, ((0, 32), (1, 8)))
    resp_q = draw_resp_q(jax.random.fold_in(key_of[13], 71), 0)
    resp_k = centred(key_of[6], (SLOTS, KV_HEADS * HEAD_DIM), 1.0, 6.0, ((0, 256),))
    resp_v = centred(key_of[7], (SLOTS, KV_HEADS * HEAD_DIM), 1.0, 6.0, ((0, 256),))
    resp_out = centred(key_of[8], (SLOTS, Q_HEADS * HEAD_DIM), 0.3, 3.0, ((0, 256),))
    resp_dout = centred(key_of[9], (SLOTS, Q_HEADS * HEAD_DIM), 0.25, 1.5, ((0, 256),))
    lengths = draw_lengths(jax.random.fold_in(key_of[13], 71), 0)
    resp_row = draw_resp_row(jax.random.fold_in(key_of[13], 71), 0)
    block_index = jax.random.permutation(key_of[12], N_CTX).astype(jnp.int32)
    return {"prompt_q": prompt_q, "prompt_k": prompt_k, "prompt_v": prompt_v, "prompt_out": prompt_out, "prompt_dout": prompt_dout, "resp_q": resp_q, "resp_k": resp_k, "resp_v": resp_v, "resp_out": resp_out, "resp_dout": resp_dout, "lengths": lengths, "resp_row": resp_row, "block_index": block_index}


def token_layout(lengths, resp_row, block_index):
    number = jnp.arange(RESPONSES, dtype=jnp.int32)
    same_row = resp_row[:, None] == resp_row[None, :]
    earlier = same_row & (number[None, :] < number[:, None])
    first_slot = jnp.sum(jnp.where(earlier, lengths[None, :], 0), axis=1).astype(jnp.int32)
    slot_ids = jnp.arange(SLOTS, dtype=jnp.int32)
    row_ids = slot_ids // ROW_TOK
    offset = slot_ids % ROW_TOK
    member = (resp_row[:, None] == row_ids[None, :]) & (offset[None, :] >= first_slot[:, None]) & (offset[None, :] < first_slot[:, None] + lengths[:, None])
    slot_owner = jnp.where(jnp.any(member, axis=0), jnp.sum(jnp.where(member, number[:, None], 0), axis=0), -2).astype(jnp.int32)
    slot_place = (PROMPT + offset - jnp.sum(jnp.where(member, first_slot[:, None], 0), axis=0)).astype(jnp.int32)
    prompt_rows = jnp.arange(PROMPT, dtype=jnp.int32)
    prompt_place = (block_index[prompt_rows // BLOCK] * BLOCK + prompt_rows % BLOCK).astype(jnp.int32)
    token_owner = jnp.concatenate([jnp.full((PROMPT,), -1, dtype=jnp.int32), slot_owner], axis=0)
    token_place = jnp.concatenate([prompt_place, slot_place], axis=0)
    return token_owner, token_place


def finish_stats(stat_pair):
    peak_score, total_exp = stat_pair
    filled = total_exp > 0.0
    return jnp.where(filled, peak_score + jnp.log(jnp.where(filled, total_exp, 1.0)), 0.0)


def reference(prompt_q, prompt_k, prompt_v, prompt_out, prompt_dout, resp_q, resp_k, resp_v, resp_out, resp_dout, lengths, resp_row, block_index):
    token_owner, token_place = token_layout(lengths, resp_row, block_index)
    token_count = PROMPT + SLOTS
    group_size = Q_HEADS // KV_HEADS
    score_scale = HEAD_DIM ** -0.5

    def query_heads(first_part, second_part):
        joined = jnp.concatenate([first_part, second_part], axis=0)
        return jnp.moveaxis(joined.reshape(token_count, KV_HEADS, group_size, HEAD_DIM), 1, 0)

    def key_heads(first_part, second_part):
        joined = jnp.concatenate([first_part, second_part], axis=0)
        return jnp.moveaxis(joined.reshape(token_count, KV_HEADS, HEAD_DIM), 1, 0)

    queries = query_heads(prompt_q, resp_q)
    outputs = query_heads(prompt_out, resp_out)
    cotangent = query_heads(prompt_dout, resp_dout)
    key_rows = key_heads(prompt_k, resp_k)
    value_rows = key_heads(prompt_v, resp_v)

    block_rows = math.gcd(token_count, 512)
    block_total = token_count // block_rows
    key_live = token_owner != -2

    def one_head(head_arrays):
        query_head, output_head, cot_head, key_head, value_head = head_arrays
        key_float = key_head.astype(jnp.float32)
        value_float = value_head.astype(jnp.float32)

        def visit(carried, block_items):
            key_grad, value_grad = carried
            query_block, output_block, cot_block, owner_block, place_block = block_items
            visible = (token_place[None, :] <= place_block[:, None]) & ((token_owner[None, :] == -1) | (token_owner[None, :] == owner_block[:, None])) & (owner_block[:, None] != -2) & key_live[None, :]
            query_float = query_block.astype(jnp.float32)
            cot_float = cot_block.astype(jnp.float32)
            scores = jnp.einsum("qgd,kd->gqk", query_float, key_float) * score_scale
            scores = jnp.where(visible[None], scores, -jnp.inf)
            any_visible = jnp.any(visible, axis=1)
            peak_score = jnp.where(any_visible[None], jnp.max(scores, axis=2), 0.0)
            total_exp = jnp.sum(jnp.exp(scores - peak_score[..., None]), axis=2)
            log_total = finish_stats((peak_score, total_exp))
            probs = jnp.exp(scores - log_total[..., None])
            delta = jnp.transpose(jnp.sum(output_block.astype(jnp.float32) * cot_float, axis=2), (1, 0))
            dprob = jnp.einsum("qgd,kd->gqk", cot_float, value_float)
            dscore = (probs * (dprob - delta[..., None])).astype(jnp.bfloat16)
            dscore = lax.optimization_barrier(dscore)
            prob_half = lax.optimization_barrier(probs.astype(jnp.bfloat16))
            dscore_float = dscore.astype(jnp.float32)
            prob_float = prob_half.astype(jnp.float32)
            query_grad = (score_scale * jnp.einsum("gqk,kd->qgd", dscore_float, key_float)).astype(jnp.bfloat16)
            key_grad = key_grad + score_scale * jnp.einsum("gqk,qgd->kd", dscore_float, query_float)
            value_grad = value_grad + jnp.einsum("gqk,qgd->kd", prob_float, cot_float)
            return (key_grad, value_grad), query_grad

        block_items = (
            query_head.reshape(block_total, block_rows, group_size, HEAD_DIM),
            output_head.reshape(block_total, block_rows, group_size, HEAD_DIM),
            cot_head.reshape(block_total, block_rows, group_size, HEAD_DIM),
            token_owner.reshape(block_total, block_rows),
            token_place.reshape(block_total, block_rows),
        )
        zero_grad = jnp.zeros((token_count, HEAD_DIM), dtype=jnp.float32)
        (key_grad, value_grad), query_blocks = lax.scan(visit, (zero_grad, zero_grad), block_items)
        return query_blocks.reshape(token_count, group_size, HEAD_DIM), key_grad.astype(jnp.bfloat16), value_grad.astype(jnp.bfloat16)

    query_grad, key_grad, value_grad = lax.map(one_head, (queries, outputs, cotangent, key_rows, value_rows))
    query_all = jnp.moveaxis(query_grad, 0, 1).reshape(token_count, Q_HEADS * HEAD_DIM)
    key_all = jnp.moveaxis(key_grad, 0, 1).reshape(token_count, KV_HEADS * HEAD_DIM)
    value_all = jnp.moveaxis(value_grad, 0, 1).reshape(token_count, KV_HEADS * HEAD_DIM)
    return (query_all[:PROMPT], key_all[:PROMPT], value_all[:PROMPT], query_all[PROMPT:], key_all[PROMPT:], value_all[PROMPT:])
```

```python
import functools

import jax
import jax.numpy as jnp
from jax import lax
from jax.experimental import pallas as pl
from jax.experimental.pallas import tpu as pltpu
from jax.sharding import PartitionSpec as P

MESH = pl.DeviceIdType.MESH
F32, BF16 = jnp.float32, jnp.bfloat16
HD = 128
GROUP = 8
BLK = 128
NZ = 8
QW = GROUP * BLK
CK = 4 * BLK
QT = 512
SCALE = HD ** -0.5
EXP_SCALE = SCALE * 1.4426950408889634
LOW = -1e30
NEG = float("-inf")
DEAD = 1 << 20


def dot(a, b):
    return jnp.dot(a, b, preferred_element_type=F32)


def kernel(
    nresp,
    len_ref, row_ref, bi_ref,
    pq, pk, pv, pout, pdo, sq, sk, sv, sout, sdo,
    dqp, dkp, dvp, dqr, dkr, dvr,
    kall, vall, rq, rdo, rk, rv, rdel, dbuf,
    qa, doa, qT, doT, pt, own_pt, mh, mrun, lrun, delta, dqT, psc, dssc,
    gpart, grecv, kept, ysb, yrb, zsb, zrb, dqrows, dkrows, dvrows,
    kzs, kzr, kys, kyr, kcs, kcr, vzs, vzr, vys, vyr, vcs, vcr,
    as_, ar_, gcs, gcr, gys, gyr, gzs, gzr, bs_, br_, loc,
):
    c = lax.axis_index("ctx")
    r = lax.axis_index("resp")
    z = c // 4
    lane4 = c % 4
    core = c % 2
    ylo = lane4 // 2
    cpart = c + 1 - 2 * core
    ypart = c + 2 - 4 * ylo

    def zpeer(d):
        return lax.rem(z + d, NZ) * 4 + lane4

    def rpeer(d):
        return lax.rem(r + d, nresp)

    def remote(src, dst, ss, rs, dev):
        return pltpu.make_async_remote_copy(
            src_ref=src, dst_ref=dst, send_sem=ss, recv_sem=rs, device_id=dev, device_id_type=MESH
        )

    def blk(ref, b):
        return ref.at[pl.ds(pl.multiple_of(b * BLK, BLK), BLK), :]

    def zoff(i):
        return jnp.where(i % 2 == 1, (i + 1) // 2, (NZ - i // 2) % NZ)

    barrier = pltpu.get_barrier_semaphore()

    def greet(dev):
        pl.semaphore_signal(barrier, inc=1, device_id=dev, device_id_type=MESH)

    def greet_z(d, carry):
        greet((zpeer(d), r))
        return carry

    def greet_r(d, carry):
        greet((c, rpeer(d)))
        return carry

    lax.fori_loop(1, NZ, greet_z, 0)
    lax.fori_loop(1, nresp, greet_r, 0)
    greet((cpart, r))
    greet((ypart, r))
    pl.semaphore_wait(barrier, (NZ - 1) + (nresp - 1) + 2)

    def z_copy(src, dst, ss, rs, d):
        return remote(src, blk(dst, c), ss.at[d], rs.at[NZ - d], (zpeer(d), r))

    def z_wait(dst, ss, rs, d):
        b = zpeer(d)
        remote(blk(dst, b), blk(dst, b), ss.at[d], rs.at[d], (b, r)).wait_recv()

    def y_copy(dst, ss, rs, d):
        b = zpeer(d)
        return remote(blk(dst, b), blk(dst, b), ss.at[d], rs.at[d], (ypart, r))

    def y_wait(dst, ss, rs, d):
        b = zpeer(d) + 2 - 4 * ylo
        remote(blk(dst, b), blk(dst, b), ss.at[d], rs.at[d], (ypart, r)).wait_recv()

    def c_copy(dst, ss, rs, d, far):
        b = zpeer(d) + far * (2 - 4 * ylo)
        return remote(blk(dst, b), blk(dst, b), ss.at[d, far], rs.at[d, far], (cpart, r))

    def c_wait(dst, ss, rs, d, far):
        b = zpeer(d) + 1 - 2 * core + far * (2 - 4 * ylo)
        remote(blk(dst, b), blk(dst, b), ss.at[d, far], rs.at[d, far], (cpart, r)).wait_recv()

    ksems = (kzs, kzr, kys, kyr, kcs, kcr)
    vsems = (vzs, vzr, vys, vyr, vcs, vcr)

    def send_own(src, dst, sems):
        zs, zr, ys, yr, cs, cr = sems

        def send(d, carry):
            z_copy(src, dst, zs, zr, d).start()
            return carry

        lax.fori_loop(1, NZ, send, 0)
        dst[pl.ds(pl.multiple_of(c * BLK, BLK), BLK), :] = src[...]
        y_copy(dst, ys, yr, 0).start()
        c_copy(dst, cs, cr, 0, 0).start()

    def pass_on(dst, sems, i):
        zs, zr, ys, yr, cs, cr = sems

        @pl.when(i < NZ)
        def _():
            d = zoff(i)
            z_wait(dst, zs, zr, d)
            y_copy(dst, ys, yr, d).start()
            c_copy(dst, cs, cr, d, 0).start()

    def arrive(dst, sems, i):
        zs, zr, ys, yr, cs, cr = sems
        d = zoff(i)
        y_wait(dst, ys, yr, d)
        c_copy(dst, cs, cr, d, 1).start()
        pass_on(dst, sems, i + 1)
        c_wait(dst, cs, cr, d, 0)
        c_wait(dst, cs, cr, d, 1)

    def drain_gather(src, dst, sems):
        zs, zr, ys, yr, cs, cr = sems

        def drain_z(d, carry):
            z_copy(src, dst, zs, zr, d).wait_send()
            return carry

        def drain_rest(d, carry):
            y_copy(dst, ys, yr, d).wait_send()
            c_copy(dst, cs, cr, d, 0).wait_send()
            c_copy(dst, cs, cr, d, 1).wait_send()
            return carry

        lax.fori_loop(1, NZ, drain_z, 0)
        lax.fori_loop(0, NZ, drain_rest, 0)

    def cols(ref, p, w):
        return ref.at[:, pl.ds(pl.multiple_of(p * w, 128), w)]

    def slots(ref, p):
        return ref.at[pl.ds(pl.multiple_of(p * 16, 16), 16), :]

    def sources(p):
        return (cols(sq, p, QW), cols(sdo, p, QW), cols(sk, p, HD), cols(sv, p, HD), dbuf.at[p])

    landings = (rq, rdo, rk, rv, rdel)

    def exchange(d, which):
        p = rpeer(d)
        src = sources(p)
        return [
            remote(src[n], slots(landings[n], r), as_.at[n, d], ar_.at[n, nresp - d], (c, p))
            for n in which
        ]

    def exchange_in(d):
        p = rpeer(d)
        return [
            remote(slots(landings[n], p), slots(landings[n], p), as_.at[n, d], ar_.at[n, d], (c, p))
            for n in range(5)
        ]

    def local_in(which):
        src = sources(r)
        return [pltpu.make_async_copy(src[n], slots(landings[n], r), loc.at[n]) for n in which]

    send_own(pk, kall, ksems)

    def send_qdo(d, carry):
        for cp in exchange(d, range(4)):
            cp.start()
        return carry

    lax.fori_loop(1, nresp, send_qdo, 0)
    for cp in local_in(range(4)):
        cp.start()
    send_own(pv, vall, vsems)

    lane16 = lax.broadcasted_iota(jnp.int32, (16, 128), 1)
    for g in range(nresp):
        acc = jnp.zeros((16, 128), F32)
        for h in range(GROUP):
            sl = slice((g * GROUP + h) * HD, (g * GROUP + h + 1) * HD)
            prod = sout[:, sl].astype(F32) * sdo[:, sl].astype(F32)
            acc = jnp.where(lane16 == h, jnp.sum(prod, axis=1, keepdims=True), acc)
        dbuf[g] = acc

    def send_delta(d, carry):
        exchange(d, (4,))[0].start()
        return carry

    lax.fori_loop(1, nresp, send_delta, 0)
    local_in((4,))[0].start()

    lane = lax.broadcasted_iota(jnp.int32, (128, 128), 1)
    subl = lax.broadcasted_iota(jnp.int32, (128, 128), 0)
    diff = lane - subl
    my = bi_ref[c]

    def load_queries(q, do, base):
        for h in range(GROUP):
            sl = slice(h * HD, (h + 1) * HD)
            out = slice(base + h * BLK, base + (h + 1) * BLK)
            qh, dh = q[:, sl], do[:, sl]
            qa[out, :] = qh
            doa[out, :] = dh
            qT[:, out] = qh.T
            doT[:, out] = dh.T

    def place_delta(rows, base):
        rows_t = rows.T
        for h in range(GROUP):
            delta[:, base + h * BLK: base + (h + 1) * BLK] = rows_t[h:h + 1, :]

    load_queries(pq, pdo, 0)
    acc = jnp.zeros((BLK, 128), F32)
    for h in range(GROUP):
        sl = slice(h * HD, (h + 1) * HD)
        prod = pout[:, sl].astype(F32) * pdo[:, sl].astype(F32)
        acc = jnp.where(lane == h, jnp.sum(prod, axis=1, keepdims=True), acc)
    place_delta(acc, 0)
    mrun[...] = jnp.full((1, 2 * QW), LOW, F32)
    lrun[...] = jnp.zeros((1, 2 * QW), F32)

    def stats_chunk(i, base, masked):
        zc = lax.rem(z + zoff(i), NZ)
        kc = kall[pl.ds(pl.multiple_of(zc * CK, CK), CK), :]
        prow = pl.ds(pl.multiple_of(i * CK, CK), CK)
        if masked:
            masks = [diff >= (bi_ref[zc * 4 + b] - my) * BLK for b in range(4)]
            masks = [jnp.concatenate([mk] * (QT // BLK), axis=1) for mk in masks]
        for t in range(QW // QT):
            sl = slice(base + t * QT, base + (t + 1) * QT)
            s = dot(kc, qT[:, sl])
            if masked:
                s = jnp.concatenate(
                    [jnp.where(masks[b], s[b * BLK:(b + 1) * BLK, :], NEG) for b in range(4)], axis=0
                )
            mo = mrun[:, sl]
            m = jnp.maximum(mo, jnp.max(s, axis=0, keepdims=True))
            p = jnp.exp2((s - m) * EXP_SCALE)
            pt[prow, sl] = p.astype(BF16)
            mrun[:, sl] = m
            mh[pl.ds(i, 1), sl] = m
            lrun[:, sl] = lrun[:, sl] * jnp.exp2((mo - m) * EXP_SCALE) + jnp.sum(p, axis=0, keepdims=True)

    def prompt_stats(i, carry):
        arrive(kall, ksems, i)
        stats_chunk(i, 0, True)
        return carry

    lax.fori_loop(0, NZ, prompt_stats, 0)

    def wait_in(d, carry):
        for cp in exchange_in(d):
            cp.wait_recv()
        return carry

    lax.fori_loop(1, nresp, wait_in, 0)
    for cp in local_in(range(5)):
        cp.wait()
    load_queries(rq, rdo, QW)
    place_delta(rdel[...], QW)

    lane1 = lax.broadcasted_iota(jnp.int32, (1, 128), 1)
    startq = jnp.full((1, 128), DEAD, jnp.int32)
    cum = jnp.int32(0)
    for n in range(len_ref.shape[0]):
        count = jnp.where(row_ref[n] == c, len_ref[n], 0)
        startq = jnp.where((lane1 >= cum) & (lane1 < cum + count), cum, startq)
        cum = cum + count
    live = jnp.where(startq < DEAD, 1.0, 0.0)
    own_mask = (subl >= startq) & (diff >= 0)
    for h in range(GROUP):
        sl = slice(QW + h * BLK, QW + (h + 1) * BLK)
        s = jnp.where(own_mask, dot(rk[...], qT[:, sl]), NEG)
        m = jnp.maximum(jnp.max(s, axis=0, keepdims=True), LOW)
        p = jnp.exp2((s - m) * EXP_SCALE)
        own_pt[:, h * BLK:(h + 1) * BLK] = p.astype(BF16)
        mh[NZ:NZ + 1, sl] = m
        mrun[:, sl] = m
        lrun[:, sl] = jnp.sum(p, axis=0, keepdims=True)

    def resp_stats(i, carry):
        arrive(vall, vsems, i)
        stats_chunk(i, QW, False)
        return carry

    lax.fori_loop(0, NZ, resp_stats, 0)

    total = lrun[...]
    inv = jnp.where(total > 0.0, 1.0 / total, 0.0)
    inv = inv * jnp.concatenate([jnp.ones((1, QW), F32)] + [live] * GROUP, axis=1)
    mh[0:NZ, :] = jnp.exp2((mh[0:NZ, :] - mrun[...]) * EXP_SCALE) * inv
    own_f = jnp.exp2((mh[NZ:NZ + 1, QW:] - mrun[:, QW:]) * EXP_SCALE) * inv[:, QW:]
    dqT[...] = jnp.zeros_like(dqT)

    def core_send(j):
        return remote(gpart.at[j, 1 - core], grecv.at[j], gcs.at[j], gcr.at[j], (cpart, r))

    def y_send(j):
        return remote(ysb.at[j], yrb.at[j], gys.at[j], gyr.at[j], (ypart, r))

    def z_send(j):
        d = zoff(NZ - 1 - j)
        return remote(zsb.at[j], zrb.at[NZ - d], gzs.at[d], gzr.at[NZ - d], (zpeer(d), r))

    def after_core(j):
        core_send(j).wait_recv()
        kept[j] = gpart[j, core, ylo] + grecv[j, ylo]
        ysb[j] = (gpart[j, core, 1 - ylo] + grecv[j, 1 - ylo]).astype(BF16)
        y_send(j).start()

    def after_y(j):
        y_send(j).wait_recv()
        zsb[j] = (kept[j] + yrb[j].astype(F32)).astype(BF16)
        z_send(j).start()

    def grads(j, carry):
        i = NZ - 1 - j
        zc = lax.rem(z + zoff(i), NZ)
        krow = pl.ds(pl.multiple_of(zc * CK, CK), CK)
        prow = pl.ds(pl.multiple_of(i * CK, CK), CK)
        vc = vall[krow, :]
        kTc = kall[krow, :].T
        f = mh[pl.ds(i, 1), :]
        for t in range(2 * QW // QT):
            sl = slice(t * QT, (t + 1) * QT)
            dp = dot(vc, doT[:, sl])
            p = pt[prow, sl].astype(F32) * f[:, sl]
            ds = (p * (dp - delta[:, sl])).astype(BF16)
            psc[:, sl] = p.astype(BF16)
            dssc[:, sl] = ds
            dqT[:, sl] += dot(kTc, ds)
        dk = dot(dssc[...], qa[...])
        dv = dot(psc[...], doa[...])
        for b in range(4):
            gpart[j, b % 2, b // 2, 0] = dk[b * BLK:(b + 1) * BLK, :]
            gpart[j, b % 2, b // 2, 1] = dv[b * BLK:(b + 1) * BLK, :]
        core_send(j).start()

        @pl.when(j >= 1)
        def _():
            after_core(j - 1)

        @pl.when(j >= 2)
        def _():
            after_y(j - 2)

        return carry

    lax.fori_loop(0, NZ, grads, 0)

    rkT = rk[...].T
    for h in range(GROUP):
        sl = slice(QW + h * BLK, QW + (h + 1) * BLK)
        dp = dot(rv[...], doT[:, sl])
        p = own_pt[:, h * BLK:(h + 1) * BLK].astype(F32) * own_f[:, h * BLK:(h + 1) * BLK]
        ds = (p * (dp - delta[:, sl])).astype(BF16)
        psc[0:BLK, sl] = p.astype(BF16)
        dssc[0:BLK, sl] = ds
        dqT[:, sl] += dot(rkT, ds)
    dvrows[...] = dot(psc[0:BLK, QW:], doa[QW:, :]).astype(BF16)
    dkrows[...] = (dot(dssc[0:BLK, QW:], qa[QW:, :]) * SCALE).astype(BF16)
    for h in range(GROUP):
        dqrows[:, h * HD:(h + 1) * HD] = (dqT[:, QW + h * BLK:QW + (h + 1) * BLK].T * SCALE).astype(BF16)

    def back(d):
        p = rpeer(d)
        dev = (c, p)
        e = nresp - d
        return (
            remote(slots(dqrows, p), cols(dqr, r, QW), bs_.at[0, d], br_.at[0, e], dev),
            remote(slots(dkrows, p), cols(dkr, r, HD), bs_.at[1, d], br_.at[1, e], dev),
            remote(slots(dvrows, p), cols(dvr, r, HD), bs_.at[2, d], br_.at[2, e], dev),
        )

    def back_in(d):
        p = rpeer(d)
        dev = (c, p)
        return (
            remote(cols(dqr, p, QW), cols(dqr, p, QW), bs_.at[0, d], br_.at[0, d], dev),
            remote(cols(dkr, p, HD), cols(dkr, p, HD), bs_.at[1, d], br_.at[1, d], dev),
            remote(cols(dvr, p, HD), cols(dvr, p, HD), bs_.at[2, d], br_.at[2, d], dev),
        )

    def local_back():
        return (
            pltpu.make_async_copy(slots(dqrows, r), cols(dqr, r, QW), loc.at[5]),
            pltpu.make_async_copy(slots(dkrows, r), cols(dkr, r, HD), loc.at[6]),
            pltpu.make_async_copy(slots(dvrows, r), cols(dvr, r, HD), loc.at[7]),
        )

    def send_back(d, carry):
        for cp in back(d):
            cp.start()
        return carry

    lax.fori_loop(1, nresp, send_back, 0)
    for cp in local_back():
        cp.start()

    after_core(NZ - 1)
    after_y(NZ - 2)
    for h in range(GROUP):
        dqp[:, h * HD:(h + 1) * HD] = (dqT[:, h * BLK:(h + 1) * BLK].T * SCALE).astype(BF16)
    y_send(NZ - 1).wait_recv()
    kept[NZ - 1] = kept[NZ - 1] + yrb[NZ - 1].astype(F32)

    drain_gather(pk, kall, ksems)
    drain_gather(pv, vall, vsems)

    def drain_exchange(d, carry):
        for cp in exchange(d, range(5)):
            cp.wait_send()
        return carry

    lax.fori_loop(1, nresp, drain_exchange, 0)

    def drain_parts(j, carry):
        core_send(j).wait_send()
        y_send(j).wait_send()
        return carry

    lax.fori_loop(0, NZ, drain_parts, 0)

    def drain_z(j, carry):
        z_send(j).wait_send()
        return carry

    lax.fori_loop(0, NZ - 1, drain_z, 0)

    def z_parts(d, carry):
        remote(zrb.at[d], zrb.at[d], gzs.at[d], gzr.at[d], (zpeer(d), r)).wait_recv()
        kept[NZ - 1] = kept[NZ - 1] + zrb[d].astype(F32)
        return carry

    lax.fori_loop(1, NZ, z_parts, 0)
    dkp[...] = (kept[NZ - 1, 0] * SCALE).astype(BF16)
    dvp[...] = kept[NZ - 1, 1].astype(BF16)

    def finish_back(d, carry):
        for cp in back(d):
            cp.wait_send()
        for cp in back_in(d):
            cp.wait_recv()
        return carry

    lax.fori_loop(1, nresp, finish_back, 0)
    for cp in local_back():
        cp.wait()


def solution(mesh):
    nresp = mesh.shape["resp"]
    keys = mesh.shape["ctx"] * BLK

    def body(
        prompt_q, prompt_k, prompt_v, prompt_out, prompt_dout,
        resp_q, resp_k, resp_v, resp_out, resp_dout,
        lengths, resp_row, block_index,
    ):
        shape = jax.ShapeDtypeStruct
        smem = pl.BlockSpec(memory_space=pltpu.SMEM)
        vmem = pl.BlockSpec(memory_space=pltpu.VMEM)
        dma = pltpu.SemaphoreType.DMA
        own = prompt_q.shape[0]
        gather_sems = [dma((NZ,)), dma((NZ,)), dma((NZ,)), dma((NZ,)), dma((NZ, 2)), dma((NZ, 2))]
        return pl.pallas_call(
            functools.partial(kernel, nresp),
            out_shape=(
                shape(prompt_q.shape, BF16),
                shape(prompt_k.shape, BF16),
                shape(prompt_v.shape, BF16),
                shape(resp_q.shape, BF16),
                shape(resp_k.shape, BF16),
                shape(resp_v.shape, BF16),
            ),
            in_specs=[smem] * 3 + [vmem] * 10,
            out_specs=(vmem,) * 6,
            scratch_shapes=[
                pltpu.VMEM((keys, HD), BF16),
                pltpu.VMEM((keys, HD), BF16),
                pltpu.VMEM((own, QW), BF16),
                pltpu.VMEM((own, QW), BF16),
                pltpu.VMEM((own, HD), BF16),
                pltpu.VMEM((own, HD), BF16),
                pltpu.VMEM((own, 128), F32),
                pltpu.VMEM((nresp, 16, 128), F32),
                pltpu.VMEM((2 * QW, HD), BF16),
                pltpu.VMEM((2 * QW, HD), BF16),
                pltpu.VMEM((HD, 2 * QW), BF16),
                pltpu.VMEM((HD, 2 * QW), BF16),
                pltpu.VMEM((keys, 2 * QW), BF16),
                pltpu.VMEM((BLK, QW), BF16),
                pltpu.VMEM((2 * NZ, 2 * QW), F32),
                pltpu.VMEM((1, 2 * QW), F32),
                pltpu.VMEM((1, 2 * QW), F32),
                pltpu.VMEM((1, 2 * QW), F32),
                pltpu.VMEM((HD, 2 * QW), F32),
                pltpu.VMEM((CK, 2 * QW), BF16),
                pltpu.VMEM((CK, 2 * QW), BF16),
                pltpu.VMEM((NZ, 2, 2, 2, BLK, HD), F32),
                pltpu.VMEM((NZ, 2, 2, BLK, HD), F32),
                pltpu.VMEM((NZ, 2, BLK, HD), F32),
                pltpu.VMEM((NZ, 2, BLK, HD), BF16),
                pltpu.VMEM((NZ, 2, BLK, HD), BF16),
                pltpu.VMEM((NZ, 2, BLK, HD), BF16),
                pltpu.VMEM((NZ, 2, BLK, HD), BF16),
                pltpu.VMEM((own, QW), BF16),
                pltpu.VMEM((own, HD), BF16),
                pltpu.VMEM((own, HD), BF16),
            ]
            + gather_sems
            + gather_sems
            + [
                dma((5, nresp)),
                dma((5, nresp)),
                dma((NZ,)),
                dma((NZ,)),
                dma((NZ,)),
                dma((NZ,)),
                dma((NZ,)),
                dma((NZ,)),
                dma((3, nresp)),
                dma((3, nresp)),
                dma((8,)),
            ],
            compiler_params=pltpu.CompilerParams(
                collective_id=0, has_side_effects=True, vmem_limit_bytes=60 * 1024 * 1024
            ),
            name="attn_bwd",
        )(
            lengths, resp_row, block_index,
            prompt_q, prompt_k, prompt_v, prompt_out, prompt_dout,
            resp_q, resp_k, resp_v, resp_out, resp_dout,
        )

    heads, rows, whole = P("ctx", "resp"), P(("ctx", "resp"), None), P()
    return jax.shard_map(
        body,
        mesh=mesh,
        in_specs=(heads,) * 5 + (rows,) * 5 + (whole,) * 3,
        out_specs=(heads,) * 3 + (rows,) * 3,
        check_vma=False,
    )
```

```python
import functools

import jax
import jax.numpy as jnp
from jax import lax
from jax.experimental import pallas as pl
from jax.experimental.pallas import tpu as pltpu
from jax.sharding import PartitionSpec as P

MESH = pl.DeviceIdType.MESH
F32, BF16 = jnp.float32, jnp.bfloat16
HD = 128
GROUP = 8
BLK = 128
NZ = 8
LEAD = 3
QW = GROUP * BLK
CK = 4 * BLK
QT = 512
SCALE = HD ** -0.5
EXP_SCALE = SCALE * 1.4426950408889634
LOW = -1e30
NEG = float("-inf")
DEAD = 1 << 20


def dot(a, b):
    return jnp.dot(a, b, preferred_element_type=F32)


def kernel(
    nresp,
    len_ref, row_ref, bi_ref,
    pq, pk, pv, pout, pdo, sq, sk, sv, sout, sdo,
    dqp, dkp, dvp, dqr, dkr, dvr,
    kv, rq, rdo, rk, rv, rdel, dbuf,
    qa, doa, qT, doT, pt, own_pt, mh, mrun, lrun, delta, dqT, psc, dssc,
    gpart, grecv, kept, ysb, yrb, zsb, zrb, dqrows, dkrows, dvrows,
    zs, zr, ys, yr, cs, cr,
    as_, ar_, gcs, gcr, gys, gyr, gzs, gzr, bs_, br_, loc,
):
    c = lax.axis_index("ctx")
    r = lax.axis_index("resp")
    z = c // 4
    lane4 = c % 4
    core = c % 2
    ylo = lane4 // 2
    cpart = c + 1 - 2 * core
    ypart = c + 2 - 4 * ylo

    def zpeer(d):
        return lax.rem(z + d, NZ) * 4 + lane4

    def rpeer(d):
        return lax.rem(r + d, nresp)

    def remote(src, dst, ss, rs, dev):
        return pltpu.make_async_remote_copy(
            src_ref=src, dst_ref=dst, send_sem=ss, recv_sem=rs, device_id=dev, device_id_type=MESH
        )

    def zoff(i):
        return jnp.where(i % 2 == 1, (i + 1) // 2, (NZ - i // 2) % NZ)

    barrier = pltpu.get_barrier_semaphore()

    def greet(dev):
        pl.semaphore_signal(barrier, inc=1, device_id=dev, device_id_type=MESH)

    def greet_z(d, carry):
        greet((zpeer(d), r))
        return carry

    def greet_r(d, carry):
        greet((c, rpeer(d)))
        return carry

    lax.fori_loop(1, NZ, greet_z, 0)
    lax.fori_loop(1, nresp, greet_r, 0)
    greet((cpart, r))
    greet((ypart, r))
    pl.semaphore_wait(barrier, (NZ - 1) + (nresp - 1) + 2)

    def z_copy(d):
        return remote(kv.at[c], kv.at[c], zs.at[d], zr.at[NZ - d], (zpeer(d), r))

    def z_wait(d):
        b = zpeer(d)
        remote(kv.at[b], kv.at[b], zs.at[d], zr.at[d], (b, r)).wait_recv()

    def y_copy(d):
        b = zpeer(d)
        return remote(kv.at[b], kv.at[b], ys.at[d], yr.at[d], (ypart, r))

    def y_wait(d):
        b = zpeer(d) + 2 - 4 * ylo
        remote(kv.at[b], kv.at[b], ys.at[d], yr.at[d], (ypart, r)).wait_recv()

    def c_copy(d, far):
        b = zpeer(d) + far * (2 - 4 * ylo)
        return remote(kv.at[b], kv.at[b], cs.at[d, far], cr.at[d, far], (cpart, r))

    def c_wait(d, far):
        b = zpeer(d) + 1 - 2 * core + far * (2 - 4 * ylo)
        remote(kv.at[b], kv.at[b], cs.at[d, far], cr.at[d, far], (cpart, r)).wait_recv()

    def send_own():
        kv[c, 0] = pk[...]
        kv[c, 1] = pv[...]
        y_copy(0).start()
        c_copy(0, 0).start()

        def send(i, carry):
            z_copy(zoff(i)).start()
            return carry

        lax.fori_loop(1, NZ, send, 0)

    def pass_near(i):
        @pl.when(i < NZ)
        def _():
            d = zoff(i)
            z_wait(d)
            y_copy(d).start()
            c_copy(d, 0).start()

    def pass_far(i):
        @pl.when(i < NZ)
        def _():
            d = zoff(i)
            y_wait(d)
            c_copy(d, 1).start()

    def arrive(i):
        pass_near(i + LEAD + 1)
        pass_far(i + 1)
        d = zoff(i)
        c_wait(d, 0)
        c_wait(d, 1)

    def drain_gather():
        def drain_z(d, carry):
            z_copy(d).wait_send()
            return carry

        def drain_rest(d, carry):
            y_copy(d).wait_send()
            c_copy(d, 0).wait_send()
            c_copy(d, 1).wait_send()
            return carry

        lax.fori_loop(1, NZ, drain_z, 0)
        lax.fori_loop(0, NZ, drain_rest, 0)

    def cols(ref, p, w):
        return ref.at[:, pl.ds(pl.multiple_of(p * w, 128), w)]

    def slots(ref, p):
        return ref.at[pl.ds(pl.multiple_of(p * 16, 16), 16), :]

    def sources(p):
        return (cols(sq, p, QW), cols(sdo, p, QW), cols(sk, p, HD), cols(sv, p, HD), dbuf.at[p])

    landings = (rq, rdo, rk, rv, rdel)

    def exchange(d, which):
        p = rpeer(d)
        src = sources(p)
        return [
            remote(src[n], slots(landings[n], r), as_.at[n, d], ar_.at[n, nresp - d], (c, p))
            for n in which
        ]

    def exchange_in(d):
        p = rpeer(d)
        return [
            remote(slots(landings[n], p), slots(landings[n], p), as_.at[n, d], ar_.at[n, d], (c, p))
            for n in range(5)
        ]

    def local_in(which):
        src = sources(r)
        return [pltpu.make_async_copy(src[n], slots(landings[n], r), loc.at[n]) for n in which]

    send_own()

    def send_qdo(d, carry):
        for cp in exchange(d, range(4)):
            cp.start()
        return carry

    lax.fori_loop(1, nresp, send_qdo, 0)
    for cp in local_in(range(4)):
        cp.start()

    lane16 = lax.broadcasted_iota(jnp.int32, (16, 128), 1)
    for g in range(nresp):
        acc = jnp.zeros((16, 128), F32)
        for h in range(GROUP):
            sl = slice((g * GROUP + h) * HD, (g * GROUP + h + 1) * HD)
            prod = sout[:, sl].astype(F32) * sdo[:, sl].astype(F32)
            acc = jnp.where(lane16 == h, jnp.sum(prod, axis=1, keepdims=True), acc)
        dbuf[g] = acc

    def send_delta(d, carry):
        exchange(d, (4,))[0].start()
        return carry

    lax.fori_loop(1, nresp, send_delta, 0)
    local_in((4,))[0].start()

    lane = lax.broadcasted_iota(jnp.int32, (128, 128), 1)
    subl = lax.broadcasted_iota(jnp.int32, (128, 128), 0)
    diff = lane - subl
    my = bi_ref[c]

    def load_queries(q, do, base):
        for h in range(GROUP):
            sl = slice(h * HD, (h + 1) * HD)
            out = slice(base + h * BLK, base + (h + 1) * BLK)
            qh, dh = q[:, sl], do[:, sl]
            qa[out, :] = qh
            doa[out, :] = dh
            qT[:, out] = qh.T
            doT[:, out] = dh.T

    def place_delta(rows, base):
        rows_t = rows.T
        for h in range(GROUP):
            delta[:, base + h * BLK: base + (h + 1) * BLK] = rows_t[h:h + 1, :]

    load_queries(pq, pdo, 0)
    acc = jnp.zeros((BLK, 128), F32)
    for h in range(GROUP):
        sl = slice(h * HD, (h + 1) * HD)
        prod = pout[:, sl].astype(F32) * pdo[:, sl].astype(F32)
        acc = jnp.where(lane == h, jnp.sum(prod, axis=1, keepdims=True), acc)
    place_delta(acc, 0)
    mrun[...] = jnp.full((1, 2 * QW), LOW, F32)
    lrun[...] = jnp.zeros((1, 2 * QW), F32)

    def stats_chunk(i, base, masked):
        zc = lax.rem(z + zoff(i), NZ)
        kc = kv[pl.ds(zc * 4, 4), 0].reshape(CK, HD)
        prow = pl.ds(pl.multiple_of(i * CK, CK), CK)
        if masked:
            masks = [diff >= (bi_ref[zc * 4 + b] - my) * BLK for b in range(4)]
            masks = [jnp.concatenate([mk] * (QT // BLK), axis=1) for mk in masks]
        for t in range(QW // QT):
            sl = slice(base + t * QT, base + (t + 1) * QT)
            s = dot(kc, qT[:, sl])
            if masked:
                s = jnp.concatenate(
                    [jnp.where(masks[b], s[b * BLK:(b + 1) * BLK, :], NEG) for b in range(4)], axis=0
                )
            mo = mrun[:, sl]
            m = jnp.maximum(mo, jnp.max(s, axis=0, keepdims=True))
            p = jnp.exp2((s - m) * EXP_SCALE)
            pt[prow, sl] = p.astype(BF16)
            mrun[:, sl] = m
            mh[pl.ds(i, 1), sl] = m
            lrun[:, sl] = lrun[:, sl] * jnp.exp2((mo - m) * EXP_SCALE) + jnp.sum(p, axis=0, keepdims=True)

    def near_first(i, carry):
        pass_near(i)
        return carry

    def prompt_stats(i, carry):
        arrive(i)
        stats_chunk(i, 0, True)
        return carry

    lax.fori_loop(1, LEAD + 1, near_first, 0)
    pass_far(0)
    lax.fori_loop(0, NZ, prompt_stats, 0)

    def wait_in(d, carry):
        for cp in exchange_in(d):
            cp.wait_recv()
        return carry

    lax.fori_loop(1, nresp, wait_in, 0)
    for cp in local_in(range(5)):
        cp.wait()
    load_queries(rq, rdo, QW)
    place_delta(rdel[...], QW)

    lane1 = lax.broadcasted_iota(jnp.int32, (1, 128), 1)
    startq = jnp.full((1, 128), DEAD, jnp.int32)
    cum = jnp.int32(0)
    for n in range(len_ref.shape[0]):
        count = jnp.where(row_ref[n] == c, len_ref[n], 0)
        startq = jnp.where((lane1 >= cum) & (lane1 < cum + count), cum, startq)
        cum = cum + count
    live = jnp.where(startq < DEAD, 1.0, 0.0)
    own_mask = (subl >= startq) & (diff >= 0)
    for h in range(GROUP):
        sl = slice(QW + h * BLK, QW + (h + 1) * BLK)
        s = jnp.where(own_mask, dot(rk[...], qT[:, sl]), NEG)
        m = jnp.maximum(jnp.max(s, axis=0, keepdims=True), LOW)
        p = jnp.exp2((s - m) * EXP_SCALE)
        own_pt[:, h * BLK:(h + 1) * BLK] = p.astype(BF16)
        mh[NZ:NZ + 1, sl] = m
        mrun[:, sl] = m
        lrun[:, sl] = jnp.sum(p, axis=0, keepdims=True)

    def resp_stats(i, carry):
        stats_chunk(i, QW, False)
        return carry

    lax.fori_loop(0, NZ, resp_stats, 0)

    total = lrun[...]
    inv = jnp.where(total > 0.0, 1.0 / total, 0.0)
    inv = inv * jnp.concatenate([jnp.ones((1, QW), F32)] + [live] * GROUP, axis=1)
    mh[0:NZ, :] = jnp.exp2((mh[0:NZ, :] - mrun[...]) * EXP_SCALE) * inv
    own_f = jnp.exp2((mh[NZ:NZ + 1, QW:] - mrun[:, QW:]) * EXP_SCALE) * inv[:, QW:]
    dqT[...] = jnp.zeros_like(dqT)

    def core_send(j):
        return remote(gpart.at[j, 1 - core], grecv.at[j], gcs.at[j], gcr.at[j], (cpart, r))

    def y_send(j):
        return remote(ysb.at[j], yrb.at[j], gys.at[j], gyr.at[j], (ypart, r))

    def z_send(j):
        d = zoff(NZ - 1 - j)
        return remote(zsb.at[j], zrb.at[NZ - d], gzs.at[d], gzr.at[NZ - d], (zpeer(d), r))

    def after_core(j):
        core_send(j).wait_recv()
        kept[j] = gpart[j, core, ylo] + grecv[j, ylo]
        ysb[j] = (gpart[j, core, 1 - ylo] + grecv[j, 1 - ylo]).astype(BF16)
        y_send(j).start()

    def after_y(j):
        y_send(j).wait_recv()
        zsb[j] = (kept[j] + yrb[j].astype(F32)).astype(BF16)
        z_send(j).start()

    def grads(j, carry):
        i = NZ - 1 - j
        zc = lax.rem(z + zoff(i), NZ)
        prow = pl.ds(pl.multiple_of(i * CK, CK), CK)
        vc = kv[pl.ds(zc * 4, 4), 1].reshape(CK, HD)
        kTc = kv[pl.ds(zc * 4, 4), 0].reshape(CK, HD).T
        f = mh[pl.ds(i, 1), :]
        for t in range(2 * QW // QT):
            sl = slice(t * QT, (t + 1) * QT)
            dp = dot(vc, doT[:, sl])
            p = pt[prow, sl].astype(F32) * f[:, sl]
            ds = (p * (dp - delta[:, sl])).astype(BF16)
            psc[:, sl] = p.astype(BF16)
            dssc[:, sl] = ds
            dqT[:, sl] += dot(kTc, ds)
        dk = dot(dssc[...], qa[...])
        dv = dot(psc[...], doa[...])
        for b in range(4):
            gpart[j, b % 2, b // 2, 0] = dk[b * BLK:(b + 1) * BLK, :]
            gpart[j, b % 2, b // 2, 1] = dv[b * BLK:(b + 1) * BLK, :]
        core_send(j).start()

        @pl.when(j >= 1)
        def _():
            after_core(j - 1)

        @pl.when(j >= 2)
        def _():
            after_y(j - 2)

        return carry

    lax.fori_loop(0, NZ, grads, 0)

    rkT = rk[...].T
    for h in range(GROUP):
        sl = slice(QW + h * BLK, QW + (h + 1) * BLK)
        dp = dot(rv[...], doT[:, sl])
        p = own_pt[:, h * BLK:(h + 1) * BLK].astype(F32) * own_f[:, h * BLK:(h + 1) * BLK]
        ds = (p * (dp - delta[:, sl])).astype(BF16)
        psc[0:BLK, sl] = p.astype(BF16)
        dssc[0:BLK, sl] = ds
        dqT[:, sl] += dot(rkT, ds)
    dvrows[...] = dot(psc[0:BLK, QW:], doa[QW:, :]).astype(BF16)
    dkrows[...] = (dot(dssc[0:BLK, QW:], qa[QW:, :]) * SCALE).astype(BF16)
    for h in range(GROUP):
        dqrows[:, h * HD:(h + 1) * HD] = (dqT[:, QW + h * BLK:QW + (h + 1) * BLK].T * SCALE).astype(BF16)

    def back(d):
        p = rpeer(d)
        dev = (c, p)
        e = nresp - d
        return (
            remote(slots(dqrows, p), cols(dqr, r, QW), bs_.at[0, d], br_.at[0, e], dev),
            remote(slots(dkrows, p), cols(dkr, r, HD), bs_.at[1, d], br_.at[1, e], dev),
            remote(slots(dvrows, p), cols(dvr, r, HD), bs_.at[2, d], br_.at[2, e], dev),
        )

    def back_in(d):
        p = rpeer(d)
        dev = (c, p)
        return (
            remote(cols(dqr, p, QW), cols(dqr, p, QW), bs_.at[0, d], br_.at[0, d], dev),
            remote(cols(dkr, p, HD), cols(dkr, p, HD), bs_.at[1, d], br_.at[1, d], dev),
            remote(cols(dvr, p, HD), cols(dvr, p, HD), bs_.at[2, d], br_.at[2, d], dev),
        )

    def local_back():
        return (
            pltpu.make_async_copy(slots(dqrows, r), cols(dqr, r, QW), loc.at[5]),
            pltpu.make_async_copy(slots(dkrows, r), cols(dkr, r, HD), loc.at[6]),
            pltpu.make_async_copy(slots(dvrows, r), cols(dvr, r, HD), loc.at[7]),
        )

    def send_back(d, carry):
        for cp in back(d):
            cp.start()
        return carry

    lax.fori_loop(1, nresp, send_back, 0)
    for cp in local_back():
        cp.start()

    after_core(NZ - 1)
    after_y(NZ - 2)
    for h in range(GROUP):
        dqp[:, h * HD:(h + 1) * HD] = (dqT[:, h * BLK:(h + 1) * BLK].T * SCALE).astype(BF16)
    y_send(NZ - 1).wait_recv()
    kept[NZ - 1] = kept[NZ - 1] + yrb[NZ - 1].astype(F32)

    drain_gather()

    def drain_exchange(d, carry):
        for cp in exchange(d, range(5)):
            cp.wait_send()
        return carry

    lax.fori_loop(1, nresp, drain_exchange, 0)

    def drain_parts(j, carry):
        core_send(j).wait_send()
        y_send(j).wait_send()
        return carry

    lax.fori_loop(0, NZ, drain_parts, 0)

    def drain_z(j, carry):
        z_send(j).wait_send()
        return carry

    lax.fori_loop(0, NZ - 1, drain_z, 0)

    def z_parts(d, carry):
        remote(zrb.at[d], zrb.at[d], gzs.at[d], gzr.at[d], (zpeer(d), r)).wait_recv()
        kept[NZ - 1] = kept[NZ - 1] + zrb[d].astype(F32)
        return carry

    lax.fori_loop(1, NZ, z_parts, 0)
    dkp[...] = (kept[NZ - 1, 0] * SCALE).astype(BF16)
    dvp[...] = kept[NZ - 1, 1].astype(BF16)

    def finish_back(d, carry):
        for cp in back(d):
            cp.wait_send()
        for cp in back_in(d):
            cp.wait_recv()
        return carry

    lax.fori_loop(1, nresp, finish_back, 0)
    for cp in local_back():
        cp.wait()


def settle(*refs):
    n = (len(refs) - 1) // 2
    sems = refs[-1]
    copies = [pltpu.make_async_copy(refs[k], refs[n + k], sems.at[k]) for k in range(n)]
    for cp in copies:
        cp.start()
    for cp in copies:
        cp.wait()


def solution(mesh):
    nresp = mesh.shape["resp"]
    keys = mesh.shape["ctx"] * BLK

    def body(
        prompt_q, prompt_k, prompt_v, prompt_out, prompt_dout,
        resp_q, resp_k, resp_v, resp_out, resp_dout,
        lengths, resp_row, block_index,
    ):
        shape = jax.ShapeDtypeStruct
        smem = pl.BlockSpec(memory_space=pltpu.SMEM)
        vmem = pl.BlockSpec(memory_space=pltpu.VMEM)
        dma = pltpu.SemaphoreType.DMA
        own = prompt_q.shape[0]
        gather_sems = [dma((NZ,)), dma((NZ,)), dma((NZ,)), dma((NZ,)), dma((NZ, 2)), dma((NZ, 2))]
        parts = pl.pallas_call(
            functools.partial(kernel, nresp),
            out_shape=(
                shape(prompt_q.shape, BF16),
                shape(prompt_k.shape, BF16),
                shape(prompt_v.shape, BF16),
                shape(resp_q.shape, BF16),
                shape(resp_k.shape, BF16),
                shape(resp_v.shape, BF16),
            ),
            in_specs=[smem] * 3 + [vmem] * 10,
            out_specs=(vmem,) * 6,
            scratch_shapes=[
                pltpu.VMEM((keys // BLK, 2, BLK, HD), BF16),
                pltpu.VMEM((own, QW), BF16),
                pltpu.VMEM((own, QW), BF16),
                pltpu.VMEM((own, HD), BF16),
                pltpu.VMEM((own, HD), BF16),
                pltpu.VMEM((own, 128), F32),
                pltpu.VMEM((nresp, 16, 128), F32),
                pltpu.VMEM((2 * QW, HD), BF16),
                pltpu.VMEM((2 * QW, HD), BF16),
                pltpu.VMEM((HD, 2 * QW), BF16),
                pltpu.VMEM((HD, 2 * QW), BF16),
                pltpu.VMEM((keys, 2 * QW), BF16),
                pltpu.VMEM((BLK, QW), BF16),
                pltpu.VMEM((2 * NZ, 2 * QW), F32),
                pltpu.VMEM((1, 2 * QW), F32),
                pltpu.VMEM((1, 2 * QW), F32),
                pltpu.VMEM((1, 2 * QW), F32),
                pltpu.VMEM((HD, 2 * QW), F32),
                pltpu.VMEM((CK, 2 * QW), BF16),
                pltpu.VMEM((CK, 2 * QW), BF16),
                pltpu.VMEM((NZ, 2, 2, 2, BLK, HD), F32),
                pltpu.VMEM((NZ, 2, 2, BLK, HD), F32),
                pltpu.VMEM((NZ, 2, BLK, HD), F32),
                pltpu.VMEM((NZ, 2, BLK, HD), BF16),
                pltpu.VMEM((NZ, 2, BLK, HD), BF16),
                pltpu.VMEM((NZ, 2, BLK, HD), BF16),
                pltpu.VMEM((NZ, 2, BLK, HD), BF16),
                pltpu.VMEM((own, QW), BF16),
                pltpu.VMEM((own, HD), BF16),
                pltpu.VMEM((own, HD), BF16),
            ]
            + gather_sems
            + [
                dma((5, nresp)),
                dma((5, nresp)),
                dma((NZ,)),
                dma((NZ,)),
                dma((NZ,)),
                dma((NZ,)),
                dma((NZ,)),
                dma((NZ,)),
                dma((3, nresp)),
                dma((3, nresp)),
                dma((8,)),
            ],
            compiler_params=pltpu.CompilerParams(
                collective_id=0, has_side_effects=True, vmem_limit_bytes=60 * 1024 * 1024
            ),
            name="attn_bwd",
        )(
            lengths, resp_row, block_index,
            prompt_q, prompt_k, prompt_v, prompt_out, prompt_dout,
            resp_q, resp_k, resp_v, resp_out, resp_dout,
        )
        anywhere = pl.BlockSpec(memory_space=pltpu.HBM)
        return pl.pallas_call(
            settle,
            out_shape=tuple(shape(part.shape, part.dtype) for part in parts),
            in_specs=[anywhere] * 6,
            out_specs=(anywhere,) * 6,
            scratch_shapes=[dma((6,))],
            name="settle",
        )(*parts)

    heads, rows, whole = P("ctx", "resp"), P(("ctx", "resp"), None), P()
    return jax.shard_map(
        body,
        mesh=mesh,
        in_specs=(heads,) * 5 + (rows,) * 5 + (whole,) * 3,
        out_specs=(heads,) * 3 + (rows,) * 3,
        check_vma=False,
    )
```

```python
import functools

import jax
import jax.numpy as jnp
from jax import lax
from jax.experimental import pallas as pl
from jax.experimental.pallas import tpu as pltpu
from jax.sharding import PartitionSpec as P

MESH = pl.DeviceIdType.MESH
F32, BF16 = jnp.float32, jnp.bfloat16
HD = 128
GROUP = 8
BLK = 128
NZ = 8
LEAD = 3
QW = GROUP * BLK
CK = 4 * BLK
QT = 512
SCALE = HD ** -0.5
EXP_SCALE = SCALE * 1.4426950408889634
LOW = -1e30
NEG = float("-inf")
DEAD = 1 << 20


def dot(a, b):
    return jnp.dot(a, b, preferred_element_type=F32)


def kernel(
    nresp,
    len_ref, row_ref, bi_ref,
    pq, pk, pv, pout, pdo, sq, sk, sv, sout, sdo,
    dqp, dkp, dvp, dqr, dkr, dvr,
    kk, vv, lq, lout, ldo, tout, tdo, rq, rdo, rk, rv, rdel, dbuf,
    qa, doa, qT, doT, pt, own_pt, mh, mrun, lrun, delta, dqT, psc, dssc, bias,
    gpart, grecv, kept, ysb, yrb, zsb, zrb, dqrows, dkrows, dvrows, dqloc, dkvloc,
    kzs, kzr, kys, kyr, kcs, kcr, vzs, vzr, vys, vyr, vcs, vcr,
    as_, ar_, gcs, gcr, gys, gyr, gzs, gzr, bs_, br_, loc,
):
    c = lax.axis_index("ctx")
    r = lax.axis_index("resp")
    z = c // 4
    lane4 = c % 4
    core = c % 2
    ylo = lane4 // 2
    cpart = c + 1 - 2 * core
    ystep = 2 - 4 * ylo
    ypart = c + ystep

    def zpeer(d):
        return lax.rem(z + d, NZ) * 4 + lane4

    def rpeer(d):
        return lax.rem(r + d, nresp)

    def remote(src, dst, ss, rs, dev):
        return pltpu.make_async_remote_copy(
            src_ref=src, dst_ref=dst, send_sem=ss, recv_sem=rs, device_id=dev, device_id_type=MESH
        )

    def zoff(i):
        return jnp.where(i % 2 == 1, (i + 1) // 2, (NZ - i // 2) % NZ)

    def cols(ref, p, w):
        return ref.at[:, pl.ds(pl.multiple_of(p * w, 128), w)]

    def slots(ref, p):
        return ref.at[pl.ds(pl.multiple_of(p * 16, 16), 16), :]

    pairs = (
        lambda: (pk, kk.at[c]),
        lambda: (pv, vv.at[c]),
        lambda: (pq, lq),
        lambda: (pdo, ldo),
        lambda: (sdo, tdo),
        lambda: (sout, tout),
        lambda: (pout, lout),
        lambda: (cols(sq, r, QW), slots(rq, r)),
        lambda: (cols(sdo, r, QW), slots(rdo, r)),
        lambda: (cols(sk, r, HD), slots(rk, r)),
        lambda: (cols(sv, r, HD), slots(rv, r)),
        lambda: (dbuf.at[r], slots(rdel, r)),
        lambda: (dqloc, dqp),
        lambda: (dkvloc.at[0], dkp),
        lambda: (dkvloc.at[1], dvp),
        lambda: (slots(dqrows, r), cols(dqr, r, QW)),
        lambda: (slots(dkrows, r), cols(dkr, r, HD)),
        lambda: (slots(dvrows, r), cols(dvr, r, HD)),
    )

    def local(n):
        src, dst = pairs[n]()
        return pltpu.make_async_copy(src, dst, loc.at[n])

    for n in range(11):
        local(n).start()

    barrier = pltpu.get_barrier_semaphore()

    def greet(dev):
        pl.semaphore_signal(barrier, inc=1, device_id=dev, device_id_type=MESH)

    def greet_z(d, carry):
        greet((zpeer(d), r))
        return carry

    def greet_r(d, carry):
        greet((c, rpeer(d)))
        return carry

    lax.fori_loop(1, NZ, greet_z, 0)
    greet((cpart, r))
    greet((ypart, r))
    lax.fori_loop(1, nresp, greet_r, 0)
    pl.semaphore_wait(barrier, (NZ - 1) + (nresp - 1) + 2)

    def kz(d):
        return remote(kk.at[c], kk.at[c], kzs.at[d], kzr.at[NZ - d], (zpeer(d), r))

    def kz_wait(d):
        b = zpeer(d)
        remote(kk.at[b], kk.at[b], kzs.at[d], kzr.at[d], (b, r)).wait_recv()

    def ky(d):
        b = zpeer(d)
        return remote(kk.at[b], kk.at[b], kys.at[d], kyr.at[d], (ypart, r))

    def ky_wait(d):
        b = zpeer(d) + ystep
        remote(kk.at[b], kk.at[b], kys.at[d], kyr.at[d], (ypart, r)).wait_recv()

    def kc(d, far):
        b = zpeer(d) + far * ystep
        return remote(kk.at[b], kk.at[b], kcs.at[d, far], kcr.at[d, far], (cpart, r))

    def kc_wait(d, far):
        b = zpeer(d) + 1 - 2 * core + far * ystep
        remote(kk.at[b], kk.at[b], kcs.at[d, far], kcr.at[d, far], (cpart, r)).wait_recv()

    def pass_near(i):
        @pl.when(i < NZ)
        def _():
            d = zoff(i)
            kz_wait(d)
            ky(d).start()
            kc(d, 0).start()

    def pass_far(i):
        @pl.when(i < NZ)
        def _():
            d = zoff(i)
            ky_wait(d)
            kc(d, 1).start()

    def vy():
        return remote(vv.at[c], vv.at[c], vys.at[0], vyr.at[0], (ypart, r))

    def vy_wait():
        remote(vv.at[ypart], vv.at[ypart], vys.at[0], vyr.at[0], (ypart, r)).wait_recv()

    def vz(d, far):
        b = c + far * ystep
        return remote(vv.at[b], vv.at[b], vzs.at[d, far], vzr.at[NZ - d, far], (zpeer(d), r))

    def vz_wait(d, far):
        b = zpeer(d) + far * ystep
        remote(vv.at[b], vv.at[b], vzs.at[d, far], vzr.at[d, far], (zpeer(d), r)).wait_recv()

    def vc(d, far):
        b = zpeer(d) + far * ystep
        return remote(vv.at[b], vv.at[b], vcs.at[d, far], vcr.at[d, far], (cpart, r))

    def vc_wait(d, far):
        b = zpeer(d) + 1 - 2 * core + far * ystep
        remote(vv.at[b], vv.at[b], vcs.at[d, far], vcr.at[d, far], (cpart, r)).wait_recv()

    local(0).wait()
    ky(0).start()
    kc(0, 0).start()

    def send_keys(i, carry):
        kz(zoff(i)).start()
        return carry

    lax.fori_loop(1, NZ, send_keys, 0)
    local(1).wait()
    vy().start()
    vc(0, 0).start()

    lane = lax.broadcasted_iota(jnp.int32, (128, 128), 1)
    subl = lax.broadcasted_iota(jnp.int32, (128, 128), 0)
    diff = lane - subl
    my = bi_ref[c]

    def load_queries(q, do, base):
        for h in range(GROUP):
            sl = slice(h * HD, (h + 1) * HD)
            out = slice(base + h * BLK, base + (h + 1) * BLK)
            qh, dh = q[:, sl], do[:, sl]
            qa[out, :] = qh
            doa[out, :] = dh
            qT[:, out] = qh.T
            doT[:, out] = dh.T

    def place_delta(rows, base):
        rows_t = rows.T
        for h in range(GROUP):
            delta[:, base + h * BLK: base + (h + 1) * BLK] = rows_t[h:h + 1, :]

    local(2).wait()
    local(3).wait()
    load_queries(lq, ldo, 0)
    mrun[...] = jnp.full((8, 2 * QW), LOW, F32)
    lrun[...] = jnp.zeros((8, 2 * QW), F32)

    def near_first(i, carry):
        pass_near(i)
        return carry

    lax.fori_loop(1, LEAD + 1, near_first, 0)
    pass_far(0)

    def sources(p):
        return (cols(sq, p, QW), cols(sdo, p, QW), cols(sk, p, HD), cols(sv, p, HD), dbuf.at[p])

    landings = (rq, rdo, rk, rv, rdel)

    def exchange(d, which):
        p = rpeer(d)
        src = sources(p)
        return [
            remote(src[n], slots(landings[n], r), as_.at[n, d], ar_.at[n, nresp - d], (c, p))
            for n in which
        ]

    def exchange_in(d):
        p = rpeer(d)
        return [
            remote(slots(landings[n], p), slots(landings[n], p), as_.at[n, d], ar_.at[n, d], (c, p))
            for n in range(5)
        ]

    def send_rows(d, carry):
        for cp in exchange(d, range(4)):
            cp.start()
        return carry

    lax.fori_loop(1, nresp, send_rows, 0)
    local(4).wait()
    local(5).wait()
    lane16 = lax.broadcasted_iota(jnp.int32, (16, 128), 1)
    for g in range(nresp):
        acc = jnp.zeros((16, 128), F32)
        for h in range(GROUP):
            sl = slice((g * GROUP + h) * HD, (g * GROUP + h + 1) * HD)
            prod = tout[:, sl].astype(F32) * tdo[:, sl].astype(F32)
            acc = jnp.where(lane16 == h, jnp.sum(prod, axis=1, keepdims=True), acc)
        dbuf[g] = acc

    def send_delta(d, carry):
        exchange(d, (4,))[0].start()
        return carry

    lax.fori_loop(1, nresp, send_delta, 0)
    local(11).start()
    vy_wait()
    vc(0, 1).start()

    def merge(p3, m, mo, sl):
        mrun[:, sl] = m
        lrun[:, sl] = lrun[:, sl] * jnp.exp2((mo - m) * EXP_SCALE) + jnp.sum(p3, axis=0)

    def stats_chunk(i, base, masked):
        zc = lax.rem(z + zoff(i), NZ)
        if masked:
            for b in range(4):
                ahead = (bi_ref[zc * 4 + b] - my) * BLK
                bias[b * BLK:(b + 1) * BLK, :] = jnp.where(diff >= ahead, 0.0, NEG)
        for t in range(QW // QT):
            sl = slice(base + t * QT, base + (t + 1) * QT)
            for b in range(4):
                s = dot(kk[zc * 4 + b], qT[:, sl])
                if masked:
                    s = s + jnp.concatenate([bias[b * BLK:(b + 1) * BLK, :]] * (QT // BLK), axis=1)
                s3 = s.reshape(BLK // 8, 8, QT)
                mo = mrun[:, sl]
                m = jnp.maximum(mo, jnp.max(s3, axis=0))
                p3 = jnp.exp2((s3 - m[None]) * EXP_SCALE)
                prow = pl.ds(pl.multiple_of(i * CK + b * BLK, BLK), BLK)
                pt[prow, sl] = p3.reshape(BLK, QT).astype(BF16)
                mh[i * 4 + b, :, sl] = m
                merge(p3, m, mo, sl)

    def prompt_stats(i, carry):
        pass_near(i + LEAD + 1)
        pass_far(i + 1)
        d = zoff(i)

        @pl.when(i >= 1)
        def _():
            vz(d, 0).start()
            vz(d, 1).start()

        kc_wait(d, 0)
        kc_wait(d, 1)
        stats_chunk(i, 0, True)
        return carry

    lax.fori_loop(0, NZ, prompt_stats, 0)

    local(6).wait()
    acc = jnp.zeros((BLK, 128), F32)
    for h in range(GROUP):
        sl = slice(h * HD, (h + 1) * HD)
        prod = lout[:, sl].astype(F32) * ldo[:, sl].astype(F32)
        acc = jnp.where(lane == h, jnp.sum(prod, axis=1, keepdims=True), acc)
    place_delta(acc, 0)

    def wait_in(d, carry):
        for cp in exchange_in(d):
            cp.wait_recv()
        return carry

    lax.fori_loop(1, nresp, wait_in, 0)
    for n in range(7, 12):
        local(n).wait()
    load_queries(rq, rdo, QW)
    place_delta(rdel[...], QW)

    lane1 = lax.broadcasted_iota(jnp.int32, (1, 128), 1)
    startq = jnp.full((1, 128), DEAD, jnp.int32)
    cum = jnp.int32(0)
    for n in range(len_ref.shape[0]):
        count = jnp.where(row_ref[n] == c, len_ref[n], 0)
        startq = jnp.where((lane1 >= cum) & (lane1 < cum + count), cum, startq)
        cum = cum + count
    live = jnp.where(startq < DEAD, 1.0, 0.0)
    own_mask = (subl >= startq) & (diff >= 0)
    for h in range(GROUP):
        sl = slice(QW + h * BLK, QW + (h + 1) * BLK)
        s3 = jnp.where(own_mask, dot(rk[...], qT[:, sl]), NEG).reshape(BLK // 8, 8, BLK)
        mo = mrun[:, sl]
        m = jnp.maximum(mo, jnp.max(s3, axis=0))
        p3 = jnp.exp2((s3 - m[None]) * EXP_SCALE)
        own_pt[:, h * BLK:(h + 1) * BLK] = p3.reshape(BLK, BLK).astype(BF16)
        mh[4 * NZ, :, sl] = m
        merge(p3, m, mo, sl)

    def resp_stats(i, carry):
        d = zoff(i)

        @pl.when(i >= 1)
        def _():
            vz_wait(d, 0)
            vc(d, 0).start()
            vz_wait(d, 1)
            vc(d, 1).start()

        stats_chunk(i, QW, False)
        return carry

    lax.fori_loop(0, NZ, resp_stats, 0)

    peak = jnp.max(mrun[...], axis=0, keepdims=True)
    total = jnp.sum(lrun[...] * jnp.exp2((mrun[...] - peak) * EXP_SCALE), axis=0, keepdims=True)
    inv = jnp.where(total > 0.0, 1.0 / total, 0.0)
    inv = inv * jnp.concatenate([jnp.ones((1, QW), F32)] + [live] * GROUP, axis=1)
    for n in range(4 * NZ):
        mh[n] = jnp.exp2((mh[n] - peak) * EXP_SCALE) * inv
    own_f = jnp.exp2((mh[4 * NZ, :, QW:] - peak[:, QW:]) * EXP_SCALE) * inv[:, QW:]
    dqT[...] = jnp.zeros_like(dqT)

    def back(d, which):
        p = rpeer(d)
        dev = (c, p)
        e = nresp - d
        out = (
            lambda: remote(slots(dqrows, p), cols(dqr, r, QW), bs_.at[0, d], br_.at[0, e], dev),
            lambda: remote(slots(dkrows, p), cols(dkr, r, HD), bs_.at[1, d], br_.at[1, e], dev),
            lambda: remote(slots(dvrows, p), cols(dvr, r, HD), bs_.at[2, d], br_.at[2, e], dev),
        )
        return [out[n]() for n in which]

    def back_in(d):
        p = rpeer(d)
        dev = (c, p)
        return [
            remote(cols(dqr, p, QW), cols(dqr, p, QW), bs_.at[0, d], br_.at[0, d], dev),
            remote(cols(dkr, p, HD), cols(dkr, p, HD), bs_.at[1, d], br_.at[1, d], dev),
            remote(cols(dvr, p, HD), cols(dvr, p, HD), bs_.at[2, d], br_.at[2, d], dev),
        ]

    rkT = rk[...].T
    for h in range(GROUP):
        sl = slice(QW + h * BLK, QW + (h + 1) * BLK)
        hs = slice(h * BLK, (h + 1) * BLK)
        dp = dot(rv[...], doT[:, sl])
        p3 = own_pt[:, hs].astype(F32).reshape(BLK // 8, 8, BLK) * own_f[:, hs][None]
        p = p3.reshape(BLK, BLK)
        ds = (p * (dp - delta[:, sl])).astype(BF16)
        psc[0:BLK, sl] = p.astype(BF16)
        dssc[0:BLK, sl] = ds
        dqT[:, sl] += dot(rkT, ds)
    dvrows[...] = dot(psc[0:BLK, QW:], doa[QW:, :]).astype(BF16)
    dkrows[...] = (dot(dssc[0:BLK, QW:], qa[QW:, :]) * SCALE).astype(BF16)

    def send_back_kv(d, carry):
        for cp in back(d, (1, 2)):
            cp.start()
        return carry

    lax.fori_loop(1, nresp, send_back_kv, 0)
    local(16).start()
    local(17).start()

    def core_send(j):
        return remote(gpart.at[j, 1 - core], grecv.at[j], gcs.at[j], gcr.at[j], (cpart, r))

    def y_send(j):
        return remote(ysb.at[j], yrb.at[j], gys.at[j], gyr.at[j], (ypart, r))

    def z_send(j):
        d = zoff(NZ - 1 - j)
        return remote(zsb.at[j], zrb.at[NZ - d], gzs.at[d], gzr.at[NZ - d], (zpeer(d), r))

    def after_core(j):
        core_send(j).wait_recv()
        kept[j] = gpart[j, core, ylo] + grecv[j, ylo]
        ysb[j] = (gpart[j, core, 1 - ylo] + grecv[j, 1 - ylo]).astype(BF16)
        y_send(j).start()

    def after_y(j):
        y_send(j).wait_recv()
        zsb[j] = (kept[j] + yrb[j].astype(F32)).astype(BF16)
        z_send(j).start()

    def grads(j, carry):
        i = NZ - 1 - j
        d = zoff(i)
        zc = lax.rem(z + d, NZ)
        vc_wait(d, 0)
        vc_wait(d, 1)
        vc_rows = vv[pl.ds(zc * 4, 4)].reshape(CK, HD)
        kTc = kk[pl.ds(zc * 4, 4)].reshape(CK, HD).T
        prow = pl.ds(pl.multiple_of(i * CK, CK), CK)
        for t in range(2 * QW // QT):
            sl = slice(t * QT, (t + 1) * QT)
            dp = dot(vc_rows, doT[:, sl])
            f = mh[pl.ds(i * 4, 4), :, sl][:, None]
            p = (pt[prow, sl].astype(F32).reshape(4, BLK // 8, 8, QT) * f).reshape(CK, QT)
            ds = (p * (dp - delta[:, sl])).astype(BF16)
            psc[:, sl] = p.astype(BF16)
            dssc[:, sl] = ds
            dqT[:, sl] += dot(kTc, ds)
        dk = dot(dssc[...], qa[...])
        dv = dot(psc[...], doa[...])
        for b in range(4):
            gpart[j, b % 2, b // 2, 0] = dk[b * BLK:(b + 1) * BLK, :]
            gpart[j, b % 2, b // 2, 1] = dv[b * BLK:(b + 1) * BLK, :]
        core_send(j).start()

        @pl.when(j >= 1)
        def _():
            after_core(j - 1)

        @pl.when(j >= 2)
        def _():
            after_y(j - 2)

        return carry

    lax.fori_loop(0, NZ, grads, 0)

    for h in range(GROUP):
        dqrows[:, h * HD:(h + 1) * HD] = (dqT[:, QW + h * BLK:QW + (h + 1) * BLK].T * SCALE).astype(BF16)

    def send_back_q(d, carry):
        for cp in back(d, (0,)):
            cp.start()
        return carry

    lax.fori_loop(1, nresp, send_back_q, 0)
    local(15).start()

    after_core(NZ - 1)
    after_y(NZ - 2)
    for h in range(GROUP):
        dqloc[:, h * HD:(h + 1) * HD] = (dqT[:, h * BLK:(h + 1) * BLK].T * SCALE).astype(BF16)
    local(12).start()
    y_send(NZ - 1).wait_recv()
    kept[NZ - 1] = kept[NZ - 1] + yrb[NZ - 1].astype(F32)

    def drain_z(d, carry):
        kz(d).wait_send()
        vz(d, 0).wait_send()
        vz(d, 1).wait_send()
        return carry

    def drain_rest(d, carry):
        ky(d).wait_send()
        for far in range(2):
            kc(d, far).wait_send()
            vc(d, far).wait_send()
        return carry

    lax.fori_loop(1, NZ, drain_z, 0)
    lax.fori_loop(0, NZ, drain_rest, 0)
    vy().wait_send()

    def drain_exchange(d, carry):
        for cp in exchange(d, range(5)):
            cp.wait_send()
        return carry

    lax.fori_loop(1, nresp, drain_exchange, 0)

    def drain_parts(j, carry):
        core_send(j).wait_send()
        y_send(j).wait_send()
        return carry

    lax.fori_loop(0, NZ, drain_parts, 0)

    def drain_zparts(j, carry):
        z_send(j).wait_send()
        return carry

    def z_parts(d, carry):
        remote(zrb.at[d], zrb.at[d], gzs.at[d], gzr.at[d], (zpeer(d), r)).wait_recv()
        kept[NZ - 1] = kept[NZ - 1] + zrb[d].astype(F32)
        return carry

    lax.fori_loop(1, NZ, z_parts, 0)
    dkvloc[0] = (kept[NZ - 1, 0] * SCALE).astype(BF16)
    dkvloc[1] = kept[NZ - 1, 1].astype(BF16)
    local(13).start()
    local(14).start()
    lax.fori_loop(0, NZ - 1, drain_zparts, 0)

    def finish_back(d, carry):
        for cp in back(d, range(3)):
            cp.wait_send()
        for cp in back_in(d):
            cp.wait_recv()
        return carry

    lax.fori_loop(1, nresp, finish_back, 0)
    for n in range(12, 18):
        local(n).wait()


def settle(*refs):
    n = len(refs) // 2
    for src, dst in zip(refs[:n], refs[n:]):
        dst[...] = src[...]


def solution(mesh):
    nresp = mesh.shape["resp"]
    nctx = mesh.shape["ctx"]

    def body(
        prompt_q, prompt_k, prompt_v, prompt_out, prompt_dout,
        resp_q, resp_k, resp_v, resp_out, resp_dout,
        lengths, resp_row, block_index,
    ):
        shape = jax.ShapeDtypeStruct
        smem = pl.BlockSpec(memory_space=pltpu.SMEM)
        vmem = pl.BlockSpec(memory_space=pltpu.VMEM)
        dma = pltpu.SemaphoreType.DMA
        anywhere = pl.BlockSpec(memory_space=pl.ANY)
        parts = pl.pallas_call(
            functools.partial(kernel, nresp),
            out_shape=(
                shape(prompt_q.shape, BF16),
                shape(prompt_k.shape, BF16),
                shape(prompt_v.shape, BF16),
                shape(resp_q.shape, BF16),
                shape(resp_k.shape, BF16),
                shape(resp_v.shape, BF16),
            ),
            in_specs=[smem] * 3 + [anywhere] * 10,
            out_specs=(anywhere,) * 6,
            scratch_shapes=[
                pltpu.VMEM((nctx, BLK, HD), BF16),
                pltpu.VMEM((nctx, BLK, HD), BF16),
                pltpu.VMEM((BLK, QW), BF16),
                pltpu.VMEM((BLK, QW), BF16),
                pltpu.VMEM((BLK, QW), BF16),
                pltpu.VMEM(resp_out.shape, BF16),
                pltpu.VMEM(resp_out.shape, BF16),
                pltpu.VMEM((BLK, QW), BF16),
                pltpu.VMEM((BLK, QW), BF16),
                pltpu.VMEM((BLK, HD), BF16),
                pltpu.VMEM((BLK, HD), BF16),
                pltpu.VMEM((BLK, 128), F32),
                pltpu.VMEM((nresp, 16, 128), F32),
                pltpu.VMEM((2 * QW, HD), BF16),
                pltpu.VMEM((2 * QW, HD), BF16),
                pltpu.VMEM((HD, 2 * QW), BF16),
                pltpu.VMEM((HD, 2 * QW), BF16),
                pltpu.VMEM((nctx * BLK, 2 * QW), BF16),
                pltpu.VMEM((BLK, QW), BF16),
                pltpu.VMEM((nctx + 1, 8, 2 * QW), F32),
                pltpu.VMEM((8, 2 * QW), F32),
                pltpu.VMEM((8, 2 * QW), F32),
                pltpu.VMEM((1, 2 * QW), F32),
                pltpu.VMEM((HD, 2 * QW), F32),
                pltpu.VMEM((CK, 2 * QW), BF16),
                pltpu.VMEM((CK, 2 * QW), BF16),
                pltpu.VMEM((CK, BLK), F32),
                pltpu.VMEM((NZ, 2, 2, 2, BLK, HD), F32),
                pltpu.VMEM((NZ, 2, 2, BLK, HD), F32),
                pltpu.VMEM((NZ, 2, BLK, HD), F32),
                pltpu.VMEM((NZ, 2, BLK, HD), BF16),
                pltpu.VMEM((NZ, 2, BLK, HD), BF16),
                pltpu.VMEM((NZ, 2, BLK, HD), BF16),
                pltpu.VMEM((NZ, 2, BLK, HD), BF16),
                pltpu.VMEM((BLK, QW), BF16),
                pltpu.VMEM((BLK, HD), BF16),
                pltpu.VMEM((BLK, HD), BF16),
                pltpu.VMEM((BLK, QW), BF16),
                pltpu.VMEM((2, BLK, HD), BF16),
                dma((NZ,)), dma((NZ,)), dma((NZ,)), dma((NZ,)), dma((NZ, 2)), dma((NZ, 2)),
                dma((NZ, 2)), dma((NZ, 2)), dma((1,)), dma((1,)), dma((NZ, 2)), dma((NZ, 2)),
                dma((5, nresp)), dma((5, nresp)),
                dma((NZ,)), dma((NZ,)), dma((NZ,)), dma((NZ,)), dma((NZ,)), dma((NZ,)),
                dma((3, nresp)), dma((3, nresp)),
                dma((18,)),
            ],
            compiler_params=pltpu.CompilerParams(
                collective_id=0, has_side_effects=True, vmem_limit_bytes=60 * 1024 * 1024
            ),
            name="attn_bwd",
        )(
            lengths, resp_row, block_index,
            prompt_q, prompt_k, prompt_v, prompt_out, prompt_dout,
            resp_q, resp_k, resp_v, resp_out, resp_dout,
        )
        return pl.pallas_call(
            settle,
            out_shape=tuple(shape(part.shape, part.dtype) for part in parts),
            in_specs=[vmem] * 6,
            out_specs=(vmem,) * 6,
            compiler_params=pltpu.CompilerParams(vmem_limit_bytes=60 * 1024 * 1024),
            name="settle",
        )(*parts)

    heads, rows, whole = P("ctx", "resp"), P(("ctx", "resp"), None), P()
    return jax.shard_map(
        body,
        mesh=mesh,
        in_specs=(heads,) * 5 + (rows,) * 5 + (whole,) * 3,
        out_specs=(heads,) * 3 + (rows,) * 3,
        check_vma=False,
    )
```

```python
import functools

import jax
import jax.numpy as jnp
from jax import lax
from jax.experimental import pallas as pl
from jax.experimental.pallas import tpu as pltpu
from jax.sharding import PartitionSpec as P

MESH = pl.DeviceIdType.MESH
F32, BF16 = jnp.float32, jnp.bfloat16
HD = 128
GROUP = 8
BLK = 128
NZ = 8
QW = GROUP * BLK
CK = 4 * BLK
QT = 512
SCALE = HD ** -0.5
EXP_SCALE = SCALE * 1.4426950408889634
LOW = -1e30
NEG = float("-inf")
DEAD = 1 << 20


def dot(a, b):
    return jnp.dot(a, b, preferred_element_type=F32)


def kernel(
    nresp,
    len_ref, row_ref, bi_ref,
    pq, pk, pv, pout, pdo, sq, sk, sv, sout, sdo,
    dqp, dkp, dvp, dqr, dkr, dvr,
    kk, vv, lq, lout, ldo, tout, tdo, rq, rdo, rk, rv, rdel, dbuf,
    qa, doa, qT, doT, pt, own_pt, mh, mrun, lrun, delta, dqT, psc, dssc, bias,
    gpart, grecv, kept, ysb, yrb, zsb, zrb, dqrows, dkrows, dvrows, dqloc, dkvloc,
    kzs, kzr, kys, kyr, kcs, kcr, vzs, vzr, vys, vyr, vcs, vcr,
    as_, ar_, gcs, gcr, gys, gyr, gzs, gzr, bs_, br_, loc,
):
    c = lax.axis_index("ctx")
    r = lax.axis_index("resp")
    z = c // 4
    lane4 = c % 4
    core = c % 2
    ylo = lane4 // 2
    cpart = c + 1 - 2 * core
    ystep = 2 - 4 * ylo
    ypart = c + ystep

    def zpeer(d):
        return lax.rem(z + d, NZ) * 4 + lane4

    def rpeer(d):
        return lax.rem(r + d, nresp)

    def remote(src, dst, ss, rs, dev):
        return pltpu.make_async_remote_copy(
            src_ref=src, dst_ref=dst, send_sem=ss, recv_sem=rs, device_id=dev, device_id_type=MESH
        )

    def zoff(i):
        return jnp.where(i % 2 == 1, (i + 1) // 2, (NZ - i // 2) % NZ)

    def cols(ref, p, w):
        return ref.at[:, pl.ds(pl.multiple_of(p * w, 128), w)]

    def slots(ref, p):
        return ref.at[pl.ds(pl.multiple_of(p * 16, 16), 16), :]

    pairs = (
        lambda: (pk, kk.at[c]),
        lambda: (pv, vv.at[c]),
        lambda: (pq, lq),
        lambda: (pdo, ldo),
        lambda: (sdo, tdo),
        lambda: (sout, tout),
        lambda: (pout, lout),
        lambda: (cols(sq, r, QW), slots(rq, r)),
        lambda: (cols(sdo, r, QW), slots(rdo, r)),
        lambda: (cols(sk, r, HD), slots(rk, r)),
        lambda: (cols(sv, r, HD), slots(rv, r)),
        lambda: (dbuf.at[r], slots(rdel, r)),
        lambda: (dqloc, dqp),
        lambda: (dkvloc.at[0], dkp),
        lambda: (dkvloc.at[1], dvp),
        lambda: (slots(dqrows, r), cols(dqr, r, QW)),
        lambda: (slots(dkrows, r), cols(dkr, r, HD)),
        lambda: (slots(dvrows, r), cols(dvr, r, HD)),
    )

    def local(n):
        src, dst = pairs[n]()
        return pltpu.make_async_copy(src, dst, loc.at[n])

    for n in range(11):
        local(n).start()

    barrier = pltpu.get_barrier_semaphore()

    def greet(dev):
        pl.semaphore_signal(barrier, inc=1, device_id=dev, device_id_type=MESH)

    def greet_z(d, carry):
        greet((zpeer(d), r))
        return carry

    def greet_r(d, carry):
        greet((c, rpeer(d)))
        return carry

    lax.fori_loop(1, NZ, greet_z, 0)
    greet((cpart, r))
    greet((ypart, r))
    lax.fori_loop(1, nresp, greet_r, 0)
    pl.semaphore_wait(barrier, (NZ - 1) + (nresp - 1) + 2)

    ksems = (kk, kzs, kzr, kys, kyr, kcs, kcr)
    vsems = (vv, vzs, vzr, vys, vyr, vcs, vcr)

    def y_swap(sems):
        ref, zs, zr, ys, yr, cs, cr = sems
        return remote(ref.at[c], ref.at[c], ys.at[0], yr.at[0], (ypart, r))

    def y_wait(sems):
        ref, zs, zr, ys, yr, cs, cr = sems
        remote(ref.at[ypart], ref.at[ypart], ys.at[0], yr.at[0], (ypart, r)).wait_recv()

    def hop(sems, d, e, far, to):
        ref, zs, zr, ys, yr, cs, cr = sems
        b = zpeer(d) + far * ystep
        return remote(ref.at[b], ref.at[b], zs.at[e, far], zr.at[e, far], (to, r))

    def hop_wait(sems, d, far):
        ref, zs, zr, ys, yr, cs, cr = sems
        b = zpeer(d) + far * ystep
        remote(ref.at[b], ref.at[b], zs.at[d, far], zr.at[d, far], (zpeer(1), r)).wait_recv()

    def share(sems, d, far):
        ref, zs, zr, ys, yr, cs, cr = sems
        b = zpeer(d) + far * ystep
        return remote(ref.at[b], ref.at[b], cs.at[d, far], cr.at[d, far], (cpart, r))

    def share_wait(sems, d, far):
        ref, zs, zr, ys, yr, cs, cr = sems
        b = zpeer(d) + 1 - 2 * core + far * ystep
        remote(ref.at[b], ref.at[b], cs.at[d, far], cr.at[d, far], (cpart, r)).wait_recv()

    def begin(sems, far):
        hop(sems, 0, 1, far, zpeer(NZ - 1)).start()
        hop(sems, 0, NZ - 1, far, zpeer(1)).start()
        share(sems, 0, far).start()

    def relay(sems, i):
        d = zoff(i)
        odd = i % 2 == 1
        e = jnp.where(odd, d + 1, d - 1)
        to = jnp.where(odd, zpeer(NZ - 1), zpeer(1))
        for far in range(2):
            hop_wait(sems, d, far)

            @pl.when((i <= NZ - 4) | (i == NZ - 3 + far))
            def _():
                hop(sems, d, e, far, to).start()

            share(sems, d, far).start()

    def drain_gather(sems):
        ref, zs, zr, ys, yr, cs, cr = sems

        def drain_hops(e, carry):
            for far in range(2):
                hop(sems, 0, e, far, zpeer(1)).wait_send()
            return carry

        def drain_shares(d, carry):
            for far in range(2):
                share(sems, d, far).wait_send()
            return carry

        lax.fori_loop(1, NZ, drain_hops, 0)
        lax.fori_loop(0, NZ, drain_shares, 0)
        y_swap(sems).wait_send()

    def sources(p):
        return (cols(sq, p, QW), cols(sdo, p, QW), cols(sk, p, HD), cols(sv, p, HD), dbuf.at[p])

    landings = (rq, rdo, rk, rv, rdel)

    def exchange(d, which):
        p = rpeer(d)
        src = sources(p)
        return [
            remote(src[n], slots(landings[n], r), as_.at[n, d], ar_.at[n, nresp - d], (c, p))
            for n in which
        ]

    def exchange_in(d):
        p = rpeer(d)
        return [
            remote(slots(landings[n], p), slots(landings[n], p), as_.at[n, d], ar_.at[n, d], (c, p))
            for n in range(5)
        ]

    def send_rows(d, carry):
        for cp in exchange(d, range(4)):
            cp.start()
        return carry

    local(0).wait()
    y_swap(ksems).start()
    begin(ksems, 0)
    local(1).wait()
    y_swap(vsems).start()
    y_wait(ksems)
    begin(ksems, 1)
    begin(vsems, 0)
    y_wait(vsems)
    begin(vsems, 1)
    lax.fori_loop(1, nresp, send_rows, 0)

    lane = lax.broadcasted_iota(jnp.int32, (128, 128), 1)
    subl = lax.broadcasted_iota(jnp.int32, (128, 128), 0)
    diff = lane - subl
    my = bi_ref[c]

    def load_queries(q, do, base):
        for h in range(GROUP):
            sl = slice(h * HD, (h + 1) * HD)
            out = slice(base + h * BLK, base + (h + 1) * BLK)
            qh, dh = q[:, sl], do[:, sl]
            qa[out, :] = qh
            doa[out, :] = dh
            qT[:, out] = qh.T
            doT[:, out] = dh.T

    def place_delta(rows, base):
        rows_t = rows.T
        for h in range(GROUP):
            delta[:, base + h * BLK: base + (h + 1) * BLK] = rows_t[h:h + 1, :]

    local(2).wait()
    local(3).wait()
    load_queries(lq, ldo, 0)
    mrun[...] = jnp.full((8, 2 * QW), LOW, F32)
    lrun[...] = jnp.zeros((8, 2 * QW), F32)

    relay(ksems, 1)
    local(4).wait()
    local(5).wait()
    lane16 = lax.broadcasted_iota(jnp.int32, (16, 128), 1)
    for g in range(nresp):
        acc = jnp.zeros((16, 128), F32)
        for h in range(GROUP):
            sl = slice((g * GROUP + h) * HD, (g * GROUP + h + 1) * HD)
            prod = tout[:, sl].astype(F32) * tdo[:, sl].astype(F32)
            acc = jnp.where(lane16 == h, jnp.sum(prod, axis=1, keepdims=True), acc)
        dbuf[g] = acc

    def send_delta(d, carry):
        exchange(d, (4,))[0].start()
        return carry

    lax.fori_loop(1, nresp, send_delta, 0)
    local(11).start()

    def merge(p3, m, mo, sl):
        mrun[:, sl] = m
        lrun[:, sl] = lrun[:, sl] * jnp.exp2((mo - m) * EXP_SCALE) + jnp.sum(p3, axis=0)

    def stats_chunk(i, base, masked):
        zc = lax.rem(z + zoff(i), NZ)
        if masked:
            for b in range(4):
                ahead = (bi_ref[zc * 4 + b] - my) * BLK
                bias[b * BLK:(b + 1) * BLK, :] = jnp.where(diff >= ahead, 0.0, NEG)
        for t in range(QW // QT):
            sl = slice(base + t * QT, base + (t + 1) * QT)
            for b in range(4):
                s = dot(kk[zc * 4 + b], qT[:, sl])
                if masked:
                    s = s + jnp.concatenate([bias[b * BLK:(b + 1) * BLK, :]] * (QT // BLK), axis=1)
                s3 = s.reshape(BLK // 8, 8, QT)
                mo = mrun[:, sl]
                m = jnp.maximum(mo, jnp.max(s3, axis=0))
                p3 = jnp.exp2((s3 - m[None]) * EXP_SCALE)
                prow = pl.ds(pl.multiple_of(i * CK + b * BLK, BLK), BLK)
                pt[prow, sl] = p3.reshape(BLK, QT).astype(BF16)
                mh[i * 4 + b, :, sl] = m
                merge(p3, m, mo, sl)

    def prompt_stats(i, carry):
        @pl.when(i < NZ - 2)
        def _():
            relay(ksems, i + 2)

        @pl.when(i < NZ - 1)
        def _():
            relay(vsems, i + 1)

        d = zoff(i)
        share_wait(ksems, d, 0)
        share_wait(ksems, d, 1)
        stats_chunk(i, 0, True)
        return carry

    lax.fori_loop(0, NZ, prompt_stats, 0)

    local(6).wait()
    acc = jnp.zeros((BLK, 128), F32)
    for h in range(GROUP):
        sl = slice(h * HD, (h + 1) * HD)
        prod = lout[:, sl].astype(F32) * ldo[:, sl].astype(F32)
        acc = jnp.where(lane == h, jnp.sum(prod, axis=1, keepdims=True), acc)
    place_delta(acc, 0)

    def wait_in(d, carry):
        for cp in exchange_in(d):
            cp.wait_recv()
        return carry

    lax.fori_loop(1, nresp, wait_in, 0)
    for n in range(7, 12):
        local(n).wait()
    load_queries(rq, rdo, QW)
    place_delta(rdel[...], QW)

    lane1 = lax.broadcasted_iota(jnp.int32, (1, 128), 1)
    startq = jnp.full((1, 128), DEAD, jnp.int32)
    cum = jnp.int32(0)
    for n in range(len_ref.shape[0]):
        count = jnp.where(row_ref[n] == c, len_ref[n], 0)
        startq = jnp.where((lane1 >= cum) & (lane1 < cum + count), cum, startq)
        cum = cum + count
    live = jnp.where(startq < DEAD, 1.0, 0.0)
    own_mask = (subl >= startq) & (diff >= 0)
    for h in range(GROUP):
        sl = slice(QW + h * BLK, QW + (h + 1) * BLK)
        s3 = jnp.where(own_mask, dot(rk[...], qT[:, sl]), NEG).reshape(BLK // 8, 8, BLK)
        mo = mrun[:, sl]
        m = jnp.maximum(mo, jnp.max(s3, axis=0))
        p3 = jnp.exp2((s3 - m[None]) * EXP_SCALE)
        own_pt[:, h * BLK:(h + 1) * BLK] = p3.reshape(BLK, BLK).astype(BF16)
        mh[4 * NZ, :, sl] = m
        merge(p3, m, mo, sl)

    def resp_stats(i, carry):
        stats_chunk(i, QW, False)
        return carry

    lax.fori_loop(0, NZ, resp_stats, 0)

    peak = jnp.max(mrun[...], axis=0, keepdims=True)
    total = jnp.sum(lrun[...] * jnp.exp2((mrun[...] - peak) * EXP_SCALE), axis=0, keepdims=True)
    inv = jnp.where(total > 0.0, 1.0 / total, 0.0)
    inv = inv * jnp.concatenate([jnp.ones((1, QW), F32)] + [live] * GROUP, axis=1)
    for n in range(4 * NZ):
        mh[n] = jnp.exp2((mh[n] - peak) * EXP_SCALE) * inv
    own_f = jnp.exp2((mh[4 * NZ, :, QW:] - peak[:, QW:]) * EXP_SCALE) * inv[:, QW:]
    dqT[...] = jnp.zeros_like(dqT)

    def back(d, which):
        p = rpeer(d)
        dev = (c, p)
        e = nresp - d
        out = (
            lambda: remote(slots(dqrows, p), cols(dqr, r, QW), bs_.at[0, d], br_.at[0, e], dev),
            lambda: remote(slots(dkrows, p), cols(dkr, r, HD), bs_.at[1, d], br_.at[1, e], dev),
            lambda: remote(slots(dvrows, p), cols(dvr, r, HD), bs_.at[2, d], br_.at[2, e], dev),
        )
        return [out[n]() for n in which]

    def back_in(d):
        p = rpeer(d)
        dev = (c, p)
        return [
            remote(cols(dqr, p, QW), cols(dqr, p, QW), bs_.at[0, d], br_.at[0, d], dev),
            remote(cols(dkr, p, HD), cols(dkr, p, HD), bs_.at[1, d], br_.at[1, d], dev),
            remote(cols(dvr, p, HD), cols(dvr, p, HD), bs_.at[2, d], br_.at[2, d], dev),
        ]

    rkT = rk[...].T
    for h in range(GROUP):
        sl = slice(QW + h * BLK, QW + (h + 1) * BLK)
        hs = slice(h * BLK, (h + 1) * BLK)
        dp = dot(rv[...], doT[:, sl])
        p3 = own_pt[:, hs].astype(F32).reshape(BLK // 8, 8, BLK) * own_f[:, hs][None]
        p = p3.reshape(BLK, BLK)
        ds = (p * (dp - delta[:, sl])).astype(BF16)
        psc[0:BLK, sl] = p.astype(BF16)
        dssc[0:BLK, sl] = ds
        dqT[:, sl] += dot(rkT, ds)
    dvrows[...] = dot(psc[0:BLK, QW:], doa[QW:, :]).astype(BF16)
    dkrows[...] = (dot(dssc[0:BLK, QW:], qa[QW:, :]) * SCALE).astype(BF16)

    def send_back_kv(d, carry):
        for cp in back(d, (1, 2)):
            cp.start()
        return carry

    lax.fori_loop(1, nresp, send_back_kv, 0)
    local(16).start()
    local(17).start()

    def core_send(j):
        return remote(gpart.at[j, 1 - core], grecv.at[j], gcs.at[j], gcr.at[j], (cpart, r))

    def y_send(j):
        return remote(ysb.at[j], yrb.at[j], gys.at[j], gyr.at[j], (ypart, r))

    def z_send(j):
        d = zoff(NZ - 1 - j)
        return remote(zsb.at[j], zrb.at[NZ - d], gzs.at[d], gzr.at[NZ - d], (zpeer(d), r))

    def after_core(j):
        core_send(j).wait_recv()
        kept[j] = gpart[j, core, ylo] + grecv[j, ylo]
        ysb[j] = (gpart[j, core, 1 - ylo] + grecv[j, 1 - ylo]).astype(BF16)
        y_send(j).start()

    def after_y(j):
        y_send(j).wait_recv()
        zsb[j] = (kept[j] + yrb[j].astype(F32)).astype(BF16)
        z_send(j).start()

    def grads(j, carry):
        i = NZ - 1 - j
        d = zoff(i)
        zc = lax.rem(z + d, NZ)
        share_wait(vsems, d, 0)
        share_wait(vsems, d, 1)
        vc_rows = vv[pl.ds(zc * 4, 4)].reshape(CK, HD)
        kTc = kk[pl.ds(zc * 4, 4)].reshape(CK, HD).T
        prow = pl.ds(pl.multiple_of(i * CK, CK), CK)
        for t in range(2 * QW // QT):
            sl = slice(t * QT, (t + 1) * QT)
            dp = dot(vc_rows, doT[:, sl])
            f = mh[pl.ds(i * 4, 4), :, sl][:, None]
            p = (pt[prow, sl].astype(F32).reshape(4, BLK // 8, 8, QT) * f).reshape(CK, QT)
            ds = (p * (dp - delta[:, sl])).astype(BF16)
            psc[:, sl] = p.astype(BF16)
            dssc[:, sl] = ds
            dqT[:, sl] += dot(kTc, ds)
        dk = dot(dssc[...], qa[...])
        dv = dot(psc[...], doa[...])
        for b in range(4):
            gpart[j, b % 2, b // 2, 0] = dk[b * BLK:(b + 1) * BLK, :]
            gpart[j, b % 2, b // 2, 1] = dv[b * BLK:(b + 1) * BLK, :]
        core_send(j).start()

        @pl.when(j >= 1)
        def _():
            after_core(j - 1)

        @pl.when(j >= 2)
        def _():
            after_y(j - 2)

        return carry

    lax.fori_loop(0, NZ, grads, 0)

    for h in range(GROUP):
        dqrows[:, h * HD:(h + 1) * HD] = (dqT[:, QW + h * BLK:QW + (h + 1) * BLK].T * SCALE).astype(BF16)

    def send_back_q(d, carry):
        for cp in back(d, (0,)):
            cp.start()
        return carry

    lax.fori_loop(1, nresp, send_back_q, 0)
    local(15).start()

    after_core(NZ - 1)
    after_y(NZ - 2)
    for h in range(GROUP):
        dqloc[:, h * HD:(h + 1) * HD] = (dqT[:, h * BLK:(h + 1) * BLK].T * SCALE).astype(BF16)
    local(12).start()
    y_send(NZ - 1).wait_recv()
    kept[NZ - 1] = kept[NZ - 1] + yrb[NZ - 1].astype(F32)

    drain_gather(ksems)
    drain_gather(vsems)

    def drain_exchange(d, carry):
        for cp in exchange(d, range(5)):
            cp.wait_send()
        return carry

    lax.fori_loop(1, nresp, drain_exchange, 0)

    def drain_parts(j, carry):
        core_send(j).wait_send()
        y_send(j).wait_send()
        return carry

    lax.fori_loop(0, NZ, drain_parts, 0)

    def drain_zparts(j, carry):
        z_send(j).wait_send()
        return carry

    def z_parts(d, carry):
        remote(zrb.at[d], zrb.at[d], gzs.at[d], gzr.at[d], (zpeer(d), r)).wait_recv()
        kept[NZ - 1] = kept[NZ - 1] + zrb[d].astype(F32)
        return carry

    lax.fori_loop(1, NZ, z_parts, 0)
    dkvloc[0] = (kept[NZ - 1, 0] * SCALE).astype(BF16)
    dkvloc[1] = kept[NZ - 1, 1].astype(BF16)
    local(13).start()
    local(14).start()
    lax.fori_loop(0, NZ - 1, drain_zparts, 0)

    def finish_back(d, carry):
        for cp in back(d, range(3)):
            cp.wait_send()
        for cp in back_in(d):
            cp.wait_recv()
        return carry

    lax.fori_loop(1, nresp, finish_back, 0)
    for n in range(12, 18):
        local(n).wait()


def settle(*refs):
    n = len(refs) // 2
    for src, dst in zip(refs[:n], refs[n:]):
        dst[...] = src[...]


def solution(mesh):
    nresp = mesh.shape["resp"]
    nctx = mesh.shape["ctx"]

    def body(
        prompt_q, prompt_k, prompt_v, prompt_out, prompt_dout,
        resp_q, resp_k, resp_v, resp_out, resp_dout,
        lengths, resp_row, block_index,
    ):
        shape = jax.ShapeDtypeStruct
        smem = pl.BlockSpec(memory_space=pltpu.SMEM)
        vmem = pl.BlockSpec(memory_space=pltpu.VMEM)
        dma = pltpu.SemaphoreType.DMA
        anywhere = pl.BlockSpec(memory_space=pl.ANY)
        parts = pl.pallas_call(
            functools.partial(kernel, nresp),
            out_shape=(
                shape(prompt_q.shape, BF16),
                shape(prompt_k.shape, BF16),
                shape(prompt_v.shape, BF16),
                shape(resp_q.shape, BF16),
                shape(resp_k.shape, BF16),
                shape(resp_v.shape, BF16),
            ),
            in_specs=[smem] * 3 + [anywhere] * 10,
            out_specs=(anywhere,) * 6,
            scratch_shapes=[
                pltpu.VMEM((nctx, BLK, HD), BF16),
                pltpu.VMEM((nctx, BLK, HD), BF16),
                pltpu.VMEM((BLK, QW), BF16),
                pltpu.VMEM((BLK, QW), BF16),
                pltpu.VMEM((BLK, QW), BF16),
                pltpu.VMEM(resp_out.shape, BF16),
                pltpu.VMEM(resp_out.shape, BF16),
                pltpu.VMEM((BLK, QW), BF16),
                pltpu.VMEM((BLK, QW), BF16),
                pltpu.VMEM((BLK, HD), BF16),
                pltpu.VMEM((BLK, HD), BF16),
                pltpu.VMEM((BLK, 128), F32),
                pltpu.VMEM((nresp, 16, 128), F32),
                pltpu.VMEM((2 * QW, HD), BF16),
                pltpu.VMEM((2 * QW, HD), BF16),
                pltpu.VMEM((HD, 2 * QW), BF16),
                pltpu.VMEM((HD, 2 * QW), BF16),
                pltpu.VMEM((nctx * BLK, 2 * QW), BF16),
                pltpu.VMEM((BLK, QW), BF16),
                pltpu.VMEM((nctx + 1, 8, 2 * QW), F32),
                pltpu.VMEM((8, 2 * QW), F32),
                pltpu.VMEM((8, 2 * QW), F32),
                pltpu.VMEM((1, 2 * QW), F32),
                pltpu.VMEM((HD, 2 * QW), F32),
                pltpu.VMEM((CK, 2 * QW), BF16),
                pltpu.VMEM((CK, 2 * QW), BF16),
                pltpu.VMEM((CK, BLK), F32),
                pltpu.VMEM((NZ, 2, 2, 2, BLK, HD), F32),
                pltpu.VMEM((NZ, 2, 2, BLK, HD), F32),
                pltpu.VMEM((NZ, 2, BLK, HD), F32),
                pltpu.VMEM((NZ, 2, BLK, HD), BF16),
                pltpu.VMEM((NZ, 2, BLK, HD), BF16),
                pltpu.VMEM((NZ, 2, BLK, HD), BF16),
                pltpu.VMEM((NZ, 2, BLK, HD), BF16),
                pltpu.VMEM((BLK, QW), BF16),
                pltpu.VMEM((BLK, HD), BF16),
                pltpu.VMEM((BLK, HD), BF16),
                pltpu.VMEM((BLK, QW), BF16),
                pltpu.VMEM((2, BLK, HD), BF16),
                dma((NZ, 2)), dma((NZ, 2)), dma((1,)), dma((1,)), dma((NZ, 2)), dma((NZ, 2)),
                dma((NZ, 2)), dma((NZ, 2)), dma((1,)), dma((1,)), dma((NZ, 2)), dma((NZ, 2)),
                dma((5, nresp)), dma((5, nresp)),
                dma((NZ,)), dma((NZ,)), dma((NZ,)), dma((NZ,)), dma((NZ,)), dma((NZ,)),
                dma((3, nresp)), dma((3, nresp)),
                dma((18,)),
            ],
            compiler_params=pltpu.CompilerParams(
                collective_id=0, has_side_effects=True, vmem_limit_bytes=60 * 1024 * 1024
            ),
            name="attn_bwd",
        )(
            lengths, resp_row, block_index,
            prompt_q, prompt_k, prompt_v, prompt_out, prompt_dout,
            resp_q, resp_k, resp_v, resp_out, resp_dout,
        )
        return pl.pallas_call(
            settle,
            out_shape=tuple(shape(part.shape, part.dtype) for part in parts),
            in_specs=[vmem] * 6,
            out_specs=(vmem,) * 6,
            compiler_params=pltpu.CompilerParams(vmem_limit_bytes=60 * 1024 * 1024),
            name="settle",
        )(*parts)

    heads, rows, whole = P("ctx", "resp"), P(("ctx", "resp"), None), P()
    return jax.shard_map(
        body,
        mesh=mesh,
        in_specs=(heads,) * 5 + (rows,) * 5 + (whole,) * 3,
        out_specs=(heads,) * 3 + (rows,) * 3,
        check_vma=False,
    )
```

```python
import functools

import jax
import jax.numpy as jnp
from jax import lax
from jax.experimental import pallas as pl
from jax.experimental.pallas import tpu as pltpu
from jax.sharding import PartitionSpec as P

MESH = pl.DeviceIdType.MESH
F32, BF16 = jnp.float32, jnp.bfloat16
HD = 128
GROUP = 8
BLK = 128
NZ = 8
LEAD = 3
QW = GROUP * BLK
CK = 4 * BLK
QT = 512
SCALE = HD ** -0.5
EXP_SCALE = SCALE * 1.4426950408889634
LOW = -1e30
NEG = float("-inf")
DEAD = 1 << 20


def dot(a, b):
    return jnp.dot(a, b, preferred_element_type=F32)


def kernel(
    nresp,
    len_ref, row_ref, bi_ref,
    pq, pk, pv, pout, pdo, sq, sk, sv, sout, sdo,
    dqp, dkp, dvp, dqr, dkr, dvr,
    kk, vv, lq, lout, ldo, tout, tdo, rq, rdo, rk, rv, rdel, dbuf,
    qa, doa, qT, doT, pt, own_pt, mh, mrun, lrun, delta, dqT, psc, dssc, bias,
    gpart, grecv, kept, ysb, yrb, zsb, zrb, dqrows, dkrows, dvrows, dqloc, dkvloc,
    kzs, kzr, kys, kyr, kcs, kcr, vzs, vzr, vys, vyr, vcs, vcr,
    as_, ar_, gcs, gcr, gys, gyr, gzs, gzr, bs_, br_, loc,
):
    c = lax.axis_index("ctx")
    r = lax.axis_index("resp")
    z = c // 4
    lane4 = c % 4
    core = c % 2
    ylo = lane4 // 2
    cpart = c + 1 - 2 * core
    ystep = 2 - 4 * ylo
    ypart = c + ystep

    def zpeer(d):
        return lax.rem(z + d, NZ) * 4 + lane4

    def rpeer(d):
        return lax.rem(r + d, nresp)

    def remote(src, dst, ss, rs, dev):
        return pltpu.make_async_remote_copy(
            src_ref=src, dst_ref=dst, send_sem=ss, recv_sem=rs, device_id=dev, device_id_type=MESH
        )

    def zoff(i):
        return jnp.where(i % 2 == 1, (i + 1) // 2, (NZ - i // 2) % NZ)

    def cols(ref, p, w):
        return ref.at[:, pl.ds(pl.multiple_of(p * w, 128), w)]

    def slots(ref, p):
        return ref.at[pl.ds(pl.multiple_of(p * 16, 16), 16), :]

    pairs = (
        lambda: (pk, kk.at[c]),
        lambda: (pv, vv.at[c]),
        lambda: (pq, lq),
        lambda: (pdo, ldo),
        lambda: (sdo, tdo),
        lambda: (sout, tout),
        lambda: (pout, lout),
        lambda: (cols(sq, r, QW), slots(rq, r)),
        lambda: (cols(sdo, r, QW), slots(rdo, r)),
        lambda: (cols(sk, r, HD), slots(rk, r)),
        lambda: (cols(sv, r, HD), slots(rv, r)),
        lambda: (dbuf.at[r], slots(rdel, r)),
        lambda: (dqloc, dqp),
        lambda: (dkvloc.at[0], dkp),
        lambda: (dkvloc.at[1], dvp),
        lambda: (slots(dqrows, r), cols(dqr, r, QW)),
        lambda: (slots(dkrows, r), cols(dkr, r, HD)),
        lambda: (slots(dvrows, r), cols(dvr, r, HD)),
    )

    def local(n):
        src, dst = pairs[n]()
        return pltpu.make_async_copy(src, dst, loc.at[n])

    for n in range(11):
        local(n).start()

    barrier = pltpu.get_barrier_semaphore()

    def greet(dev):
        pl.semaphore_signal(barrier, inc=1, device_id=dev, device_id_type=MESH)

    def greet_z(d, carry):
        greet((zpeer(d), r))
        return carry

    def greet_r(d, carry):
        greet((c, rpeer(d)))
        return carry

    lax.fori_loop(1, NZ, greet_z, 0)
    greet((cpart, r))
    greet((ypart, r))
    lax.fori_loop(1, nresp, greet_r, 0)
    pl.semaphore_wait(barrier, (NZ - 1) + (nresp - 1) + 2)

    ksems = (kk, kzs, kzr, kys, kyr, kcs, kcr)
    vsems = (vv, vzs, vzr, vys, vyr, vcs, vcr)

    def swap(sems, d):
        ref, zs, zr, ys, yr, cs, cr = sems
        b = zpeer(d)
        return remote(ref.at[b], ref.at[b], ys.at[d], yr.at[d], (ypart, r))

    def swap_wait(sems, d):
        ref, zs, zr, ys, yr, cs, cr = sems
        b = zpeer(d) + ystep
        remote(ref.at[b], ref.at[b], ys.at[d], yr.at[d], (ypart, r)).wait_recv()

    def hop(sems, d, e, far):
        ref, zs, zr, ys, yr, cs, cr = sems
        b = zpeer(d) + far * ystep
        to = (zpeer(lax.rem(d - e + NZ, NZ)), r)
        return remote(ref.at[b], ref.at[b], zs.at[e, far], zr.at[e, far], to)

    def hop_wait(sems, d, far):
        ref, zs, zr, ys, yr, cs, cr = sems
        b = zpeer(d) + far * ystep
        remote(ref.at[b], ref.at[b], zs.at[d, far], zr.at[d, far], (zpeer(1), r)).wait_recv()

    def share(sems, d, far):
        ref, zs, zr, ys, yr, cs, cr = sems
        b = zpeer(d) + far * ystep
        return remote(ref.at[b], ref.at[b], cs.at[d, far], cr.at[d, far], (cpart, r))

    def share_wait(sems, d, far):
        ref, zs, zr, ys, yr, cs, cr = sems
        b = zpeer(d) + 1 - 2 * core + far * ystep
        remote(ref.at[b], ref.at[b], cs.at[d, far], cr.at[d, far], (cpart, r)).wait_recv()

    def send_keys(i, carry):
        hop(ksems, 0, zoff(i), 0).start()
        return carry

    def key_near(i):
        @pl.when(i < NZ)
        def _():
            d = zoff(i)
            hop_wait(ksems, d, 0)
            swap(ksems, d).start()
            share(ksems, d, 0).start()

    def key_far(i):
        @pl.when(i < NZ)
        def _():
            d = zoff(i)
            swap_wait(ksems, d)
            share(ksems, d, 1).start()

    def send_values(far):
        for e in (1, NZ - 1, 2, NZ - 2):
            hop(vsems, 0, e, far).start()
        share(vsems, 0, far).start()

    def value_step(i):
        d = zoff(i)
        for far in range(2):
            hop_wait(vsems, d, far)

            @pl.when(i == 3)
            def _():
                hop(vsems, 2, 3, far).start()

            @pl.when(i == 4)
            def _():
                hop(vsems, NZ - 2, NZ - 3, far).start()

            @pl.when(i == 3 + far)
            def _():
                hop(vsems, d, 4, far).start()

            share(vsems, d, far).start()

    def drain_gather():
        def drain_hops(e, carry):
            hop(ksems, 0, e, 0).wait_send()
            for far in range(2):
                hop(vsems, 0, e, far).wait_send()
            return carry

        def drain_shares(d, carry):
            swap(ksems, d).wait_send()
            for far in range(2):
                share(ksems, d, far).wait_send()
                share(vsems, d, far).wait_send()
            return carry

        lax.fori_loop(1, NZ, drain_hops, 0)
        lax.fori_loop(0, NZ, drain_shares, 0)
        swap(vsems, 0).wait_send()

    def sources(p):
        return (cols(sq, p, QW), cols(sdo, p, QW), cols(sk, p, HD), cols(sv, p, HD), dbuf.at[p])

    landings = (rq, rdo, rk, rv, rdel)

    def exchange(d, which):
        p = rpeer(d)
        src = sources(p)
        return [
            remote(src[n], slots(landings[n], r), as_.at[n, d], ar_.at[n, nresp - d], (c, p))
            for n in which
        ]

    def exchange_in(d):
        p = rpeer(d)
        return [
            remote(slots(landings[n], p), slots(landings[n], p), as_.at[n, d], ar_.at[n, d], (c, p))
            for n in range(5)
        ]

    def send_rows(n, carry):
        for cp in exchange(n, range(4)):
            cp.start()
        return carry

    local(0).wait()
    swap(ksems, 0).start()
    share(ksems, 0, 0).start()
    lax.fori_loop(1, NZ, send_keys, 0)
    local(1).wait()
    swap(vsems, 0).start()
    lax.fori_loop(1, nresp // 2, lambda n, carry: send_rows(2 * n, carry), 0)

    lane = lax.broadcasted_iota(jnp.int32, (128, 128), 1)
    subl = lax.broadcasted_iota(jnp.int32, (128, 128), 0)
    diff = lane - subl
    my = bi_ref[c]

    def load_queries(q, do, base):
        for h in range(GROUP):
            sl = slice(h * HD, (h + 1) * HD)
            out = slice(base + h * BLK, base + (h + 1) * BLK)
            qh, dh = q[:, sl], do[:, sl]
            qa[out, :] = qh
            doa[out, :] = dh
            qT[:, out] = qh.T
            doT[:, out] = dh.T

    def place_delta(rows, base):
        rows_t = rows.T
        for h in range(GROUP):
            delta[:, base + h * BLK: base + (h + 1) * BLK] = rows_t[h:h + 1, :]

    local(2).wait()
    local(3).wait()
    load_queries(lq, ldo, 0)
    mrun[...] = jnp.full((8, 2 * QW), LOW, F32)
    lrun[...] = jnp.zeros((8, 2 * QW), F32)

    def near_first(i, carry):
        key_near(i)
        return carry

    lax.fori_loop(1, LEAD + 1, near_first, 0)
    key_far(0)
    lax.fori_loop(0, nresp // 2, lambda n, carry: send_rows(2 * n + 1, carry), 0)
    send_values(0)
    swap_wait(vsems, 0)
    send_values(1)
    local(4).wait()
    local(5).wait()
    lane16 = lax.broadcasted_iota(jnp.int32, (16, 128), 1)
    for g in range(nresp):
        acc = jnp.zeros((16, 128), F32)
        for h in range(GROUP):
            sl = slice((g * GROUP + h) * HD, (g * GROUP + h + 1) * HD)
            prod = tout[:, sl].astype(F32) * tdo[:, sl].astype(F32)
            acc = jnp.where(lane16 == h, jnp.sum(prod, axis=1, keepdims=True), acc)
        dbuf[g] = acc

    def send_delta(d, carry):
        exchange(d, (4,))[0].start()
        return carry

    lax.fori_loop(1, nresp, send_delta, 0)
    local(11).start()

    def merge(p3, m, mo, sl):
        mrun[:, sl] = m
        lrun[:, sl] = lrun[:, sl] * jnp.exp2((mo - m) * EXP_SCALE) + jnp.sum(p3, axis=0)

    def stats_chunk(i, base, masked):
        zc = lax.rem(z + zoff(i), NZ)
        if masked:
            for b in range(4):
                ahead = (bi_ref[zc * 4 + b] - my) * BLK
                bias[b * BLK:(b + 1) * BLK, :] = jnp.where(diff >= ahead, 0.0, NEG)
        for t in range(QW // QT):
            sl = slice(base + t * QT, base + (t + 1) * QT)
            for b in range(4):
                s = dot(kk[zc * 4 + b], qT[:, sl])
                if masked:
                    s = s + jnp.concatenate([bias[b * BLK:(b + 1) * BLK, :]] * (QT // BLK), axis=1)
                s3 = s.reshape(BLK // 8, 8, QT)
                mo = mrun[:, sl]
                m = jnp.maximum(mo, jnp.max(s3, axis=0))
                p3 = jnp.exp2((s3 - m[None]) * EXP_SCALE)
                prow = pl.ds(pl.multiple_of(i * CK + b * BLK, BLK), BLK)
                pt[prow, sl] = p3.reshape(BLK, QT).astype(BF16)
                mh[i * 4 + b, :, sl] = m
                merge(p3, m, mo, sl)

    def prompt_stats(i, carry):
        key_near(i + LEAD + 1)
        key_far(i + 1)

        @pl.when(i >= NZ - 4)
        def _():
            value_step(i - (NZ - 5))

        d = zoff(i)
        share_wait(ksems, d, 0)
        share_wait(ksems, d, 1)
        stats_chunk(i, 0, True)
        return carry

    lax.fori_loop(0, NZ, prompt_stats, 0)

    local(6).wait()
    acc = jnp.zeros((BLK, 128), F32)
    for h in range(GROUP):
        sl = slice(h * HD, (h + 1) * HD)
        prod = lout[:, sl].astype(F32) * ldo[:, sl].astype(F32)
        acc = jnp.where(lane == h, jnp.sum(prod, axis=1, keepdims=True), acc)
    place_delta(acc, 0)

    def wait_in(d, carry):
        for cp in exchange_in(d):
            cp.wait_recv()
        return carry

    lax.fori_loop(1, nresp, wait_in, 0)
    for n in range(7, 12):
        local(n).wait()
    load_queries(rq, rdo, QW)
    place_delta(rdel[...], QW)

    lane1 = lax.broadcasted_iota(jnp.int32, (1, 128), 1)
    startq = jnp.full((1, 128), DEAD, jnp.int32)
    cum = jnp.int32(0)
    for n in range(len_ref.shape[0]):
        count = jnp.where(row_ref[n] == c, len_ref[n], 0)
        startq = jnp.where((lane1 >= cum) & (lane1 < cum + count), cum, startq)
        cum = cum + count
    live = jnp.where(startq < DEAD, 1.0, 0.0)
    own_mask = (subl >= startq) & (diff >= 0)
    for h in range(GROUP):
        sl = slice(QW + h * BLK, QW + (h + 1) * BLK)
        s3 = jnp.where(own_mask, dot(rk[...], qT[:, sl]), NEG).reshape(BLK // 8, 8, BLK)
        mo = mrun[:, sl]
        m = jnp.maximum(mo, jnp.max(s3, axis=0))
        p3 = jnp.exp2((s3 - m[None]) * EXP_SCALE)
        own_pt[:, h * BLK:(h + 1) * BLK] = p3.reshape(BLK, BLK).astype(BF16)
        mh[4 * NZ, :, sl] = m
        merge(p3, m, mo, sl)

    def resp_stats(i, carry):
        @pl.when(i < NZ - 5)
        def _():
            value_step(i + NZ - 3)

        stats_chunk(i, QW, False)
        return carry

    lax.fori_loop(0, NZ, resp_stats, 0)

    peak = jnp.max(mrun[...], axis=0, keepdims=True)
    total = jnp.sum(lrun[...] * jnp.exp2((mrun[...] - peak) * EXP_SCALE), axis=0, keepdims=True)
    inv = jnp.where(total > 0.0, 1.0 / total, 0.0)
    inv = inv * jnp.concatenate([jnp.ones((1, QW), F32)] + [live] * GROUP, axis=1)
    for n in range(4 * NZ):
        mh[n] = jnp.exp2((mh[n] - peak) * EXP_SCALE) * inv
    own_f = jnp.exp2((mh[4 * NZ, :, QW:] - peak[:, QW:]) * EXP_SCALE) * inv[:, QW:]
    dqT[...] = jnp.zeros_like(dqT)

    def back(d, which):
        p = rpeer(d)
        dev = (c, p)
        e = nresp - d
        out = (
            lambda: remote(slots(dqrows, p), cols(dqr, r, QW), bs_.at[0, d], br_.at[0, e], dev),
            lambda: remote(slots(dkrows, p), cols(dkr, r, HD), bs_.at[1, d], br_.at[1, e], dev),
            lambda: remote(slots(dvrows, p), cols(dvr, r, HD), bs_.at[2, d], br_.at[2, e], dev),
        )
        return [out[n]() for n in which]

    def back_in(d):
        p = rpeer(d)
        dev = (c, p)
        return [
            remote(cols(dqr, p, QW), cols(dqr, p, QW), bs_.at[0, d], br_.at[0, d], dev),
            remote(cols(dkr, p, HD), cols(dkr, p, HD), bs_.at[1, d], br_.at[1, d], dev),
            remote(cols(dvr, p, HD), cols(dvr, p, HD), bs_.at[2, d], br_.at[2, d], dev),
        ]

    rkT = rk[...].T
    for h in range(GROUP):
        sl = slice(QW + h * BLK, QW + (h + 1) * BLK)
        hs = slice(h * BLK, (h + 1) * BLK)
        dp = dot(rv[...], doT[:, sl])
        p3 = own_pt[:, hs].astype(F32).reshape(BLK // 8, 8, BLK) * own_f[:, hs][None]
        p = p3.reshape(BLK, BLK)
        ds = (p * (dp - delta[:, sl])).astype(BF16)
        psc[0:BLK, sl] = p.astype(BF16)
        dssc[0:BLK, sl] = ds
        dqT[:, sl] += dot(rkT, ds)
    dvrows[...] = dot(psc[0:BLK, QW:], doa[QW:, :]).astype(BF16)
    dkrows[...] = (dot(dssc[0:BLK, QW:], qa[QW:, :]) * SCALE).astype(BF16)

    def send_back_kv(d, carry):
        for cp in back(d, (1, 2)):
            cp.start()
        return carry

    lax.fori_loop(1, nresp, send_back_kv, 0)
    local(16).start()
    local(17).start()

    def core_send(j):
        return remote(gpart.at[j, 1 - core], grecv.at[j], gcs.at[j], gcr.at[j], (cpart, r))

    def y_send(j):
        return remote(ysb.at[j], yrb.at[j], gys.at[j], gyr.at[j], (ypart, r))

    def z_send(j):
        d = zoff(NZ - 1 - j)
        return remote(zsb.at[j], zrb.at[NZ - d], gzs.at[d], gzr.at[NZ - d], (zpeer(d), r))

    def after_core(j):
        core_send(j).wait_recv()
        kept[j] = gpart[j, core, ylo] + grecv[j, ylo]
        ysb[j] = (gpart[j, core, 1 - ylo] + grecv[j, 1 - ylo]).astype(BF16)
        y_send(j).start()

    def after_y(j):
        y_send(j).wait_recv()
        zsb[j] = (kept[j] + yrb[j].astype(F32)).astype(BF16)
        z_send(j).start()

    def grads(j, carry):
        i = NZ - 1 - j
        d = zoff(i)
        zc = lax.rem(z + d, NZ)
        share_wait(vsems, d, 0)
        share_wait(vsems, d, 1)
        vc_rows = vv[pl.ds(zc * 4, 4)].reshape(CK, HD)
        kTc = kk[pl.ds(zc * 4, 4)].reshape(CK, HD).T
        prow = pl.ds(pl.multiple_of(i * CK, CK), CK)
        for t in range(2 * QW // QT):
            sl = slice(t * QT, (t + 1) * QT)
            dp = dot(vc_rows, doT[:, sl])
            f = mh[pl.ds(i * 4, 4), :, sl][:, None]
            p = (pt[prow, sl].astype(F32).reshape(4, BLK // 8, 8, QT) * f).reshape(CK, QT)
            ds = (p * (dp - delta[:, sl])).astype(BF16)
            psc[:, sl] = p.astype(BF16)
            dssc[:, sl] = ds
            dqT[:, sl] += dot(kTc, ds)
            if t == 1:
                @pl.when(j >= 1)
                def _():
                    after_core(j - 1)

        dk = dot(dssc[...], qa[...])
        dv = dot(psc[...], doa[...])
        for b in range(4):
            gpart[j, b % 2, b // 2, 0] = dk[b * BLK:(b + 1) * BLK, :]
            gpart[j, b % 2, b // 2, 1] = dv[b * BLK:(b + 1) * BLK, :]
        core_send(j).start()

        @pl.when(j >= 1)
        def _():
            after_y(j - 1)

        return carry

    lax.fori_loop(0, NZ, grads, 0)

    for h in range(GROUP):
        dqrows[:, h * HD:(h + 1) * HD] = (dqT[:, QW + h * BLK:QW + (h + 1) * BLK].T * SCALE).astype(BF16)

    def send_back_q(d, carry):
        for cp in back(d, (0,)):
            cp.start()
        return carry

    lax.fori_loop(1, nresp, send_back_q, 0)
    local(15).start()

    after_core(NZ - 1)
    for h in range(GROUP):
        dqloc[:, h * HD:(h + 1) * HD] = (dqT[:, h * BLK:(h + 1) * BLK].T * SCALE).astype(BF16)
    local(12).start()
    y_send(NZ - 1).wait_recv()
    kept[NZ - 1] = kept[NZ - 1] + yrb[NZ - 1].astype(F32)

    drain_gather()

    def drain_exchange(d, carry):
        for cp in exchange(d, range(5)):
            cp.wait_send()
        return carry

    lax.fori_loop(1, nresp, drain_exchange, 0)

    def drain_parts(j, carry):
        core_send(j).wait_send()
        y_send(j).wait_send()
        return carry

    lax.fori_loop(0, NZ, drain_parts, 0)

    def drain_zparts(j, carry):
        z_send(j).wait_send()
        return carry

    def z_parts(d, carry):
        remote(zrb.at[d], zrb.at[d], gzs.at[d], gzr.at[d], (zpeer(d), r)).wait_recv()
        kept[NZ - 1] = kept[NZ - 1] + zrb[d].astype(F32)
        return carry

    lax.fori_loop(1, NZ, z_parts, 0)
    dkvloc[0] = (kept[NZ - 1, 0] * SCALE).astype(BF16)
    dkvloc[1] = kept[NZ - 1, 1].astype(BF16)
    local(13).start()
    local(14).start()
    lax.fori_loop(0, NZ - 1, drain_zparts, 0)

    def finish_back(d, carry):
        for cp in back(d, range(3)):
            cp.wait_send()
        for cp in back_in(d):
            cp.wait_recv()
        return carry

    lax.fori_loop(1, nresp, finish_back, 0)
    for n in range(12, 18):
        local(n).wait()


def settle(*refs):
    n = len(refs) // 2
    for src, dst in zip(refs[:n], refs[n:]):
        dst[...] = src[...]


def solution(mesh):
    nresp = mesh.shape["resp"]
    nctx = mesh.shape["ctx"]

    def body(
        prompt_q, prompt_k, prompt_v, prompt_out, prompt_dout,
        resp_q, resp_k, resp_v, resp_out, resp_dout,
        lengths, resp_row, block_index,
    ):
        shape = jax.ShapeDtypeStruct
        smem = pl.BlockSpec(memory_space=pltpu.SMEM)
        vmem = pl.BlockSpec(memory_space=pltpu.VMEM)
        dma = pltpu.SemaphoreType.DMA
        anywhere = pl.BlockSpec(memory_space=pl.ANY)
        parts = pl.pallas_call(
            functools.partial(kernel, nresp),
            out_shape=(
                shape(prompt_q.shape, BF16),
                shape(prompt_k.shape, BF16),
                shape(prompt_v.shape, BF16),
                shape(resp_q.shape, BF16),
                shape(resp_k.shape, BF16),
                shape(resp_v.shape, BF16),
            ),
            in_specs=[smem] * 3 + [anywhere] * 10,
            out_specs=(anywhere,) * 6,
            scratch_shapes=[
                pltpu.VMEM((nctx, BLK, HD), BF16),
                pltpu.VMEM((nctx, BLK, HD), BF16),
                pltpu.VMEM((BLK, QW), BF16),
                pltpu.VMEM((BLK, QW), BF16),
                pltpu.VMEM((BLK, QW), BF16),
                pltpu.VMEM(resp_out.shape, BF16),
                pltpu.VMEM(resp_out.shape, BF16),
                pltpu.VMEM((BLK, QW), BF16),
                pltpu.VMEM((BLK, QW), BF16),
                pltpu.VMEM((BLK, HD), BF16),
                pltpu.VMEM((BLK, HD), BF16),
                pltpu.VMEM((BLK, 128), F32),
                pltpu.VMEM((nresp, 16, 128), F32),
                pltpu.VMEM((2 * QW, HD), BF16),
                pltpu.VMEM((2 * QW, HD), BF16),
                pltpu.VMEM((HD, 2 * QW), BF16),
                pltpu.VMEM((HD, 2 * QW), BF16),
                pltpu.VMEM((nctx * BLK, 2 * QW), BF16),
                pltpu.VMEM((BLK, QW), BF16),
                pltpu.VMEM((nctx + 1, 8, 2 * QW), F32),
                pltpu.VMEM((8, 2 * QW), F32),
                pltpu.VMEM((8, 2 * QW), F32),
                pltpu.VMEM((1, 2 * QW), F32),
                pltpu.VMEM((HD, 2 * QW), F32),
                pltpu.VMEM((CK, 2 * QW), BF16),
                pltpu.VMEM((CK, 2 * QW), BF16),
                pltpu.VMEM((CK, BLK), F32),
                pltpu.VMEM((NZ, 2, 2, 2, BLK, HD), F32),
                pltpu.VMEM((NZ, 2, 2, BLK, HD), F32),
                pltpu.VMEM((NZ, 2, BLK, HD), F32),
                pltpu.VMEM((NZ, 2, BLK, HD), BF16),
                pltpu.VMEM((NZ, 2, BLK, HD), BF16),
                pltpu.VMEM((NZ, 2, BLK, HD), BF16),
                pltpu.VMEM((NZ, 2, BLK, HD), BF16),
                pltpu.VMEM((BLK, QW), BF16),
                pltpu.VMEM((BLK, HD), BF16),
                pltpu.VMEM((BLK, HD), BF16),
                pltpu.VMEM((BLK, QW), BF16),
                pltpu.VMEM((2, BLK, HD), BF16),
                dma((NZ, 2)), dma((NZ, 2)), dma((NZ,)), dma((NZ,)), dma((NZ, 2)), dma((NZ, 2)),
                dma((NZ, 2)), dma((NZ, 2)), dma((NZ,)), dma((NZ,)), dma((NZ, 2)), dma((NZ, 2)),
                dma((5, nresp)), dma((5, nresp)),
                dma((NZ,)), dma((NZ,)), dma((NZ,)), dma((NZ,)), dma((NZ,)), dma((NZ,)),
                dma((3, nresp)), dma((3, nresp)),
                dma((18,)),
            ],
            compiler_params=pltpu.CompilerParams(
                collective_id=0, has_side_effects=True, vmem_limit_bytes=60 * 1024 * 1024
            ),
            name="attn_bwd",
        )(
            lengths, resp_row, block_index,
            prompt_q, prompt_k, prompt_v, prompt_out, prompt_dout,
            resp_q, resp_k, resp_v, resp_out, resp_dout,
        )
        return pl.pallas_call(
            settle,
            out_shape=tuple(shape(part.shape, part.dtype) for part in parts),
            in_specs=[vmem] * 6,
            out_specs=(vmem,) * 6,
            compiler_params=pltpu.CompilerParams(vmem_limit_bytes=60 * 1024 * 1024),
            name="settle",
        )(*parts)

    heads, rows, whole = P("ctx", "resp"), P(("ctx", "resp"), None), P()
    return jax.shard_map(
        body,
        mesh=mesh,
        in_specs=(heads,) * 5 + (rows,) * 5 + (whole,) * 3,
        out_specs=(heads,) * 3 + (rows,) * 3,
        check_vma=False,
    )
```

```python
import functools

import jax
import jax.numpy as jnp
from jax import lax
from jax.experimental import pallas as pl
from jax.experimental.pallas import tpu as pltpu
from jax.sharding import PartitionSpec as P

MESH = pl.DeviceIdType.MESH
F32, BF16 = jnp.float32, jnp.bfloat16
HD = 128
GROUP = 8
BLK = 128
NZ = 8
QW = GROUP * BLK
CK = 4 * BLK
QT = 512
SCALE = HD ** -0.5
EXP_SCALE = SCALE * 1.4426950408889634
LOW = -1e30
NEG = float("-inf")
DEAD = 1 << 20


def dot(a, b):
    return jnp.dot(a, b, preferred_element_type=F32)


def kernel(
    nresp,
    len_ref, row_ref, bi_ref,
    pq, pk, pv, pout, pdo, sq, sk, sv, sout, sdo,
    dqp, dkp, dvp, dqr, dkr, dvr,
    kk, vv, lq, lout, ldo, tout, tdo, rq, rdo, rk, rv, rdel, dbuf,
    qa, doa, qT, doT, pt, own_pt, mh, mrun, lrun, delta, dqT, psc, dssc, bias,
    gpart, grecv, kept, ysb, yrb, zsb, zrb, dqrows, dkrows, dvrows, dqloc, dkvloc,
    kzs, kzr, kys, kyr, kcs, kcr, vzs, vzr, vys, vyr, vcs, vcr,
    as_, ar_, gcs, gcr, gys, gyr, gzs, gzr, bs_, br_, loc,
):
    c = lax.axis_index("ctx")
    r = lax.axis_index("resp")
    z = c // 4
    lane4 = c % 4
    core = c % 2
    ylo = lane4 // 2
    cpart = c + 1 - 2 * core
    ystep = 2 - 4 * ylo
    ypart = c + ystep

    def zpeer(d):
        return lax.rem(z + d, NZ) * 4 + lane4

    def rpeer(d):
        return lax.rem(r + d, nresp)

    def remote(src, dst, ss, rs, dev):
        return pltpu.make_async_remote_copy(
            src_ref=src, dst_ref=dst, send_sem=ss, recv_sem=rs, device_id=dev, device_id_type=MESH
        )

    def zoff(i):
        return jnp.where(i % 2 == 1, (i + 1) // 2, (NZ - i // 2) % NZ)

    def cols(ref, p, w):
        return ref.at[:, pl.ds(pl.multiple_of(p * w, 128), w)]

    def slots(ref, p):
        return ref.at[pl.ds(pl.multiple_of(p * 16, 16), 16), :]

    pairs = (
        lambda: (pk, kk.at[c]),
        lambda: (pv, vv.at[c]),
        lambda: (pq, lq),
        lambda: (pdo, ldo),
        lambda: (sdo, tdo),
        lambda: (sout, tout),
        lambda: (pout, lout),
        lambda: (cols(sq, r, QW), slots(rq, r)),
        lambda: (cols(sdo, r, QW), slots(rdo, r)),
        lambda: (cols(sk, r, HD), slots(rk, r)),
        lambda: (cols(sv, r, HD), slots(rv, r)),
        lambda: (dbuf.at[r], slots(rdel, r)),
        lambda: (dqloc, dqp),
        lambda: (dkvloc.at[0], dkp),
        lambda: (dkvloc.at[1], dvp),
        lambda: (slots(dqrows, r), cols(dqr, r, QW)),
        lambda: (slots(dkrows, r), cols(dkr, r, HD)),
        lambda: (slots(dvrows, r), cols(dvr, r, HD)),
    )

    def local(n):
        src, dst = pairs[n]()
        return pltpu.make_async_copy(src, dst, loc.at[n])

    for n in range(11):
        local(n).start()

    barrier = pltpu.get_barrier_semaphore()

    def greet(dev):
        pl.semaphore_signal(barrier, inc=1, device_id=dev, device_id_type=MESH)

    def greet_z(d, carry):
        greet((zpeer(d), r))
        return carry

    def greet_r(d, carry):
        greet((c, rpeer(d)))
        return carry

    lax.fori_loop(1, NZ, greet_z, 0)
    greet((cpart, r))
    greet((ypart, r))
    lax.fori_loop(1, nresp, greet_r, 0)
    pl.semaphore_wait(barrier, (NZ - 1) + (nresp - 1) + 2)

    ksems = (kk, kzs, kzr, kys, kyr, kcs, kcr)
    vsems = (vv, vzs, vzr, vys, vyr, vcs, vcr)

    def swap(sems):
        ref, zs, zr, ys, yr, cs, cr = sems
        return remote(ref.at[c], ref.at[c], ys.at[0], yr.at[0], (ypart, r))

    def swap_wait(sems):
        ref, zs, zr, ys, yr, cs, cr = sems
        remote(ref.at[ypart], ref.at[ypart], ys.at[0], yr.at[0], (ypart, r)).wait_recv()

    def hop(sems, d, e, far):
        ref, zs, zr, ys, yr, cs, cr = sems
        b = zpeer(d) + far * ystep
        to = (zpeer(lax.rem(d - e + NZ, NZ)), r)
        return remote(ref.at[b], ref.at[b], zs.at[e, far], zr.at[e, far], to)

    def hop_wait(sems, d, far):
        ref, zs, zr, ys, yr, cs, cr = sems
        b = zpeer(d) + far * ystep
        remote(ref.at[b], ref.at[b], zs.at[d, far], zr.at[d, far], (zpeer(1), r)).wait_recv()

    def share(sems, d, far):
        ref, zs, zr, ys, yr, cs, cr = sems
        b = zpeer(d) + far * ystep
        return remote(ref.at[b], ref.at[b], cs.at[d, far], cr.at[d, far], (cpart, r))

    def share_wait(sems, d, far):
        ref, zs, zr, ys, yr, cs, cr = sems
        b = zpeer(d) + 1 - 2 * core + far * ystep
        remote(ref.at[b], ref.at[b], cs.at[d, far], cr.at[d, far], (cpart, r)).wait_recv()

    def begin(sems, far):
        for e in (1, NZ - 1, 2, NZ - 2):
            hop(sems, 0, e, far).start()
        share(sems, 0, far).start()

    def arrived(sems, i):
        d = zoff(i)
        for far in range(2):
            hop_wait(sems, d, far)
            share(sems, d, far).start()

    def relay(sems, d, e):
        for far in range(2):
            hop_wait(sems, d, far)
            hop(sems, d, e, far).start()
        hop(sems, d, NZ // 2, d // (NZ // 2)).start()
        for far in range(2):
            share(sems, d, far).start()

    def drain_gather(sems):
        def drain_hops(e, carry):
            for far in range(2):
                hop(sems, 0, e, far).wait_send()
            return carry

        def drain_shares(d, carry):
            for far in range(2):
                share(sems, d, far).wait_send()
            return carry

        lax.fori_loop(1, NZ, drain_hops, 0)
        lax.fori_loop(0, NZ, drain_shares, 0)
        swap(sems).wait_send()

    def sources(p):
        return (cols(sq, p, QW), cols(sdo, p, QW), cols(sk, p, HD), cols(sv, p, HD), dbuf.at[p])

    landings = (rq, rdo, rk, rv, rdel)

    def exchange(d, which):
        p = rpeer(d)
        src = sources(p)
        return [
            remote(src[n], slots(landings[n], r), as_.at[n, d], ar_.at[n, nresp - d], (c, p))
            for n in which
        ]

    def exchange_in(d):
        p = rpeer(d)
        return [
            remote(slots(landings[n], p), slots(landings[n], p), as_.at[n, d], ar_.at[n, d], (c, p))
            for n in range(5)
        ]

    def send_rows(n, carry):
        for cp in exchange(n, range(4)):
            cp.start()
        return carry

    local(0).wait()
    swap(ksems).start()
    begin(ksems, 0)
    local(1).wait()
    swap(vsems).start()
    lax.fori_loop(1, nresp, send_rows, 0)
    swap_wait(ksems)
    begin(ksems, 1)

    lane = lax.broadcasted_iota(jnp.int32, (128, 128), 1)
    subl = lax.broadcasted_iota(jnp.int32, (128, 128), 0)
    diff = lane - subl
    my = bi_ref[c]

    def load_queries(q, do, base):
        for h in range(GROUP):
            sl = slice(h * HD, (h + 1) * HD)
            out = slice(base + h * BLK, base + (h + 1) * BLK)
            qh, dh = q[:, sl], do[:, sl]
            qa[out, :] = qh
            doa[out, :] = dh
            qT[:, out] = qh.T
            doT[:, out] = dh.T

    def place_delta(rows, base):
        rows_t = rows.T
        for h in range(GROUP):
            delta[:, base + h * BLK: base + (h + 1) * BLK] = rows_t[h:h + 1, :]

    local(2).wait()
    local(3).wait()
    load_queries(lq, ldo, 0)
    mrun[...] = jnp.full((8, 2 * QW), LOW, F32)
    lrun[...] = jnp.zeros((8, 2 * QW), F32)

    local(4).wait()
    local(5).wait()
    lane16 = lax.broadcasted_iota(jnp.int32, (16, 128), 1)
    for g in range(nresp):
        acc = jnp.zeros((16, 128), F32)
        for h in range(GROUP):
            sl = slice((g * GROUP + h) * HD, (g * GROUP + h + 1) * HD)
            prod = tout[:, sl].astype(F32) * tdo[:, sl].astype(F32)
            acc = jnp.where(lane16 == h, jnp.sum(prod, axis=1, keepdims=True), acc)
        dbuf[g] = acc

    def send_delta(d, carry):
        exchange(d, (4,))[0].start()
        return carry

    lax.fori_loop(1, nresp, send_delta, 0)
    local(11).start()

    def merge(p3, m, mo, sl):
        mrun[:, sl] = m
        lrun[:, sl] = lrun[:, sl] * jnp.exp2((mo - m) * EXP_SCALE) + jnp.sum(p3, axis=0)

    def stats_chunk(i, base, masked):
        zc = lax.rem(z + zoff(i), NZ)
        if masked:
            for b in range(4):
                ahead = (bi_ref[zc * 4 + b] - my) * BLK
                bias[b * BLK:(b + 1) * BLK, :] = jnp.where(diff >= ahead, 0.0, NEG)
        for t in range(QW // QT):
            sl = slice(base + t * QT, base + (t + 1) * QT)
            for b in range(4):
                s = dot(kk[zc * 4 + b], qT[:, sl])
                if masked:
                    s = s + jnp.concatenate([bias[b * BLK:(b + 1) * BLK, :]] * (QT // BLK), axis=1)
                s3 = s.reshape(BLK // 8, 8, QT)
                mo = mrun[:, sl]
                m = jnp.maximum(mo, jnp.max(s3, axis=0))
                p3 = jnp.exp2((s3 - m[None]) * EXP_SCALE)
                prow = pl.ds(pl.multiple_of(i * CK + b * BLK, BLK), BLK)
                pt[prow, sl] = p3.reshape(BLK, QT).astype(BF16)
                mh[i * 4 + b, :, sl] = m
                merge(p3, m, mo, sl)

    def prompt_stats(i, carry):
        @pl.when(i == 1)
        def _():
            relay(ksems, 2, 3)
            relay(ksems, NZ - 2, NZ - 3)
            begin(vsems, 0)
            arrived(ksems, 1)
            arrived(ksems, 2)

        @pl.when(i == 3)
        def _():
            swap_wait(vsems)
            begin(vsems, 1)

        @pl.when(i == 5)
        def _():
            for n in range(5, NZ):
                arrived(ksems, n)

        d = zoff(i)
        share_wait(ksems, d, 0)
        share_wait(ksems, d, 1)
        stats_chunk(i, 0, True)
        return carry

    lax.fori_loop(0, NZ, prompt_stats, 0)

    local(6).wait()
    acc = jnp.zeros((BLK, 128), F32)
    for h in range(GROUP):
        sl = slice(h * HD, (h + 1) * HD)
        prod = lout[:, sl].astype(F32) * ldo[:, sl].astype(F32)
        acc = jnp.where(lane == h, jnp.sum(prod, axis=1, keepdims=True), acc)
    place_delta(acc, 0)

    def wait_in(d, carry):
        for cp in exchange_in(d):
            cp.wait_recv()
        return carry

    lax.fori_loop(1, nresp, wait_in, 0)
    for n in range(7, 12):
        local(n).wait()
    load_queries(rq, rdo, QW)
    place_delta(rdel[...], QW)

    lane1 = lax.broadcasted_iota(jnp.int32, (1, 128), 1)
    startq = jnp.full((1, 128), DEAD, jnp.int32)
    cum = jnp.int32(0)
    for n in range(len_ref.shape[0]):
        count = jnp.where(row_ref[n] == c, len_ref[n], 0)
        startq = jnp.where((lane1 >= cum) & (lane1 < cum + count), cum, startq)
        cum = cum + count
    live = jnp.where(startq < DEAD, 1.0, 0.0)
    own_mask = (subl >= startq) & (diff >= 0)
    for h in range(GROUP):
        sl = slice(QW + h * BLK, QW + (h + 1) * BLK)
        s3 = jnp.where(own_mask, dot(rk[...], qT[:, sl]), NEG).reshape(BLK // 8, 8, BLK)
        mo = mrun[:, sl]
        m = jnp.maximum(mo, jnp.max(s3, axis=0))
        p3 = jnp.exp2((s3 - m[None]) * EXP_SCALE)
        own_pt[:, h * BLK:(h + 1) * BLK] = p3.reshape(BLK, BLK).astype(BF16)
        mh[4 * NZ, :, sl] = m
        merge(p3, m, mo, sl)

    def resp_stats(i, carry):
        @pl.when(i == 2)
        def _():
            relay(vsems, 2, 3)
            relay(vsems, NZ - 2, NZ - 3)
            arrived(vsems, 1)
            arrived(vsems, 2)

        stats_chunk(i, QW, False)
        return carry

    lax.fori_loop(0, NZ, resp_stats, 0)

    peak = jnp.max(mrun[...], axis=0, keepdims=True)
    total = jnp.sum(lrun[...] * jnp.exp2((mrun[...] - peak) * EXP_SCALE), axis=0, keepdims=True)
    inv = jnp.where(total > 0.0, 1.0 / total, 0.0)
    inv = inv * jnp.concatenate([jnp.ones((1, QW), F32)] + [live] * GROUP, axis=1)
    for n in range(4 * NZ):
        mh[n] = jnp.exp2((mh[n] - peak) * EXP_SCALE) * inv
    own_f = jnp.exp2((mh[4 * NZ, :, QW:] - peak[:, QW:]) * EXP_SCALE) * inv[:, QW:]
    dqT[...] = jnp.zeros_like(dqT)

    def back(d, which):
        p = rpeer(d)
        dev = (c, p)
        e = nresp - d
        out = (
            lambda: remote(slots(dqrows, p), cols(dqr, r, QW), bs_.at[0, d], br_.at[0, e], dev),
            lambda: remote(slots(dkrows, p), cols(dkr, r, HD), bs_.at[1, d], br_.at[1, e], dev),
            lambda: remote(slots(dvrows, p), cols(dvr, r, HD), bs_.at[2, d], br_.at[2, e], dev),
        )
        return [out[n]() for n in which]

    def back_in(d):
        p = rpeer(d)
        dev = (c, p)
        return [
            remote(cols(dqr, p, QW), cols(dqr, p, QW), bs_.at[0, d], br_.at[0, d], dev),
            remote(cols(dkr, p, HD), cols(dkr, p, HD), bs_.at[1, d], br_.at[1, d], dev),
            remote(cols(dvr, p, HD), cols(dvr, p, HD), bs_.at[2, d], br_.at[2, d], dev),
        ]

    rkT = rk[...].T
    for h in range(GROUP):
        sl = slice(QW + h * BLK, QW + (h + 1) * BLK)
        hs = slice(h * BLK, (h + 1) * BLK)
        dp = dot(rv[...], doT[:, sl])
        p3 = own_pt[:, hs].astype(F32).reshape(BLK // 8, 8, BLK) * own_f[:, hs][None]
        p = p3.reshape(BLK, BLK)
        ds = (p * (dp - delta[:, sl])).astype(BF16)
        psc[0:BLK, sl] = p.astype(BF16)
        dssc[0:BLK, sl] = ds
        dqT[:, sl] += dot(rkT, ds)
    dvrows[...] = dot(psc[0:BLK, QW:], doa[QW:, :]).astype(BF16)
    dkrows[...] = (dot(dssc[0:BLK, QW:], qa[QW:, :]) * SCALE).astype(BF16)

    def send_back_kv(d, carry):
        for cp in back(d, (1, 2)):
            cp.start()
        return carry

    lax.fori_loop(1, nresp, send_back_kv, 0)
    local(16).start()
    local(17).start()

    def core_send(j):
        return remote(gpart.at[j, 1 - core], grecv.at[j], gcs.at[j], gcr.at[j], (cpart, r))

    def y_send(j):
        return remote(ysb.at[j], yrb.at[j], gys.at[j], gyr.at[j], (ypart, r))

    def z_send(j):
        d = zoff((j + 1) % NZ)
        return remote(zsb.at[j], zrb.at[NZ - d], gzs.at[d], gzr.at[NZ - d], (zpeer(d), r))

    def after_core(j):
        core_send(j).wait_recv()
        kept[j] = gpart[j, core, ylo] + grecv[j, ylo]
        ysb[j] = (gpart[j, core, 1 - ylo] + grecv[j, 1 - ylo]).astype(BF16)
        y_send(j).start()

    def after_y(j):
        y_send(j).wait_recv()
        zsb[j] = (kept[j] + yrb[j].astype(F32)).astype(BF16)
        z_send(j).start()

    def grads(j, carry):
        i = (j + 1) % NZ
        d = zoff(i)
        zc = lax.rem(z + d, NZ)

        @pl.when(j == 2)
        def _():
            for n in range(5, NZ):
                arrived(vsems, n)

        share_wait(vsems, d, 0)
        share_wait(vsems, d, 1)
        vc_rows = vv[pl.ds(zc * 4, 4)].reshape(CK, HD)
        kTc = kk[pl.ds(zc * 4, 4)].reshape(CK, HD).T
        prow = pl.ds(pl.multiple_of(i * CK, CK), CK)
        for t in range(2 * QW // QT):
            sl = slice(t * QT, (t + 1) * QT)
            dp = dot(vc_rows, doT[:, sl])
            f = mh[pl.ds(i * 4, 4), :, sl][:, None]
            p = (pt[prow, sl].astype(F32).reshape(4, BLK // 8, 8, QT) * f).reshape(CK, QT)
            ds = (p * (dp - delta[:, sl])).astype(BF16)
            psc[:, sl] = p.astype(BF16)
            dssc[:, sl] = ds
            dqT[:, sl] += dot(kTc, ds)
            if t == 1:
                @pl.when(j >= 1)
                def _():
                    after_core(j - 1)

                @pl.when(j >= 2)
                def _():
                    after_y(j - 2)

        dk = dot(dssc[...], qa[...])
        dv = dot(psc[...], doa[...])
        for b in range(4):
            gpart[j, b % 2, b // 2, 0] = dk[b * BLK:(b + 1) * BLK, :]
            gpart[j, b % 2, b // 2, 1] = dv[b * BLK:(b + 1) * BLK, :]
        core_send(j).start()
        return carry

    lax.fori_loop(0, NZ, grads, 0)

    for h in range(GROUP):
        dqrows[:, h * HD:(h + 1) * HD] = (dqT[:, QW + h * BLK:QW + (h + 1) * BLK].T * SCALE).astype(BF16)

    def send_back_q(d, carry):
        for cp in back(d, (0,)):
            cp.start()
        return carry

    lax.fori_loop(1, nresp, send_back_q, 0)
    local(15).start()

    after_y(NZ - 2)
    after_core(NZ - 1)
    for h in range(GROUP):
        dqloc[:, h * HD:(h + 1) * HD] = (dqT[:, h * BLK:(h + 1) * BLK].T * SCALE).astype(BF16)
    local(12).start()
    y_send(NZ - 1).wait_recv()
    kept[NZ - 1] = kept[NZ - 1] + yrb[NZ - 1].astype(F32)

    drain_gather(ksems)
    drain_gather(vsems)

    def drain_exchange(d, carry):
        for cp in exchange(d, range(5)):
            cp.wait_send()
        return carry

    lax.fori_loop(1, nresp, drain_exchange, 0)

    def drain_parts(j, carry):
        core_send(j).wait_send()
        y_send(j).wait_send()
        return carry

    lax.fori_loop(0, NZ, drain_parts, 0)

    def drain_zparts(j, carry):
        z_send(j).wait_send()
        return carry

    def z_parts(d, carry):
        remote(zrb.at[d], zrb.at[d], gzs.at[d], gzr.at[d], (zpeer(d), r)).wait_recv()
        kept[NZ - 1] = kept[NZ - 1] + zrb[d].astype(F32)
        return carry

    lax.fori_loop(1, NZ, z_parts, 0)
    dkvloc[0] = (kept[NZ - 1, 0] * SCALE).astype(BF16)
    dkvloc[1] = kept[NZ - 1, 1].astype(BF16)
    local(13).start()
    local(14).start()
    lax.fori_loop(0, NZ - 1, drain_zparts, 0)

    def finish_back(d, carry):
        for cp in back(d, range(3)):
            cp.wait_send()
        for cp in back_in(d):
            cp.wait_recv()
        return carry

    lax.fori_loop(1, nresp, finish_back, 0)
    for n in range(12, 18):
        local(n).wait()


def settle(*refs):
    n = len(refs) // 2
    for src, dst in zip(refs[:n], refs[n:]):
        dst[...] = src[...]


def solution(mesh):
    nresp = mesh.shape["resp"]
    nctx = mesh.shape["ctx"]

    def body(
        prompt_q, prompt_k, prompt_v, prompt_out, prompt_dout,
        resp_q, resp_k, resp_v, resp_out, resp_dout,
        lengths, resp_row, block_index,
    ):
        shape = jax.ShapeDtypeStruct
        smem = pl.BlockSpec(memory_space=pltpu.SMEM)
        vmem = pl.BlockSpec(memory_space=pltpu.VMEM)
        dma = pltpu.SemaphoreType.DMA
        anywhere = pl.BlockSpec(memory_space=pl.ANY)
        parts = pl.pallas_call(
            functools.partial(kernel, nresp),
            out_shape=(
                shape(prompt_q.shape, BF16),
                shape(prompt_k.shape, BF16),
                shape(prompt_v.shape, BF16),
                shape(resp_q.shape, BF16),
                shape(resp_k.shape, BF16),
                shape(resp_v.shape, BF16),
            ),
            in_specs=[smem] * 3 + [anywhere] * 10,
            out_specs=(anywhere,) * 6,
            scratch_shapes=[
                pltpu.VMEM((nctx, BLK, HD), BF16),
                pltpu.VMEM((nctx, BLK, HD), BF16),
                pltpu.VMEM((BLK, QW), BF16),
                pltpu.VMEM((BLK, QW), BF16),
                pltpu.VMEM((BLK, QW), BF16),
                pltpu.VMEM(resp_out.shape, BF16),
                pltpu.VMEM(resp_out.shape, BF16),
                pltpu.VMEM((BLK, QW), BF16),
                pltpu.VMEM((BLK, QW), BF16),
                pltpu.VMEM((BLK, HD), BF16),
                pltpu.VMEM((BLK, HD), BF16),
                pltpu.VMEM((BLK, 128), F32),
                pltpu.VMEM((nresp, 16, 128), F32),
                pltpu.VMEM((2 * QW, HD), BF16),
                pltpu.VMEM((2 * QW, HD), BF16),
                pltpu.VMEM((HD, 2 * QW), BF16),
                pltpu.VMEM((HD, 2 * QW), BF16),
                pltpu.VMEM((nctx * BLK, 2 * QW), BF16),
                pltpu.VMEM((BLK, QW), BF16),
                pltpu.VMEM((nctx + 1, 8, 2 * QW), F32),
                pltpu.VMEM((8, 2 * QW), F32),
                pltpu.VMEM((8, 2 * QW), F32),
                pltpu.VMEM((1, 2 * QW), F32),
                pltpu.VMEM((HD, 2 * QW), F32),
                pltpu.VMEM((CK, 2 * QW), BF16),
                pltpu.VMEM((CK, 2 * QW), BF16),
                pltpu.VMEM((CK, BLK), F32),
                pltpu.VMEM((NZ, 2, 2, 2, BLK, HD), F32),
                pltpu.VMEM((NZ, 2, 2, BLK, HD), F32),
                pltpu.VMEM((NZ, 2, BLK, HD), F32),
                pltpu.VMEM((NZ, 2, BLK, HD), BF16),
                pltpu.VMEM((NZ, 2, BLK, HD), BF16),
                pltpu.VMEM((NZ, 2, BLK, HD), BF16),
                pltpu.VMEM((NZ, 2, BLK, HD), BF16),
                pltpu.VMEM((BLK, QW), BF16),
                pltpu.VMEM((BLK, HD), BF16),
                pltpu.VMEM((BLK, HD), BF16),
                pltpu.VMEM((BLK, QW), BF16),
                pltpu.VMEM((2, BLK, HD), BF16),
                dma((NZ, 2)), dma((NZ, 2)), dma((1,)), dma((1,)), dma((NZ, 2)), dma((NZ, 2)),
                dma((NZ, 2)), dma((NZ, 2)), dma((1,)), dma((1,)), dma((NZ, 2)), dma((NZ, 2)),
                dma((5, nresp)), dma((5, nresp)),
                dma((NZ,)), dma((NZ,)), dma((NZ,)), dma((NZ,)), dma((NZ,)), dma((NZ,)),
                dma((3, nresp)), dma((3, nresp)),
                dma((18,)),
            ],
            compiler_params=pltpu.CompilerParams(
                collective_id=0, has_side_effects=True, vmem_limit_bytes=60 * 1024 * 1024
            ),
            name="attn_bwd",
        )(
            lengths, resp_row, block_index,
            prompt_q, prompt_k, prompt_v, prompt_out, prompt_dout,
            resp_q, resp_k, resp_v, resp_out, resp_dout,
        )
        return pl.pallas_call(
            settle,
            out_shape=tuple(shape(part.shape, part.dtype) for part in parts),
            in_specs=[vmem] * 6,
            out_specs=(vmem,) * 6,
            compiler_params=pltpu.CompilerParams(vmem_limit_bytes=60 * 1024 * 1024),
            name="settle",
        )(*parts)

    heads, rows, whole = P("ctx", "resp"), P(("ctx", "resp"), None), P()
    return jax.shard_map(
        body,
        mesh=mesh,
        in_specs=(heads,) * 5 + (rows,) * 5 + (whole,) * 3,
        out_specs=(heads,) * 3 + (rows,) * 3,
        check_vma=False,
    )
```

```python
import functools

import jax
import jax.numpy as jnp
from jax import lax
from jax.experimental import pallas as pl
from jax.experimental.pallas import tpu as pltpu
from jax.sharding import PartitionSpec as P

MESH = pl.DeviceIdType.MESH
F32, BF16 = jnp.float32, jnp.bfloat16
HD = 128
GROUP = 8
BLK = 128
NZ = 8
QW = GROUP * BLK
CK = 4 * BLK
QT = 512
SCALE = HD ** -0.5
EXP_SCALE = SCALE * 1.4426950408889634
LOW = -1e30
NEG = float("-inf")
DEAD = 1 << 20


def dot(a, b):
    return jnp.dot(a, b, preferred_element_type=F32)


def kernel(
    nresp,
    len_ref, row_ref, bi_ref,
    pq, pk, pv, pout, pdo, sq, sk, sv, sout, sdo,
    dqp, dkp, dvp, dqr, dkr, dvr,
    kk, vv, lq, lout, ldo, tout, tdo, rq, rdo, rk, rv, rdel, dbuf,
    qa, doa, qT, doT, pt, own_pt, mh, mrun, lrun, delta, dqT, psc, dssc, bias,
    gpart, grecv, kept, ysb, yrb, zsb, zrb, dqrows, dkrows, dvrows, dqloc, dkvloc,
    kzs, kzr, kys, kyr, kcs, kcr, vzs, vzr, vys, vyr, vcs, vcr,
    as_, ar_, gcs, gcr, gys, gyr, gzs, gzr, bs_, br_, loc,
):
    c = lax.axis_index("ctx")
    r = lax.axis_index("resp")
    z = c // 4
    lane4 = c % 4
    core = c % 2
    ylo = lane4 // 2
    cpart = c + 1 - 2 * core
    ystep = 2 - 4 * ylo
    ypart = c + ystep

    def zpeer(d):
        return lax.rem(z + d, NZ) * 4 + lane4

    def rpeer(d):
        return lax.rem(r + d, nresp)

    def remote(src, dst, ss, rs, dev):
        return pltpu.make_async_remote_copy(
            src_ref=src, dst_ref=dst, send_sem=ss, recv_sem=rs, device_id=dev, device_id_type=MESH
        )

    def zoff(i):
        return jnp.where(i % 2 == 1, (i + 1) // 2, (NZ - i // 2) % NZ)

    def cols(ref, p, w):
        return ref.at[:, pl.ds(pl.multiple_of(p * w, 128), w)]

    def slots(ref, p):
        return ref.at[pl.ds(pl.multiple_of(p * 16, 16), 16), :]

    pairs = (
        lambda: (pk, kk.at[c]),
        lambda: (pv, vv.at[c]),
        lambda: (pq, lq),
        lambda: (pdo, ldo),
        lambda: (sdo, tdo),
        lambda: (sout, tout),
        lambda: (pout, lout),
        lambda: (cols(sq, r, QW), slots(rq, r)),
        lambda: (cols(sdo, r, QW), slots(rdo, r)),
        lambda: (cols(sk, r, HD), slots(rk, r)),
        lambda: (cols(sv, r, HD), slots(rv, r)),
        lambda: (dbuf.at[r], slots(rdel, r)),
        lambda: (dqloc, dqp),
        lambda: (dkvloc.at[0], dkp),
        lambda: (dkvloc.at[1], dvp),
        lambda: (slots(dqrows, r), cols(dqr, r, QW)),
        lambda: (slots(dkrows, r), cols(dkr, r, HD)),
        lambda: (slots(dvrows, r), cols(dvr, r, HD)),
    )

    def local(n):
        src, dst = pairs[n]()
        return pltpu.make_async_copy(src, dst, loc.at[n])

    for n in range(11):
        local(n).start()

    barrier = pltpu.get_barrier_semaphore()

    def greet(dev):
        pl.semaphore_signal(barrier, inc=1, device_id=dev, device_id_type=MESH)

    def greet_z(d, carry):
        greet((zpeer(d), r))
        return carry

    def greet_r(d, carry):
        greet((c, rpeer(d)))
        return carry

    lax.fori_loop(1, NZ, greet_z, 0)
    greet((cpart, r))
    greet((ypart, r))
    lax.fori_loop(1, nresp, greet_r, 0)
    pl.semaphore_wait(barrier, (NZ - 1) + (nresp - 1) + 2)

    ksems = (kk, kzs, kzr, kys, kyr, kcs, kcr)
    vsems = (vv, vzs, vzr, vys, vyr, vcs, vcr)

    def swap(sems):
        ref, zs, zr, ys, yr, cs, cr = sems
        return remote(ref.at[c], ref.at[c], ys.at[0], yr.at[0], (ypart, r))

    def swap_wait(sems):
        ref, zs, zr, ys, yr, cs, cr = sems
        remote(ref.at[ypart], ref.at[ypart], ys.at[0], yr.at[0], (ypart, r)).wait_recv()

    def hop(sems, d, e, far):
        ref, zs, zr, ys, yr, cs, cr = sems
        b = zpeer(d) + far * ystep
        to = (zpeer(lax.rem(d - e + NZ, NZ)), r)
        return remote(ref.at[b], ref.at[b], zs.at[e, far], zr.at[e, far], to)

    def hop_wait(sems, d, far):
        ref, zs, zr, ys, yr, cs, cr = sems
        b = zpeer(d) + far * ystep
        remote(ref.at[b], ref.at[b], zs.at[d, far], zr.at[d, far], (zpeer(1), r)).wait_recv()

    def share(sems, d, far):
        ref, zs, zr, ys, yr, cs, cr = sems
        b = zpeer(d) + far * ystep
        return remote(ref.at[b], ref.at[b], cs.at[d, far], cr.at[d, far], (cpart, r))

    def share_wait(sems, d, far):
        ref, zs, zr, ys, yr, cs, cr = sems
        b = zpeer(d) + 1 - 2 * core + far * ystep
        remote(ref.at[b], ref.at[b], cs.at[d, far], cr.at[d, far], (cpart, r)).wait_recv()

    def begin(sems, far):
        for e in (1, NZ - 1, 2, NZ - 2):
            hop(sems, 0, e, far).start()
        share(sems, 0, far).start()

    def arrived(sems, i):
        d = zoff(i)
        for far in range(2):
            hop_wait(sems, d, far)
            share(sems, d, far).start()

    def relay(sems, d, e):
        for far in range(2):
            hop_wait(sems, d, far)
            hop(sems, d, e, far).start()
        hop(sems, d, NZ // 2, d // (NZ // 2)).start()
        for far in range(2):
            share(sems, d, far).start()

    def drain_gather(sems):
        def drain_hops(e, carry):
            for far in range(2):
                hop(sems, 0, e, far).wait_send()
            return carry

        def drain_shares(d, carry):
            for far in range(2):
                share(sems, d, far).wait_send()
            return carry

        lax.fori_loop(1, NZ, drain_hops, 0)
        lax.fori_loop(0, NZ, drain_shares, 0)
        swap(sems).wait_send()

    def sources(p):
        return (cols(sq, p, QW), cols(sdo, p, QW), cols(sk, p, HD), cols(sv, p, HD), dbuf.at[p])

    landings = (rq, rdo, rk, rv, rdel)

    def exchange(d, which):
        p = rpeer(d)
        src = sources(p)
        return [
            remote(src[n], slots(landings[n], r), as_.at[n, d], ar_.at[n, nresp - d], (c, p))
            for n in which
        ]

    def exchange_in(d):
        p = rpeer(d)
        return [
            remote(slots(landings[n], p), slots(landings[n], p), as_.at[n, d], ar_.at[n, d], (c, p))
            for n in range(5)
        ]

    def send_rows(n, carry):
        for cp in exchange(n, range(4)):
            cp.start()
        return carry

    local(0).wait()
    swap(ksems).start()
    begin(ksems, 0)
    local(1).wait()
    swap(vsems).start()
    lax.fori_loop(1, nresp, send_rows, 0)
    swap_wait(ksems)
    begin(ksems, 1)

    lane = lax.broadcasted_iota(jnp.int32, (128, 128), 1)
    subl = lax.broadcasted_iota(jnp.int32, (128, 128), 0)
    diff = lane - subl
    my = bi_ref[c]

    def load_queries(q, do, base):
        for h in range(GROUP):
            sl = slice(h * HD, (h + 1) * HD)
            out = slice(base + h * BLK, base + (h + 1) * BLK)
            qh, dh = q[:, sl], do[:, sl]
            qa[out, :] = qh
            doa[out, :] = dh
            qT[:, out] = qh.T
            doT[:, out] = dh.T

    def place_delta(rows, base):
        rows_t = rows.T
        for h in range(GROUP):
            delta[:, base + h * BLK: base + (h + 1) * BLK] = rows_t[h:h + 1, :]

    local(2).wait()
    local(3).wait()
    load_queries(lq, ldo, 0)
    mrun[...] = jnp.full((8, 2 * QW), LOW, F32)
    lrun[...] = jnp.zeros((8, 2 * QW), F32)

    local(4).wait()
    local(5).wait()
    lane16 = lax.broadcasted_iota(jnp.int32, (16, 128), 1)
    for g in range(nresp):
        acc = jnp.zeros((16, 128), F32)
        for h in range(GROUP):
            sl = slice((g * GROUP + h) * HD, (g * GROUP + h + 1) * HD)
            prod = tout[:, sl].astype(F32) * tdo[:, sl].astype(F32)
            acc = jnp.where(lane16 == h, jnp.sum(prod, axis=1, keepdims=True), acc)
        dbuf[g] = acc

    def send_delta(d, carry):
        exchange(d, (4,))[0].start()
        return carry

    lax.fori_loop(1, nresp, send_delta, 0)
    local(11).start()

    def merge(p3, m, mo, sl):
        mrun[:, sl] = m
        lrun[:, sl] = lrun[:, sl] * jnp.exp2((mo - m) * EXP_SCALE) + jnp.sum(p3, axis=0)

    def stats_chunk(i, base, masked):
        zc = lax.rem(z + zoff(i), NZ)
        if masked:
            for b in range(4):
                ahead = (bi_ref[zc * 4 + b] - my) * BLK
                bias[b * BLK:(b + 1) * BLK, :] = jnp.where(diff >= ahead, 0.0, NEG)
        for t in range(QW // QT):
            sl = slice(base + t * QT, base + (t + 1) * QT)
            for b in range(4):
                s = dot(kk[zc * 4 + b], qT[:, sl])
                if masked:
                    s = s + jnp.concatenate([bias[b * BLK:(b + 1) * BLK, :]] * (QT // BLK), axis=1)
                s3 = s.reshape(BLK // 8, 8, QT)
                mo = mrun[:, sl]
                m = jnp.maximum(mo, jnp.max(s3, axis=0))
                p3 = jnp.exp2((s3 - m[None]) * EXP_SCALE)
                prow = pl.ds(pl.multiple_of(i * CK + b * BLK, BLK), BLK)
                pt[prow, sl] = p3.reshape(BLK, QT).astype(BF16)
                mh[i * 4 + b, :, sl] = m
                merge(p3, m, mo, sl)

    def prompt_stats(i, carry):
        @pl.when(i == 1)
        def _():
            relay(ksems, 2, 3)
            relay(ksems, NZ - 2, NZ - 3)
            begin(vsems, 0)
            arrived(ksems, 1)
            arrived(ksems, 2)

        @pl.when(i == 3)
        def _():
            swap_wait(vsems)
            begin(vsems, 1)

        d = zoff(i)
        share_wait(ksems, d, 0)
        share_wait(ksems, d, 1)
        stats_chunk(i, 0, True)
        return carry

    lax.fori_loop(0, 5, prompt_stats, 0)

    local(6).wait()
    acc = jnp.zeros((BLK, 128), F32)
    for h in range(GROUP):
        sl = slice(h * HD, (h + 1) * HD)
        prod = lout[:, sl].astype(F32) * ldo[:, sl].astype(F32)
        acc = jnp.where(lane == h, jnp.sum(prod, axis=1, keepdims=True), acc)
    place_delta(acc, 0)

    def wait_in(d, carry):
        for cp in exchange_in(d):
            cp.wait_recv()
        return carry

    lax.fori_loop(1, nresp, wait_in, 0)
    for n in range(7, 12):
        local(n).wait()
    load_queries(rq, rdo, QW)
    place_delta(rdel[...], QW)

    lane1 = lax.broadcasted_iota(jnp.int32, (1, 128), 1)
    startq = jnp.full((1, 128), DEAD, jnp.int32)
    cum = jnp.int32(0)
    for n in range(len_ref.shape[0]):
        count = jnp.where(row_ref[n] == c, len_ref[n], 0)
        startq = jnp.where((lane1 >= cum) & (lane1 < cum + count), cum, startq)
        cum = cum + count
    live = jnp.where(startq < DEAD, 1.0, 0.0)
    own_mask = (subl >= startq) & (diff >= 0)
    for h in range(GROUP):
        sl = slice(QW + h * BLK, QW + (h + 1) * BLK)
        s3 = jnp.where(own_mask, dot(rk[...], qT[:, sl]), NEG).reshape(BLK // 8, 8, BLK)
        mo = mrun[:, sl]
        m = jnp.maximum(mo, jnp.max(s3, axis=0))
        p3 = jnp.exp2((s3 - m[None]) * EXP_SCALE)
        own_pt[:, h * BLK:(h + 1) * BLK] = p3.reshape(BLK, BLK).astype(BF16)
        mh[4 * NZ, :, sl] = m
        merge(p3, m, mo, sl)

    def resp_stats(i, carry):
        stats_chunk(i, QW, False)
        return carry

    lax.fori_loop(0, 5, resp_stats, 0)
    for n in range(5, NZ):
        arrived(ksems, n)

    def late_stats(i, carry):
        @pl.when(i == NZ - 1)
        def _():
            relay(vsems, 2, 3)
            relay(vsems, NZ - 2, NZ - 3)
            arrived(vsems, 1)
            arrived(vsems, 2)

        d = zoff(i)
        share_wait(ksems, d, 0)
        share_wait(ksems, d, 1)
        stats_chunk(i, 0, True)
        stats_chunk(i, QW, False)
        return carry

    lax.fori_loop(5, NZ, late_stats, 0)

    peak = jnp.max(mrun[...], axis=0, keepdims=True)
    total = jnp.sum(lrun[...] * jnp.exp2((mrun[...] - peak) * EXP_SCALE), axis=0, keepdims=True)
    inv = jnp.where(total > 0.0, 1.0 / total, 0.0)
    inv = inv * jnp.concatenate([jnp.ones((1, QW), F32)] + [live] * GROUP, axis=1)
    for n in range(4 * NZ):
        mh[n] = jnp.exp2((mh[n] - peak) * EXP_SCALE) * inv
    own_f = jnp.exp2((mh[4 * NZ, :, QW:] - peak[:, QW:]) * EXP_SCALE) * inv[:, QW:]
    dqT[...] = jnp.zeros_like(dqT)

    def back(d, which):
        p = rpeer(d)
        dev = (c, p)
        e = nresp - d
        out = (
            lambda: remote(slots(dqrows, p), cols(dqr, r, QW), bs_.at[0, d], br_.at[0, e], dev),
            lambda: remote(slots(dkrows, p), cols(dkr, r, HD), bs_.at[1, d], br_.at[1, e], dev),
            lambda: remote(slots(dvrows, p), cols(dvr, r, HD), bs_.at[2, d], br_.at[2, e], dev),
        )
        return [out[n]() for n in which]

    def back_in(d):
        p = rpeer(d)
        dev = (c, p)
        return [
            remote(cols(dqr, p, QW), cols(dqr, p, QW), bs_.at[0, d], br_.at[0, d], dev),
            remote(cols(dkr, p, HD), cols(dkr, p, HD), bs_.at[1, d], br_.at[1, d], dev),
            remote(cols(dvr, p, HD), cols(dvr, p, HD), bs_.at[2, d], br_.at[2, d], dev),
        ]

    rkT = rk[...].T
    for h in range(GROUP):
        sl = slice(QW + h * BLK, QW + (h + 1) * BLK)
        hs = slice(h * BLK, (h + 1) * BLK)
        dp = dot(rv[...], doT[:, sl])
        p3 = own_pt[:, hs].astype(F32).reshape(BLK // 8, 8, BLK) * own_f[:, hs][None]
        p = p3.reshape(BLK, BLK)
        ds = (p * (dp - delta[:, sl])).astype(BF16)
        psc[0:BLK, sl] = p.astype(BF16)
        dssc[0:BLK, sl] = ds
        dqT[:, sl] += dot(rkT, ds)
    dvrows[...] = dot(psc[0:BLK, QW:], doa[QW:, :]).astype(BF16)
    dkrows[...] = (dot(dssc[0:BLK, QW:], qa[QW:, :]) * SCALE).astype(BF16)

    def send_back_kv(d, carry):
        for cp in back(d, (1, 2)):
            cp.start()
        return carry

    lax.fori_loop(1, nresp, send_back_kv, 0)
    local(16).start()
    local(17).start()

    def core_send(j):
        return remote(gpart.at[j, 1 - core], grecv.at[j], gcs.at[j], gcr.at[j], (cpart, r))

    def y_send(j):
        return remote(ysb.at[j], yrb.at[j], gys.at[j], gyr.at[j], (ypart, r))

    def z_send(j):
        d = zoff((j + 1) % NZ)
        return remote(zsb.at[j], zrb.at[NZ - d], gzs.at[d], gzr.at[NZ - d], (zpeer(d), r))

    def after_core(j):
        core_send(j).wait_recv()
        kept[j] = gpart[j, core, ylo] + grecv[j, ylo]
        ysb[j] = (gpart[j, core, 1 - ylo] + grecv[j, 1 - ylo]).astype(BF16)
        y_send(j).start()

    def after_y(j):
        y_send(j).wait_recv()
        zsb[j] = (kept[j] + yrb[j].astype(F32)).astype(BF16)
        z_send(j).start()

    def grads(j, carry):
        i = (j + 1) % NZ
        d = zoff(i)
        zc = lax.rem(z + d, NZ)

        @pl.when(j == 2)
        def _():
            for n in range(5, NZ):
                arrived(vsems, n)

        share_wait(vsems, d, 0)
        share_wait(vsems, d, 1)
        vc_rows = vv[pl.ds(zc * 4, 4)].reshape(CK, HD)
        kTc = kk[pl.ds(zc * 4, 4)].reshape(CK, HD).T
        prow = pl.ds(pl.multiple_of(i * CK, CK), CK)
        for t in range(2 * QW // QT):
            sl = slice(t * QT, (t + 1) * QT)
            dp = dot(vc_rows, doT[:, sl])
            f = mh[pl.ds(i * 4, 4), :, sl][:, None]
            p = (pt[prow, sl].astype(F32).reshape(4, BLK // 8, 8, QT) * f).reshape(CK, QT)
            ds = (p * (dp - delta[:, sl])).astype(BF16)
            psc[:, sl] = p.astype(BF16)
            dssc[:, sl] = ds
            dqT[:, sl] += dot(kTc, ds)
        dk = dot(dssc[...], qa[...])
        dv = dot(psc[...], doa[...])
        for b in range(4):
            gpart[j, b % 2, b // 2, 0] = dk[b * BLK:(b + 1) * BLK, :]
            gpart[j, b % 2, b // 2, 1] = dv[b * BLK:(b + 1) * BLK, :]
        core_send(j).start()

        @pl.when(j >= 1)
        def _():
            after_core(j - 1)

        @pl.when(j >= 2)
        def _():
            after_y(j - 2)

        return carry

    lax.fori_loop(0, NZ, grads, 0)

    for h in range(GROUP):
        dqrows[:, h * HD:(h + 1) * HD] = (dqT[:, QW + h * BLK:QW + (h + 1) * BLK].T * SCALE).astype(BF16)

    def send_back_q(d, carry):
        for cp in back(d, (0,)):
            cp.start()
        return carry

    lax.fori_loop(1, nresp, send_back_q, 0)
    local(15).start()

    after_core(NZ - 1)
    after_y(NZ - 2)
    for h in range(GROUP):
        dqloc[:, h * HD:(h + 1) * HD] = (dqT[:, h * BLK:(h + 1) * BLK].T * SCALE).astype(BF16)
    local(12).start()
    y_send(NZ - 1).wait_recv()
    kept[NZ - 1] = kept[NZ - 1] + yrb[NZ - 1].astype(F32)

    drain_gather(ksems)
    drain_gather(vsems)

    def drain_exchange(d, carry):
        for cp in exchange(d, range(5)):
            cp.wait_send()
        return carry

    lax.fori_loop(1, nresp, drain_exchange, 0)

    def drain_parts(j, carry):
        core_send(j).wait_send()
        y_send(j).wait_send()
        return carry

    lax.fori_loop(0, NZ, drain_parts, 0)

    def drain_zparts(j, carry):
        z_send(j).wait_send()
        return carry

    def z_parts(d, carry):
        remote(zrb.at[d], zrb.at[d], gzs.at[d], gzr.at[d], (zpeer(d), r)).wait_recv()
        kept[NZ - 1] = kept[NZ - 1] + zrb[d].astype(F32)
        return carry

    lax.fori_loop(1, NZ, z_parts, 0)
    dkvloc[0] = (kept[NZ - 1, 0] * SCALE).astype(BF16)
    dkvloc[1] = kept[NZ - 1, 1].astype(BF16)
    local(13).start()
    local(14).start()
    lax.fori_loop(0, NZ - 1, drain_zparts, 0)

    def finish_back(d, carry):
        for cp in back(d, range(3)):
            cp.wait_send()
        for cp in back_in(d):
            cp.wait_recv()
        return carry

    lax.fori_loop(1, nresp, finish_back, 0)
    for n in range(12, 18):
        local(n).wait()


def settle(*refs):
    n = len(refs) // 2
    for src, dst in zip(refs[:n], refs[n:]):
        dst[...] = src[...]


def solution(mesh):
    nresp = mesh.shape["resp"]
    nctx = mesh.shape["ctx"]

    def body(
        prompt_q, prompt_k, prompt_v, prompt_out, prompt_dout,
        resp_q, resp_k, resp_v, resp_out, resp_dout,
        lengths, resp_row, block_index,
    ):
        shape = jax.ShapeDtypeStruct
        smem = pl.BlockSpec(memory_space=pltpu.SMEM)
        vmem = pl.BlockSpec(memory_space=pltpu.VMEM)
        dma = pltpu.SemaphoreType.DMA
        anywhere = pl.BlockSpec(memory_space=pl.ANY)
        parts = pl.pallas_call(
            functools.partial(kernel, nresp),
            out_shape=(
                shape(prompt_q.shape, BF16),
                shape(prompt_k.shape, BF16),
                shape(prompt_v.shape, BF16),
                shape(resp_q.shape, BF16),
                shape(resp_k.shape, BF16),
                shape(resp_v.shape, BF16),
            ),
            in_specs=[smem] * 3 + [anywhere] * 10,
            out_specs=(anywhere,) * 6,
            scratch_shapes=[
                pltpu.VMEM((nctx, BLK, HD), BF16),
                pltpu.VMEM((nctx, BLK, HD), BF16),
                pltpu.VMEM((BLK, QW), BF16),
                pltpu.VMEM((BLK, QW), BF16),
                pltpu.VMEM((BLK, QW), BF16),
                pltpu.VMEM(resp_out.shape, BF16),
                pltpu.VMEM(resp_out.shape, BF16),
                pltpu.VMEM((BLK, QW), BF16),
                pltpu.VMEM((BLK, QW), BF16),
                pltpu.VMEM((BLK, HD), BF16),
                pltpu.VMEM((BLK, HD), BF16),
                pltpu.VMEM((BLK, 128), F32),
                pltpu.VMEM((nresp, 16, 128), F32),
                pltpu.VMEM((2 * QW, HD), BF16),
                pltpu.VMEM((2 * QW, HD), BF16),
                pltpu.VMEM((HD, 2 * QW), BF16),
                pltpu.VMEM((HD, 2 * QW), BF16),
                pltpu.VMEM((nctx * BLK, 2 * QW), BF16),
                pltpu.VMEM((BLK, QW), BF16),
                pltpu.VMEM((nctx + 1, 8, 2 * QW), F32),
                pltpu.VMEM((8, 2 * QW), F32),
                pltpu.VMEM((8, 2 * QW), F32),
                pltpu.VMEM((1, 2 * QW), F32),
                pltpu.VMEM((HD, 2 * QW), F32),
                pltpu.VMEM((CK, 2 * QW), BF16),
                pltpu.VMEM((CK, 2 * QW), BF16),
                pltpu.VMEM((CK, BLK), F32),
                pltpu.VMEM((NZ, 2, 2, 2, BLK, HD), F32),
                pltpu.VMEM((NZ, 2, 2, BLK, HD), F32),
                pltpu.VMEM((NZ, 2, BLK, HD), F32),
                pltpu.VMEM((NZ, 2, BLK, HD), BF16),
                pltpu.VMEM((NZ, 2, BLK, HD), BF16),
                pltpu.VMEM((NZ, 2, BLK, HD), BF16),
                pltpu.VMEM((NZ, 2, BLK, HD), BF16),
                pltpu.VMEM((BLK, QW), BF16),
                pltpu.VMEM((BLK, HD), BF16),
                pltpu.VMEM((BLK, HD), BF16),
                pltpu.VMEM((BLK, QW), BF16),
                pltpu.VMEM((2, BLK, HD), BF16),
                dma((NZ, 2)), dma((NZ, 2)), dma((1,)), dma((1,)), dma((NZ, 2)), dma((NZ, 2)),
                dma((NZ, 2)), dma((NZ, 2)), dma((1,)), dma((1,)), dma((NZ, 2)), dma((NZ, 2)),
                dma((5, nresp)), dma((5, nresp)),
                dma((NZ,)), dma((NZ,)), dma((NZ,)), dma((NZ,)), dma((NZ,)), dma((NZ,)),
                dma((3, nresp)), dma((3, nresp)),
                dma((18,)),
            ],
            compiler_params=pltpu.CompilerParams(
                collective_id=0, has_side_effects=True, vmem_limit_bytes=60 * 1024 * 1024
            ),
            name="attn_bwd",
        )(
            lengths, resp_row, block_index,
            prompt_q, prompt_k, prompt_v, prompt_out, prompt_dout,
            resp_q, resp_k, resp_v, resp_out, resp_dout,
        )
        return pl.pallas_call(
            settle,
            out_shape=tuple(shape(part.shape, part.dtype) for part in parts),
            in_specs=[vmem] * 6,
            out_specs=(vmem,) * 6,
            compiler_params=pltpu.CompilerParams(vmem_limit_bytes=60 * 1024 * 1024),
            name="settle",
        )(*parts)

    heads, rows, whole = P("ctx", "resp"), P(("ctx", "resp"), None), P()
    return jax.shard_map(
        body,
        mesh=mesh,
        in_specs=(heads,) * 5 + (rows,) * 5 + (whole,) * 3,
        out_specs=(heads,) * 3 + (rows,) * 3,
        check_vma=False,
    )
```

```python
import functools

import jax
import jax.numpy as jnp
from jax import lax
from jax.experimental import pallas as pl
from jax.experimental.pallas import tpu as pltpu
from jax.sharding import PartitionSpec as P

MESH = pl.DeviceIdType.MESH
F32, BF16 = jnp.float32, jnp.bfloat16
HD = 128
GROUP = 8
BLK = 128
NZ = 8
QW = GROUP * BLK
CK = 4 * BLK
QT = 512
SCALE = HD ** -0.5
EXP_SCALE = SCALE * 1.4426950408889634
LOW = -1e30
NEG = float("-inf")
DEAD = 1 << 20


def dot(a, b):
    return jnp.dot(a, b, preferred_element_type=F32)


def kernel(
    nresp,
    len_ref, row_ref, bi_ref,
    pq, pk, pv, pout, pdo, sq, sk, sv, sout, sdo,
    dqp, dkp, dvp, dqr, dkr, dvr,
    kk, vv, lq, lout, ldo, tout, tdo, rq, rdo, rk, rv, rdel, dbuf,
    qa, doa, qT, doT, pt, own_pt, mh, mrun, lrun, delta, dqT, psc, dssc, bias,
    gpart, grecv, kept, ysb, yrb, zsb, zrb, dqrows, dkrows, dvrows, dqloc, dkvloc,
    kx, kzr, kcr, vx, vzr, vcr, as_, ar_, gs, gcr, gyr, gzr, bs_, br_, loc,
):
    c = lax.axis_index("ctx")
    r = lax.axis_index("resp")
    z = c // 4
    lane4 = c % 4
    core = c % 2
    ylo = lane4 // 2
    cpart = c + 1 - 2 * core
    ystep = 2 - 4 * ylo
    ypart = c + ystep

    def zpeer(d):
        return lax.rem(z + d, NZ) * 4 + lane4

    def rpeer(d):
        return lax.rem(r + d, nresp)

    def remote(src, dst, ss, rs, dev):
        return pltpu.make_async_remote_copy(
            src_ref=src, dst_ref=dst, send_sem=ss, recv_sem=rs, device_id=dev, device_id_type=MESH
        )

    def got(part, sem):
        remote(part, part, sem, sem, (cpart, r)).wait_recv()

    def sent(part, sem):
        remote(part, part, sem, sem, (cpart, r)).wait_send()

    def zoff(i):
        return jnp.where(i % 2 == 1, (i + 1) // 2, (NZ - i // 2) % NZ)

    def cols(ref, p, w):
        return ref.at[:, pl.ds(pl.multiple_of(p * w, 128), w)]

    def slots(ref, p):
        return ref.at[pl.ds(pl.multiple_of(p * 16, 16), 16), :]

    pairs = (
        lambda: (pk, kk.at[c]),
        lambda: (pv, vv.at[c]),
        lambda: (pq, lq),
        lambda: (pdo, ldo),
        lambda: (sdo, tdo),
        lambda: (sout, tout),
        lambda: (pout, lout),
        lambda: (cols(sq, r, QW), slots(rq, r)),
        lambda: (cols(sdo, r, QW), slots(rdo, r)),
        lambda: (cols(sk, r, HD), slots(rk, r)),
        lambda: (cols(sv, r, HD), slots(rv, r)),
        lambda: (dbuf.at[r], slots(rdel, r)),
        lambda: (dqloc, dqp),
        lambda: (dkvloc.at[0], dkp),
        lambda: (dkvloc.at[1], dvp),
        lambda: (slots(dqrows, r), cols(dqr, r, QW)),
        lambda: (slots(dkrows, r), cols(dkr, r, HD)),
        lambda: (slots(dvrows, r), cols(dvr, r, HD)),
    )

    def local(n):
        src, dst = pairs[n]()
        return pltpu.make_async_copy(src, dst, loc.at[n])

    for n in range(11):
        local(n).start()

    barrier = pltpu.get_barrier_semaphore()

    def greet(dev):
        pl.semaphore_signal(barrier, inc=1, device_id=dev, device_id_type=MESH)

    def greet_z(d, carry):
        greet((zpeer(d), r))
        return carry

    def greet_r(d, carry):
        greet((c, rpeer(d)))
        return carry

    lax.fori_loop(1, NZ, greet_z, 0)
    greet((cpart, r))
    greet((ypart, r))
    lax.fori_loop(1, nresp, greet_r, 0)
    pl.semaphore_wait(barrier, (NZ - 1) + (nresp - 1) + 2)

    ksems = (kk, kx, kzr, kcr)
    vsems = (vv, vx, vzr, vcr)

    def swap(sems):
        ref, x, zr, cr = sems
        return remote(ref.at[c], ref.at[c], x.at[0], x.at[1], (ypart, r))

    def swap_wait(sems):
        ref, x, zr, cr = sems
        got(ref.at[ypart], x.at[1])

    def hop(sems, d, e, far):
        ref, x, zr, cr = sems
        b = zpeer(d) + far * ystep
        to = (zpeer(lax.rem(d - e + NZ, NZ)), r)
        return remote(ref.at[b], ref.at[b], x.at[0], zr.at[e, far], to)

    def hop_wait(sems, d, far):
        ref, x, zr, cr = sems
        got(ref.at[zpeer(d) + far * ystep], zr.at[d, far])

    def share(sems, d, far):
        ref, x, zr, cr = sems
        b = zpeer(d) + far * ystep
        return remote(ref.at[b], ref.at[b], x.at[0], cr.at[d], (cpart, r))

    def share_wait(sems, d):
        ref, x, zr, cr = sems
        got(ref.at[pl.ds(lax.rem(z + d, NZ) * 4, 2)], cr.at[d])

    def begin(sems, far):
        for e in (1, NZ - 1, 2, NZ - 2):
            hop(sems, 0, e, far).start()
        share(sems, 0, far).start()

    def arrived(sems, i):
        d = zoff(i)
        for far in range(2):
            hop_wait(sems, d, far)
            share(sems, d, far).start()

    def relay(sems, d, e):
        for far in range(2):
            hop_wait(sems, d, far)
            hop(sems, d, e, far).start()
        hop(sems, d, NZ // 2, d // (NZ // 2)).start()
        for far in range(2):
            share(sems, d, far).start()

    def drain_gather(sems):
        ref, x, zr, cr = sems
        sent(ref.at[pl.ds(0, 4 * NZ - 1)], x.at[0])

    def sources(p):
        return (cols(sq, p, QW), cols(sdo, p, QW), cols(sk, p, HD), cols(sv, p, HD), dbuf.at[p])

    landings = (rq, rdo, rk, rv, rdel)

    def exchange(d, which):
        p = rpeer(d)
        src = sources(p)
        return [
            remote(src[n], slots(landings[n], r), as_.at[n], ar_.at[n], (c, p))
            for n in which
        ]

    def send_rows(n, carry):
        for cp in exchange(n, range(4)):
            cp.start()
        return carry

    local(0).wait()
    swap(ksems).start()
    begin(ksems, 0)
    local(1).wait()
    swap(vsems).start()
    lax.fori_loop(1, nresp, send_rows, 0)
    swap_wait(ksems)
    begin(ksems, 1)

    lane = lax.broadcasted_iota(jnp.int32, (128, 128), 1)
    subl = lax.broadcasted_iota(jnp.int32, (128, 128), 0)
    diff = lane - subl
    my = bi_ref[c]

    def load_queries(q, do, base):
        for h in range(GROUP):
            sl = slice(h * HD, (h + 1) * HD)
            out = slice(base + h * BLK, base + (h + 1) * BLK)
            qh, dh = q[:, sl], do[:, sl]
            qa[out, :] = qh
            doa[out, :] = dh
            qT[:, out] = qh.T
            doT[:, out] = dh.T

    def place_delta(rows, base):
        rows_t = rows.T
        for h in range(GROUP):
            delta[:, base + h * BLK: base + (h + 1) * BLK] = rows_t[h:h + 1, :]

    local(2).wait()
    local(3).wait()
    load_queries(lq, ldo, 0)
    mrun[...] = jnp.full((8, 2 * QW), LOW, F32)
    lrun[...] = jnp.zeros((8, 2 * QW), F32)

    local(4).wait()
    local(5).wait()
    lane16 = lax.broadcasted_iota(jnp.int32, (16, 128), 1)
    for g in range(nresp):
        acc = jnp.zeros((16, 128), F32)
        for h in range(GROUP):
            sl = slice((g * GROUP + h) * HD, (g * GROUP + h + 1) * HD)
            prod = tout[:, sl].astype(F32) * tdo[:, sl].astype(F32)
            acc = jnp.where(lane16 == h, jnp.sum(prod, axis=1, keepdims=True), acc)
        dbuf[g] = acc

    def send_delta(d, carry):
        exchange(d, (4,))[0].start()
        return carry

    lax.fori_loop(1, nresp, send_delta, 0)
    local(11).start()

    def merge(p3, m, mo, sl):
        mrun[:, sl] = m
        lrun[:, sl] = lrun[:, sl] * jnp.exp2((mo - m) * EXP_SCALE) + jnp.sum(p3, axis=0)

    def stats_chunk(i, base, masked):
        zc = lax.rem(z + zoff(i), NZ)
        if masked:
            for b in range(4):
                ahead = (bi_ref[zc * 4 + b] - my) * BLK
                bias[b * BLK:(b + 1) * BLK, :] = jnp.where(diff >= ahead, 0.0, NEG)
        for t in range(QW // QT):
            sl = slice(base + t * QT, base + (t + 1) * QT)
            for b in range(4):
                s = dot(kk[zc * 4 + b], qT[:, sl])
                if masked:
                    s = s + jnp.concatenate([bias[b * BLK:(b + 1) * BLK, :]] * (QT // BLK), axis=1)
                s3 = s.reshape(BLK // 8, 8, QT)
                mo = mrun[:, sl]
                m = jnp.maximum(mo, jnp.max(s3, axis=0))
                p3 = jnp.exp2((s3 - m[None]) * EXP_SCALE)
                prow = pl.ds(pl.multiple_of(i * CK + b * BLK, BLK), BLK)
                pt[prow, sl] = p3.reshape(BLK, QT).astype(BF16)
                mh[i * 4 + b, :, sl] = m
                merge(p3, m, mo, sl)

    def prompt_stats(i, carry):
        @pl.when(i == 1)
        def _():
            relay(ksems, 2, 3)
            relay(ksems, NZ - 2, NZ - 3)
            begin(vsems, 0)
            arrived(ksems, 1)
            arrived(ksems, 2)

        @pl.when(i == 3)
        def _():
            swap_wait(vsems)
            begin(vsems, 1)

        d = zoff(i)
        share_wait(ksems, d)
        stats_chunk(i, 0, True)
        return carry

    lax.fori_loop(0, 5, prompt_stats, 0)

    local(6).wait()
    acc = jnp.zeros((BLK, 128), F32)
    for h in range(GROUP):
        sl = slice(h * HD, (h + 1) * HD)
        prod = lout[:, sl].astype(F32) * ldo[:, sl].astype(F32)
        acc = jnp.where(lane == h, jnp.sum(prod, axis=1, keepdims=True), acc)
    place_delta(acc, 0)

    others = 16 * (nresp - 1)
    for n in range(5):
        got(landings[n].at[pl.ds(0, others), :], ar_.at[n])
    for n in range(7, 12):
        local(n).wait()
    load_queries(rq, rdo, QW)
    place_delta(rdel[...], QW)

    lane1 = lax.broadcasted_iota(jnp.int32, (1, 128), 1)
    startq = jnp.full((1, 128), DEAD, jnp.int32)
    cum = jnp.int32(0)
    for n in range(len_ref.shape[0]):
        count = jnp.where(row_ref[n] == c, len_ref[n], 0)
        startq = jnp.where((lane1 >= cum) & (lane1 < cum + count), cum, startq)
        cum = cum + count
    live = jnp.where(startq < DEAD, 1.0, 0.0)
    own_mask = (subl >= startq) & (diff >= 0)
    for h in range(GROUP):
        sl = slice(QW + h * BLK, QW + (h + 1) * BLK)
        s3 = jnp.where(own_mask, dot(rk[...], qT[:, sl]), NEG).reshape(BLK // 8, 8, BLK)
        mo = mrun[:, sl]
        m = jnp.maximum(mo, jnp.max(s3, axis=0))
        p3 = jnp.exp2((s3 - m[None]) * EXP_SCALE)
        own_pt[:, h * BLK:(h + 1) * BLK] = p3.reshape(BLK, BLK).astype(BF16)
        mh[4 * NZ, :, sl] = m
        merge(p3, m, mo, sl)

    def resp_stats(i, carry):
        stats_chunk(i, QW, False)
        return carry

    lax.fori_loop(0, 5, resp_stats, 0)
    for n in range(5, NZ):
        arrived(ksems, n)

    def late_stats(i, carry):
        @pl.when(i == NZ - 1)
        def _():
            relay(vsems, 2, 3)
            relay(vsems, NZ - 2, NZ - 3)
            arrived(vsems, 1)
            arrived(vsems, 2)

        d = zoff(i)
        share_wait(ksems, d)
        stats_chunk(i, 0, True)
        stats_chunk(i, QW, False)
        return carry

    lax.fori_loop(5, NZ, late_stats, 0)

    peak = jnp.max(mrun[...], axis=0, keepdims=True)
    total = jnp.sum(lrun[...] * jnp.exp2((mrun[...] - peak) * EXP_SCALE), axis=0, keepdims=True)
    inv = jnp.where(total > 0.0, 1.0 / total, 0.0)
    inv = inv * jnp.concatenate([jnp.ones((1, QW), F32)] + [live] * GROUP, axis=1)
    for n in range(4 * NZ):
        mh[n] = jnp.exp2((mh[n] - peak) * EXP_SCALE) * inv
    own_f = jnp.exp2((mh[4 * NZ, :, QW:] - peak[:, QW:]) * EXP_SCALE) * inv[:, QW:]
    dqT[...] = jnp.zeros_like(dqT)

    def back(d, which):
        p = rpeer(d)
        dev = (c, p)
        out = (
            lambda: remote(slots(dqrows, p), cols(dqr, r, QW), bs_.at[0], br_.at[0], dev),
            lambda: remote(slots(dkrows, p), cols(dkr, r, HD), bs_.at[1], br_.at[1], dev),
            lambda: remote(slots(dvrows, p), cols(dvr, r, HD), bs_.at[2], br_.at[2], dev),
        )
        return [out[n]() for n in which]

    rkT = rk[...].T
    for h in range(GROUP):
        sl = slice(QW + h * BLK, QW + (h + 1) * BLK)
        hs = slice(h * BLK, (h + 1) * BLK)
        dp = dot(rv[...], doT[:, sl])
        p3 = own_pt[:, hs].astype(F32).reshape(BLK // 8, 8, BLK) * own_f[:, hs][None]
        p = p3.reshape(BLK, BLK)
        ds = (p * (dp - delta[:, sl])).astype(BF16)
        psc[0:BLK, sl] = p.astype(BF16)
        dssc[0:BLK, sl] = ds
        dqT[:, sl] += dot(rkT, ds)
    dvrows[...] = dot(psc[0:BLK, QW:], doa[QW:, :]).astype(BF16)
    dkrows[...] = (dot(dssc[0:BLK, QW:], qa[QW:, :]) * SCALE).astype(BF16)

    def send_back_kv(d, carry):
        for cp in back(d, (1, 2)):
            cp.start()
        return carry

    lax.fori_loop(1, nresp, send_back_kv, 0)
    local(16).start()
    local(17).start()

    def core_send(j):
        return remote(gpart.at[j, 1 - core], grecv.at[j], gs.at[0], gcr.at[j], (cpart, r))

    def y_send(j):
        return remote(ysb.at[j], yrb.at[j], gs.at[1], gyr.at[j], (ypart, r))

    def z_send(j):
        d = zoff((j + 1) % NZ)
        return remote(zsb.at[j], zrb.at[NZ - d], gs.at[2], gzr.at[0], (zpeer(d), r))

    def after_core(j):
        core_send(j).wait_recv()
        kept[j] = gpart[j, core, ylo] + grecv[j, ylo]
        ysb[j] = (gpart[j, core, 1 - ylo] + grecv[j, 1 - ylo]).astype(BF16)
        y_send(j).start()

    def after_y(j):
        y_send(j).wait_recv()
        zsb[j] = (kept[j] + yrb[j].astype(F32)).astype(BF16)
        z_send(j).start()

    def grads(j, carry):
        i = (j + 1) % NZ
        d = zoff(i)
        zc = lax.rem(z + d, NZ)

        @pl.when(j == 2)
        def _():
            for n in range(5, NZ):
                arrived(vsems, n)

        share_wait(vsems, d)
        vc_rows = vv[pl.ds(zc * 4, 4)].reshape(CK, HD)
        kTc = kk[pl.ds(zc * 4, 4)].reshape(CK, HD).T
        prow = pl.ds(pl.multiple_of(i * CK, CK), CK)
        for t in range(2 * QW // QT):
            sl = slice(t * QT, (t + 1) * QT)
            dp = dot(vc_rows, doT[:, sl])
            f = mh[pl.ds(i * 4, 4), :, sl][:, None]
            p = (pt[prow, sl].astype(F32).reshape(4, BLK // 8, 8, QT) * f).reshape(CK, QT)
            ds = (p * (dp - delta[:, sl])).astype(BF16)
            psc[:, sl] = p.astype(BF16)
            dssc[:, sl] = ds
            dqT[:, sl] += dot(kTc, ds)
        dk = dot(dssc[...], qa[...])
        dv = dot(psc[...], doa[...])
        for b in range(4):
            gpart[j, b % 2, b // 2, 0] = dk[b * BLK:(b + 1) * BLK, :]
            gpart[j, b % 2, b // 2, 1] = dv[b * BLK:(b + 1) * BLK, :]
        core_send(j).start()

        @pl.when(j >= 1)
        def _():
            after_core(j - 1)

        @pl.when(j >= 2)
        def _():
            after_y(j - 2)

        return carry

    lax.fori_loop(0, NZ, grads, 0)

    for h in range(GROUP):
        dqrows[:, h * HD:(h + 1) * HD] = (dqT[:, QW + h * BLK:QW + (h + 1) * BLK].T * SCALE).astype(BF16)

    def send_back_q(d, carry):
        for cp in back(d, (0,)):
            cp.start()
        return carry

    lax.fori_loop(1, nresp, send_back_q, 0)
    local(15).start()

    after_core(NZ - 1)
    after_y(NZ - 2)
    for h in range(GROUP):
        dqloc[:, h * HD:(h + 1) * HD] = (dqT[:, h * BLK:(h + 1) * BLK].T * SCALE).astype(BF16)
    local(12).start()
    y_send(NZ - 1).wait_recv()
    kept[NZ - 1] = kept[NZ - 1] + yrb[NZ - 1].astype(F32)

    got(zrb.at[pl.ds(0, NZ - 1)], gzr.at[0])
    total_kv = kept[NZ - 1]
    for n in range(1, NZ):
        total_kv = total_kv + zrb[n].astype(F32)
    dkvloc[0] = (total_kv[0] * SCALE).astype(BF16)
    dkvloc[1] = total_kv[1].astype(BF16)
    local(13).start()
    local(14).start()
    drain_gather(ksems)
    drain_gather(vsems)
    for n in range(5):
        sent(landings[n].at[pl.ds(0, others), :], as_.at[n])
    sent(grecv, gs.at[0])
    sent(ysb, gs.at[1])
    sent(zsb.at[pl.ds(0, NZ - 1)], gs.at[2])
    for n, (rows, part) in enumerate(((dqrows, dqr), (dkrows, dkr), (dvrows, dvr))):
        sent(rows.at[pl.ds(0, others), :], bs_.at[n])
        got(part.at[:, pl.ds(0, part.shape[1] * (nresp - 1) // nresp)], br_.at[n])
    for n in range(12, 18):
        local(n).wait()


def settle(*refs):
    n = len(refs) // 2
    for src, dst in zip(refs[:n], refs[n:]):
        dst[...] = src[...]


def solution(mesh):
    nresp = mesh.shape["resp"]
    nctx = mesh.shape["ctx"]

    def body(
        prompt_q, prompt_k, prompt_v, prompt_out, prompt_dout,
        resp_q, resp_k, resp_v, resp_out, resp_dout,
        lengths, resp_row, block_index,
    ):
        shape = jax.ShapeDtypeStruct
        smem = pl.BlockSpec(memory_space=pltpu.SMEM)
        vmem = pl.BlockSpec(memory_space=pltpu.VMEM)
        dma = pltpu.SemaphoreType.DMA
        anywhere = pl.BlockSpec(memory_space=pl.ANY)
        parts = pl.pallas_call(
            functools.partial(kernel, nresp),
            out_shape=(
                shape(prompt_q.shape, BF16),
                shape(prompt_k.shape, BF16),
                shape(prompt_v.shape, BF16),
                shape(resp_q.shape, BF16),
                shape(resp_k.shape, BF16),
                shape(resp_v.shape, BF16),
            ),
            in_specs=[smem] * 3 + [anywhere] * 10,
            out_specs=(anywhere,) * 6,
            scratch_shapes=[
                pltpu.VMEM((nctx, BLK, HD), BF16),
                pltpu.VMEM((nctx, BLK, HD), BF16),
                pltpu.VMEM((BLK, QW), BF16),
                pltpu.VMEM((BLK, QW), BF16),
                pltpu.VMEM((BLK, QW), BF16),
                pltpu.VMEM(resp_out.shape, BF16),
                pltpu.VMEM(resp_out.shape, BF16),
                pltpu.VMEM((BLK, QW), BF16),
                pltpu.VMEM((BLK, QW), BF16),
                pltpu.VMEM((BLK, HD), BF16),
                pltpu.VMEM((BLK, HD), BF16),
                pltpu.VMEM((BLK, 128), F32),
                pltpu.VMEM((nresp, 16, 128), F32),
                pltpu.VMEM((2 * QW, HD), BF16),
                pltpu.VMEM((2 * QW, HD), BF16),
                pltpu.VMEM((HD, 2 * QW), BF16),
                pltpu.VMEM((HD, 2 * QW), BF16),
                pltpu.VMEM((nctx * BLK, 2 * QW), BF16),
                pltpu.VMEM((BLK, QW), BF16),
                pltpu.VMEM((nctx + 1, 8, 2 * QW), F32),
                pltpu.VMEM((8, 2 * QW), F32),
                pltpu.VMEM((8, 2 * QW), F32),
                pltpu.VMEM((1, 2 * QW), F32),
                pltpu.VMEM((HD, 2 * QW), F32),
                pltpu.VMEM((CK, 2 * QW), BF16),
                pltpu.VMEM((CK, 2 * QW), BF16),
                pltpu.VMEM((CK, BLK), F32),
                pltpu.VMEM((NZ, 2, 2, 2, BLK, HD), F32),
                pltpu.VMEM((NZ, 2, 2, BLK, HD), F32),
                pltpu.VMEM((NZ, 2, BLK, HD), F32),
                pltpu.VMEM((NZ, 2, BLK, HD), BF16),
                pltpu.VMEM((NZ, 2, BLK, HD), BF16),
                pltpu.VMEM((NZ, 2, BLK, HD), BF16),
                pltpu.VMEM((NZ, 2, BLK, HD), BF16),
                pltpu.VMEM((BLK, QW), BF16),
                pltpu.VMEM((BLK, HD), BF16),
                pltpu.VMEM((BLK, HD), BF16),
                pltpu.VMEM((BLK, QW), BF16),
                pltpu.VMEM((2, BLK, HD), BF16),
                dma((2,)), dma((NZ, 2)), dma((NZ,)),
                dma((2,)), dma((NZ, 2)), dma((NZ,)),
                dma((5,)), dma((5,)),
                dma((3,)), dma((NZ,)), dma((NZ,)), dma((1,)),
                dma((3,)), dma((3,)),
                dma((18,)),
            ],
            compiler_params=pltpu.CompilerParams(
                collective_id=0, has_side_effects=True, vmem_limit_bytes=60 * 1024 * 1024
            ),
            name="attn_bwd",
        )(
            lengths, resp_row, block_index,
            prompt_q, prompt_k, prompt_v, prompt_out, prompt_dout,
            resp_q, resp_k, resp_v, resp_out, resp_dout,
        )
        return pl.pallas_call(
            settle,
            out_shape=tuple(shape(part.shape, part.dtype) for part in parts),
            in_specs=[vmem] * 6,
            out_specs=(vmem,) * 6,
            compiler_params=pltpu.CompilerParams(vmem_limit_bytes=60 * 1024 * 1024),
            name="settle",
        )(*parts)

    heads, rows, whole = P("ctx", "resp"), P(("ctx", "resp"), None), P()
    return jax.shard_map(
        body,
        mesh=mesh,
        in_specs=(heads,) * 5 + (rows,) * 5 + (whole,) * 3,
        out_specs=(heads,) * 3 + (rows,) * 3,
        check_vma=False,
    )
```

```python
import functools

import jax
import jax.numpy as jnp
from jax import lax
from jax.experimental import pallas as pl
from jax.experimental.pallas import tpu as pltpu
from jax.sharding import PartitionSpec as P

MESH = pl.DeviceIdType.MESH
F32, BF16 = jnp.float32, jnp.bfloat16
HD = 128
GROUP = 8
BLK = 128
NZ = 8
QW = GROUP * BLK
CK = 4 * BLK
QT = 512
GT = 1024
SCALE = HD ** -0.5
EXP_SCALE = SCALE * 1.4426950408889634
LOW = -1e30
NEG = float("-inf")
DEAD = 1 << 20


def dot(a, b):
    return jnp.dot(a, b, preferred_element_type=F32)


def kernel(
    nresp,
    len_any, row_any, bi_any,
    pq, pk, pv, pout, pdo, sq, sk, sv, sout, sdo,
    dqp, dkp, dvp, dqr, dkr, dvr,
    len_ref, row_ref, bi_ref,
    kk, vv, lq, lout, ldo, tout, tdo, rq, rdo, rk, rv, rdel, dbuf,
    qa, doa, qT, doT, pt, own_pt, mh, mrun, lrun, delta, dqT, psc, dssc, bias,
    gpart, grecv, kept, ysb, yrb, zsb, zrb, dqrows, dkrows, dvrows, dqloc, dkvloc,
    kx, kzr, kcr, vx, vzr, vcr, as_, ar_, gs, gcr, gyr, gzr, bs_, br_, loc,
):
    c = lax.axis_index("ctx")
    r = lax.axis_index("resp")
    z = c // 4
    lane4 = c % 4
    core = c % 2
    ylo = lane4 // 2
    cpart = c + 1 - 2 * core
    ystep = 2 - 4 * ylo
    ypart = c + ystep

    def zpeer(d):
        return lax.rem(z + d, NZ) * 4 + lane4

    def rpeer(d):
        return lax.rem(r + d, nresp)

    def remote(src, dst, ss, rs, dev):
        return pltpu.make_async_remote_copy(
            src_ref=src, dst_ref=dst, send_sem=ss, recv_sem=rs, device_id=dev, device_id_type=MESH
        )

    def got(part, sem):
        remote(part, part, sem, sem, (cpart, r)).wait_recv()

    def sent(part, sem):
        remote(part, part, sem, sem, (cpart, r)).wait_send()

    def zoff(i):
        return jnp.where(i % 2 == 1, (i + 1) // 2, (NZ - i // 2) % NZ)

    def cols(ref, p, w):
        return ref.at[:, pl.ds(pl.multiple_of(p * w, 128), w)]

    def slots(ref, p):
        return ref.at[pl.ds(pl.multiple_of(p * 16, 16), 16), :]

    pairs = (
        lambda: (pk, kk.at[c]),
        lambda: (pv, vv.at[c]),
        lambda: (pq, lq),
        lambda: (pdo, ldo),
        lambda: (sdo, tdo),
        lambda: (sout, tout),
        lambda: (pout, lout),
        lambda: (cols(sq, r, QW), slots(rq, r)),
        lambda: (cols(sdo, r, QW), slots(rdo, r)),
        lambda: (cols(sk, r, HD), slots(rk, r)),
        lambda: (cols(sv, r, HD), slots(rv, r)),
        lambda: (dbuf.at[r], slots(rdel, r)),
        lambda: (dqloc, dqp),
        lambda: (dkvloc.at[0], dkp),
        lambda: (dkvloc.at[1], dvp),
        lambda: (slots(dqrows, r), cols(dqr, r, QW)),
        lambda: (slots(dkrows, r), cols(dkr, r, HD)),
        lambda: (slots(dvrows, r), cols(dvr, r, HD)),
        lambda: (len_any, len_ref),
        lambda: (row_any, row_ref),
        lambda: (bi_any, bi_ref),
    )

    def local(n):
        src, dst = pairs[n]()
        return pltpu.make_async_copy(src, dst, loc.at[n])

    for n in (*range(11), 18, 19, 20):
        local(n).start()

    barrier = pltpu.get_barrier_semaphore()

    def greet(dev):
        pl.semaphore_signal(barrier, inc=1, device_id=dev, device_id_type=MESH)

    def greet_z(d, carry):
        greet((zpeer(d), r))
        return carry

    def greet_r(d, carry):
        greet((c, rpeer(d)))
        return carry

    lax.fori_loop(1, NZ, greet_z, 0)
    greet((cpart, r))
    greet((ypart, r))
    lax.fori_loop(1, nresp, greet_r, 0)
    pl.semaphore_wait(barrier, (NZ - 1) + (nresp - 1) + 2)

    ksems = (kk, kx, kzr, kcr)
    vsems = (vv, vx, vzr, vcr)

    def swap(sems):
        ref, x, zr, cr = sems
        return remote(ref.at[c], ref.at[c], x.at[0], x.at[1], (ypart, r))

    def swap_wait(sems):
        ref, x, zr, cr = sems
        got(ref.at[ypart], x.at[1])

    def hop(sems, d, e, far):
        ref, x, zr, cr = sems
        b = zpeer(d) + far * ystep
        to = (zpeer(lax.rem(d - e + NZ, NZ)), r)
        return remote(ref.at[b], ref.at[b], x.at[0], zr.at[e, far], to)

    def hop_wait(sems, d, far):
        ref, x, zr, cr = sems
        got(ref.at[zpeer(d) + far * ystep], zr.at[d, far])

    def share(sems, d, far):
        ref, x, zr, cr = sems
        b = zpeer(d) + far * ystep
        return remote(ref.at[b], ref.at[b], x.at[0], cr.at[d], (cpart, r))

    def share_wait(sems, d):
        ref, x, zr, cr = sems
        got(ref.at[pl.ds(lax.rem(z + d, NZ) * 4, 2)], cr.at[d])

    def begin(sems, far):
        for e in (1, NZ - 1, 2, NZ - 2):
            hop(sems, 0, e, far).start()
        share(sems, 0, far).start()

    def arrived(sems, i):
        d = zoff(i)
        for far in range(2):
            hop_wait(sems, d, far)
            share(sems, d, far).start()

    def relay(sems, d, e):
        for far in range(2):
            hop_wait(sems, d, far)
            hop(sems, d, e, far).start()
        hop(sems, d, NZ // 2, d // (NZ // 2)).start()
        for far in range(2):
            share(sems, d, far).start()

    def drain_gather(sems):
        ref, x, zr, cr = sems
        sent(ref.at[pl.ds(0, 4 * NZ - 1)], x.at[0])

    def sources(p):
        return (cols(sq, p, QW), cols(sdo, p, QW), cols(sk, p, HD), cols(sv, p, HD), dbuf.at[p])

    landings = (rq, rdo, rk, rv, rdel)

    def exchange(d, which):
        p = rpeer(d)
        src = sources(p)
        return [
            remote(src[n], slots(landings[n], r), as_.at[n], ar_.at[n], (c, p))
            for n in which
        ]

    def send_rows(n, carry):
        for cp in exchange(n, range(4)):
            cp.start()
        return carry

    local(0).wait()
    swap(ksems).start()
    begin(ksems, 0)
    local(1).wait()
    swap(vsems).start()
    lax.fori_loop(1, nresp, send_rows, 0)
    swap_wait(ksems)
    begin(ksems, 1)

    lane = lax.broadcasted_iota(jnp.int32, (128, 128), 1)
    subl = lax.broadcasted_iota(jnp.int32, (128, 128), 0)
    diff = lane - subl
    for n in (18, 19, 20):
        local(n).wait()
    my = bi_ref[c]

    def load_queries(q, do, base):
        for h in range(GROUP):
            sl = slice(h * HD, (h + 1) * HD)
            out = slice(base + h * BLK, base + (h + 1) * BLK)
            qh, dh = q[:, sl], do[:, sl]
            qa[out, :] = qh
            doa[out, :] = dh
            qT[:, out] = qh.T
            doT[:, out] = dh.T

    def place_delta(rows, base):
        rows_t = rows.T
        for h in range(GROUP):
            delta[:, base + h * BLK: base + (h + 1) * BLK] = rows_t[h:h + 1, :]

    local(2).wait()
    local(3).wait()
    load_queries(lq, ldo, 0)
    mrun[...] = jnp.full((8, 2 * QW), LOW, F32)
    lrun[...] = jnp.zeros((8, 2 * QW), F32)

    local(4).wait()
    local(5).wait()
    lane16 = lax.broadcasted_iota(jnp.int32, (16, 128), 1)
    for g in range(nresp):
        acc = jnp.zeros((16, 128), F32)
        for h in range(GROUP):
            sl = slice((g * GROUP + h) * HD, (g * GROUP + h + 1) * HD)
            prod = tout[:, sl].astype(F32) * tdo[:, sl].astype(F32)
            acc = jnp.where(lane16 == h, jnp.sum(prod, axis=1, keepdims=True), acc)
        dbuf[g] = acc

    def send_delta(d, carry):
        exchange(d, (4,))[0].start()
        return carry

    lax.fori_loop(1, nresp, send_delta, 0)
    local(11).start()

    def merge(p3, m, mo, sl):
        mrun[:, sl] = m
        lrun[:, sl] = lrun[:, sl] * jnp.exp2((mo - m) * EXP_SCALE) + jnp.sum(p3, axis=0)

    def stats_chunk(i, base, masked):
        zc = lax.rem(z + zoff(i), NZ)
        if masked:
            for b in range(4):
                ahead = (bi_ref[zc * 4 + b] - my) * BLK
                bias[b * BLK:(b + 1) * BLK, :] = jnp.where(diff >= ahead, 0.0, NEG)
        for t in range(QW // QT):
            sl = slice(base + t * QT, base + (t + 1) * QT)
            for b in range(4):
                s = dot(kk[zc * 4 + b], qT[:, sl])
                if masked:
                    s = s + jnp.concatenate([bias[b * BLK:(b + 1) * BLK, :]] * (QT // BLK), axis=1)
                s3 = s.reshape(BLK // 8, 8, QT)
                mo = mrun[:, sl]
                m = jnp.maximum(mo, jnp.max(s3, axis=0))
                p3 = jnp.exp2((s3 - m[None]) * EXP_SCALE)
                prow = pl.ds(pl.multiple_of(i * CK + b * BLK, BLK), BLK)
                pt[prow, sl] = p3.reshape(BLK, QT).astype(BF16)
                mh[i * 4 + b, :, sl] = m
                merge(p3, m, mo, sl)

    def prompt_stats(i, carry):
        @pl.when(i == 1)
        def _():
            relay(ksems, 2, 3)
            relay(ksems, NZ - 2, NZ - 3)
            begin(vsems, 0)
            arrived(ksems, 1)
            arrived(ksems, 2)

        @pl.when(i == 3)
        def _():
            swap_wait(vsems)
            begin(vsems, 1)

        d = zoff(i)
        share_wait(ksems, d)
        stats_chunk(i, 0, True)
        return carry

    lax.fori_loop(0, 5, prompt_stats, 0)

    local(6).wait()
    acc = jnp.zeros((BLK, 128), F32)
    for h in range(GROUP):
        sl = slice(h * HD, (h + 1) * HD)
        prod = lout[:, sl].astype(F32) * ldo[:, sl].astype(F32)
        acc = jnp.where(lane == h, jnp.sum(prod, axis=1, keepdims=True), acc)
    place_delta(acc, 0)

    others = 16 * (nresp - 1)
    for n in range(5):
        got(landings[n].at[pl.ds(0, others), :], ar_.at[n])
    for n in range(7, 12):
        local(n).wait()
    load_queries(rq, rdo, QW)
    place_delta(rdel[...], QW)

    lane1 = lax.broadcasted_iota(jnp.int32, (1, 128), 1)
    startq = jnp.full((1, 128), DEAD, jnp.int32)
    cum = jnp.int32(0)
    for n in range(len_ref.shape[0]):
        count = jnp.where(row_ref[n] == c, len_ref[n], 0)
        startq = jnp.where((lane1 >= cum) & (lane1 < cum + count), cum, startq)
        cum = cum + count
    live = jnp.where(startq < DEAD, 1.0, 0.0)
    own_mask = (subl >= startq) & (diff >= 0)
    for h in range(GROUP):
        sl = slice(QW + h * BLK, QW + (h + 1) * BLK)
        s3 = jnp.where(own_mask, dot(rk[...], qT[:, sl]), NEG).reshape(BLK // 8, 8, BLK)
        mo = mrun[:, sl]
        m = jnp.maximum(mo, jnp.max(s3, axis=0))
        p3 = jnp.exp2((s3 - m[None]) * EXP_SCALE)
        own_pt[:, h * BLK:(h + 1) * BLK] = p3.reshape(BLK, BLK).astype(BF16)
        mh[4 * NZ, :, sl] = m
        merge(p3, m, mo, sl)

    def resp_stats(i, carry):
        stats_chunk(i, QW, False)
        return carry

    lax.fori_loop(0, 5, resp_stats, 0)
    for n in range(5, NZ):
        arrived(ksems, n)

    def late_stats(i, carry):
        @pl.when(i == NZ - 1)
        def _():
            relay(vsems, 2, 3)
            relay(vsems, NZ - 2, NZ - 3)
            arrived(vsems, 1)
            arrived(vsems, 2)

        d = zoff(i)
        share_wait(ksems, d)
        stats_chunk(i, 0, True)
        stats_chunk(i, QW, False)
        return carry

    lax.fori_loop(5, NZ, late_stats, 0)

    peak = jnp.max(mrun[...], axis=0, keepdims=True)
    total = jnp.sum(lrun[...] * jnp.exp2((mrun[...] - peak) * EXP_SCALE), axis=0, keepdims=True)
    inv = jnp.where(total > 0.0, 1.0 / total, 0.0)
    inv = inv * jnp.concatenate([jnp.ones((1, QW), F32)] + [live] * GROUP, axis=1)
    for n in range(4 * NZ):
        mh[n] = jnp.exp2((mh[n] - peak) * EXP_SCALE) * inv
    own_f = jnp.exp2((mh[4 * NZ, :, QW:] - peak[:, QW:]) * EXP_SCALE) * inv[:, QW:]
    dqT[...] = jnp.zeros_like(dqT)

    def back(d, which):
        p = rpeer(d)
        dev = (c, p)
        out = (
            lambda: remote(slots(dqrows, p), cols(dqr, r, QW), bs_.at[0], br_.at[0], dev),
            lambda: remote(slots(dkrows, p), cols(dkr, r, HD), bs_.at[1], br_.at[1], dev),
            lambda: remote(slots(dvrows, p), cols(dvr, r, HD), bs_.at[2], br_.at[2], dev),
        )
        return [out[n]() for n in which]

    rkT = rk[...].T
    for h in range(GROUP):
        sl = slice(QW + h * BLK, QW + (h + 1) * BLK)
        hs = slice(h * BLK, (h + 1) * BLK)
        dp = dot(rv[...], doT[:, sl])
        p3 = own_pt[:, hs].astype(F32).reshape(BLK // 8, 8, BLK) * own_f[:, hs][None]
        p = p3.reshape(BLK, BLK)
        ds = (p * (dp - delta[:, sl])).astype(BF16)
        psc[0:BLK, sl] = p.astype(BF16)
        dssc[0:BLK, sl] = ds
        dqT[:, sl] += dot(rkT, ds)
    dvrows[...] = dot(psc[0:BLK, QW:], doa[QW:, :]).astype(BF16)
    dkrows[...] = (dot(dssc[0:BLK, QW:], qa[QW:, :]) * SCALE).astype(BF16)

    def send_back_kv(d, carry):
        for cp in back(d, (1, 2)):
            cp.start()
        return carry

    lax.fori_loop(1, nresp, send_back_kv, 0)
    local(16).start()
    local(17).start()

    def core_send(j):
        return remote(gpart.at[j, 1 - core], grecv.at[j], gs.at[0], gcr.at[j], (cpart, r))

    def y_send(j):
        return remote(ysb.at[j], yrb.at[j], gs.at[1], gyr.at[j], (ypart, r))

    def z_send(j):
        d = zoff((j + 1) % NZ)
        return remote(zsb.at[j], zrb.at[NZ - d], gs.at[2], gzr.at[0], (zpeer(d), r))

    def after_core(j):
        core_send(j).wait_recv()
        kept[j] = gpart[j, core, ylo] + grecv[j, ylo]
        ysb[j] = (gpart[j, core, 1 - ylo] + grecv[j, 1 - ylo]).astype(BF16)
        y_send(j).start()

    def after_y(j):
        y_send(j).wait_recv()
        zsb[j] = (kept[j] + yrb[j].astype(F32)).astype(BF16)
        z_send(j).start()

    def grads(j, carry):
        i = (j + 1) % NZ
        d = zoff(i)
        zc = lax.rem(z + d, NZ)

        @pl.when(j == 2)
        def _():
            for n in range(5, NZ):
                arrived(vsems, n)

        share_wait(vsems, d)
        vc_rows = vv[pl.ds(zc * 4, 4)].reshape(CK, HD)
        kTc = kk[pl.ds(zc * 4, 4)].reshape(CK, HD).T
        prow = pl.ds(pl.multiple_of(i * CK, CK), CK)
        for t in range(2 * QW // GT):
            sl = slice(t * GT, (t + 1) * GT)
            dp = dot(vc_rows, doT[:, sl])
            f = mh[pl.ds(i * 4, 4), :, sl][:, None]
            p = (pt[prow, sl].astype(F32).reshape(4, BLK // 8, 8, GT) * f).reshape(CK, GT)
            ds = (p * (dp - delta[:, sl])).astype(BF16)
            psc[:, sl] = p.astype(BF16)
            dssc[:, sl] = ds
            dqT[:, sl] += dot(kTc, ds)
        dk = dot(dssc[...], qa[...])
        dv = dot(psc[...], doa[...])
        for b in range(4):
            gpart[j, b % 2, b // 2, 0] = dk[b * BLK:(b + 1) * BLK, :]
            gpart[j, b % 2, b // 2, 1] = dv[b * BLK:(b + 1) * BLK, :]
        core_send(j).start()

        @pl.when(j >= 1)
        def _():
            after_core(j - 1)

        @pl.when(j >= 2)
        def _():
            after_y(j - 2)

        return carry

    lax.fori_loop(0, NZ, grads, 0)

    for h in range(GROUP):
        dqrows[:, h * HD:(h + 1) * HD] = (dqT[:, QW + h * BLK:QW + (h + 1) * BLK].T * SCALE).astype(BF16)

    def send_back_q(d, carry):
        for cp in back(d, (0,)):
            cp.start()
        return carry

    lax.fori_loop(1, nresp, send_back_q, 0)
    local(15).start()

    after_core(NZ - 1)
    after_y(NZ - 2)
    for h in range(GROUP):
        dqloc[:, h * HD:(h + 1) * HD] = (dqT[:, h * BLK:(h + 1) * BLK].T * SCALE).astype(BF16)
    local(12).start()
    y_send(NZ - 1).wait_recv()
    kept[NZ - 1] = kept[NZ - 1] + yrb[NZ - 1].astype(F32)

    got(zrb.at[pl.ds(0, NZ - 1)], gzr.at[0])
    total_kv = kept[NZ - 1]
    for n in range(1, NZ):
        total_kv = total_kv + zrb[n].astype(F32)
    dkvloc[0] = (total_kv[0] * SCALE).astype(BF16)
    dkvloc[1] = total_kv[1].astype(BF16)
    local(13).start()
    local(14).start()
    drain_gather(ksems)
    drain_gather(vsems)
    for n in range(5):
        sent(landings[n].at[pl.ds(0, others), :], as_.at[n])
    sent(grecv, gs.at[0])
    sent(ysb, gs.at[1])
    sent(zsb.at[pl.ds(0, NZ - 1)], gs.at[2])
    for n, (rows, part) in enumerate(((dqrows, dqr), (dkrows, dkr), (dvrows, dvr))):
        sent(rows.at[pl.ds(0, others), :], bs_.at[n])
        got(part.at[:, pl.ds(0, part.shape[1] * (nresp - 1) // nresp)], br_.at[n])
    for n in range(12, 18):
        local(n).wait()


def settle(*refs):
    n = len(refs) // 2
    for src, dst in zip(refs[:n], refs[n:]):
        dst[...] = src[...]


def solution(mesh):
    nresp = mesh.shape["resp"]
    nctx = mesh.shape["ctx"]

    def body(
        prompt_q, prompt_k, prompt_v, prompt_out, prompt_dout,
        resp_q, resp_k, resp_v, resp_out, resp_dout,
        lengths, resp_row, block_index,
    ):
        shape = jax.ShapeDtypeStruct
        vmem = pl.BlockSpec(memory_space=pltpu.VMEM)
        dma = pltpu.SemaphoreType.DMA
        anywhere = pl.BlockSpec(memory_space=pl.ANY)
        parts = pl.pallas_call(
            functools.partial(kernel, nresp),
            out_shape=(
                shape(prompt_q.shape, BF16),
                shape(prompt_k.shape, BF16),
                shape(prompt_v.shape, BF16),
                shape(resp_q.shape, BF16),
                shape(resp_k.shape, BF16),
                shape(resp_v.shape, BF16),
            ),
            in_specs=[anywhere] * 13,
            out_specs=(anywhere,) * 6,
            scratch_shapes=[
                pltpu.SMEM(lengths.shape, jnp.int32),
                pltpu.SMEM(resp_row.shape, jnp.int32),
                pltpu.SMEM(block_index.shape, jnp.int32),
                pltpu.VMEM((nctx, BLK, HD), BF16),
                pltpu.VMEM((nctx, BLK, HD), BF16),
                pltpu.VMEM((BLK, QW), BF16),
                pltpu.VMEM((BLK, QW), BF16),
                pltpu.VMEM((BLK, QW), BF16),
                pltpu.VMEM(resp_out.shape, BF16),
                pltpu.VMEM(resp_out.shape, BF16),
                pltpu.VMEM((BLK, QW), BF16),
                pltpu.VMEM((BLK, QW), BF16),
                pltpu.VMEM((BLK, HD), BF16),
                pltpu.VMEM((BLK, HD), BF16),
                pltpu.VMEM((BLK, 128), F32),
                pltpu.VMEM((nresp, 16, 128), F32),
                pltpu.VMEM((2 * QW, HD), BF16),
                pltpu.VMEM((2 * QW, HD), BF16),
                pltpu.VMEM((HD, 2 * QW), BF16),
                pltpu.VMEM((HD, 2 * QW), BF16),
                pltpu.VMEM((nctx * BLK, 2 * QW), BF16),
                pltpu.VMEM((BLK, QW), BF16),
                pltpu.VMEM((nctx + 1, 8, 2 * QW), F32),
                pltpu.VMEM((8, 2 * QW), F32),
                pltpu.VMEM((8, 2 * QW), F32),
                pltpu.VMEM((1, 2 * QW), F32),
                pltpu.VMEM((HD, 2 * QW), F32),
                pltpu.VMEM((CK, 2 * QW), BF16),
                pltpu.VMEM((CK, 2 * QW), BF16),
                pltpu.VMEM((CK, BLK), F32),
                pltpu.VMEM((NZ, 2, 2, 2, BLK, HD), F32),
                pltpu.VMEM((NZ, 2, 2, BLK, HD), F32),
                pltpu.VMEM((NZ, 2, BLK, HD), F32),
                pltpu.VMEM((NZ, 2, BLK, HD), BF16),
                pltpu.VMEM((NZ, 2, BLK, HD), BF16),
                pltpu.VMEM((NZ, 2, BLK, HD), BF16),
                pltpu.VMEM((NZ, 2, BLK, HD), BF16),
                pltpu.VMEM((BLK, QW), BF16),
                pltpu.VMEM((BLK, HD), BF16),
                pltpu.VMEM((BLK, HD), BF16),
                pltpu.VMEM((BLK, QW), BF16),
                pltpu.VMEM((2, BLK, HD), BF16),
                dma((2,)), dma((NZ, 2)), dma((NZ,)),
                dma((2,)), dma((NZ, 2)), dma((NZ,)),
                dma((5,)), dma((5,)),
                dma((3,)), dma((NZ,)), dma((NZ,)), dma((1,)),
                dma((3,)), dma((3,)),
                dma((21,)),
            ],
            compiler_params=pltpu.CompilerParams(
                collective_id=0, has_side_effects=True, vmem_limit_bytes=60 * 1024 * 1024
            ),
            name="attn_bwd",
        )(
            lengths, resp_row, block_index,
            prompt_q, prompt_k, prompt_v, prompt_out, prompt_dout,
            resp_q, resp_k, resp_v, resp_out, resp_dout,
        )
        return pl.pallas_call(
            settle,
            out_shape=tuple(shape(part.shape, part.dtype) for part in parts),
            in_specs=[vmem] * 6,
            out_specs=(vmem,) * 6,
            compiler_params=pltpu.CompilerParams(vmem_limit_bytes=60 * 1024 * 1024),
            name="settle",
        )(*parts)

    heads, rows, whole = P("ctx", "resp"), P(("ctx", "resp"), None), P()
    return jax.shard_map(
        body,
        mesh=mesh,
        in_specs=(heads,) * 5 + (rows,) * 5 + (whole,) * 3,
        out_specs=(heads,) * 3 + (rows,) * 3,
        check_vma=False,
    )
```

```python
import functools

import jax
import jax.numpy as jnp
from jax import lax
from jax.experimental import pallas as pl
from jax.experimental.pallas import tpu as pltpu
from jax.sharding import PartitionSpec as P

MESH = pl.DeviceIdType.MESH
F32, BF16 = jnp.float32, jnp.bfloat16
HD = 128
GROUP = 8
BLK = 128
NZ = 8
QW = GROUP * BLK
CK = 4 * BLK
QT = 512
GT = 1024
SCALE = HD ** -0.5
EXP_SCALE = SCALE * 1.4426950408889634
LOW = -1e30
NEG = float("-inf")
DEAD = 1 << 20


def dot(a, b):
    return jnp.dot(a, b, preferred_element_type=F32)


def kernel(
    nresp,
    len_any, row_any, bi_any,
    pq, pk, pv, pout, pdo, sq, sk, sv, sout, sdo,
    dqp, dkp, dvp, dqr, dkr, dvr,
    len_ref, row_ref, bi_ref,
    kk, vv, lq, lout, ldo, tout, tdo, rq, rdo, rk, rv, rdel, dbuf,
    qa, doa, qT, doT, pt, own_pt, mh, mrun, lrun, delta, dqT, psc, dssc, bias,
    gpart, grecv, kept, ysb, yrb, zsb, zrb, dqrows, dkrows, dvrows, dqloc, dkvloc,
    kx, kzr, kcr, vx, vzr, vcr, as_, ar_, gs, gcr, gyr, gzr, bs_, br_, loc,
):
    c = lax.axis_index("ctx")
    r = lax.axis_index("resp")
    z = c // 4
    lane4 = c % 4
    core = c % 2
    ylo = lane4 // 2
    cpart = c + 1 - 2 * core
    ystep = 2 - 4 * ylo
    ypart = c + ystep

    def zpeer(d):
        return lax.rem(z + d, NZ) * 4 + lane4

    def rpeer(d):
        return lax.rem(r + d, nresp)

    def remote(src, dst, ss, rs, dev):
        return pltpu.make_async_remote_copy(
            src_ref=src, dst_ref=dst, send_sem=ss, recv_sem=rs, device_id=dev, device_id_type=MESH
        )

    def got(part, sem):
        remote(part, part, sem, sem, (cpart, r)).wait_recv()

    def sent(part, sem):
        remote(part, part, sem, sem, (cpart, r)).wait_send()

    def zoff(i):
        return jnp.where(i % 2 == 1, (i + 1) // 2, (NZ - i // 2) % NZ)

    def order(j):
        return jnp.where(j < 2, j + 1, jnp.where(j < 5, j + 3, jnp.where(j < 7, j - 2, 0)))

    def cols(ref, p, w):
        return ref.at[:, pl.ds(pl.multiple_of(p * w, 128), w)]

    def slots(ref, p):
        return ref.at[pl.ds(pl.multiple_of(p * 16, 16), 16), :]

    pairs = (
        lambda: (pk, kk.at[c]),
        lambda: (pv, vv.at[c]),
        lambda: (pq, lq),
        lambda: (pdo, ldo),
        lambda: (sdo, tdo),
        lambda: (sout, tout),
        lambda: (pout, lout),
        lambda: (cols(sq, r, QW), slots(rq, r)),
        lambda: (cols(sdo, r, QW), slots(rdo, r)),
        lambda: (cols(sk, r, HD), slots(rk, r)),
        lambda: (cols(sv, r, HD), slots(rv, r)),
        lambda: (dbuf.at[r], slots(rdel, r)),
        lambda: (dqloc, dqp),
        lambda: (dkvloc.at[0], dkp),
        lambda: (dkvloc.at[1], dvp),
        lambda: (slots(dqrows, r), cols(dqr, r, QW)),
        lambda: (slots(dkrows, r), cols(dkr, r, HD)),
        lambda: (slots(dvrows, r), cols(dvr, r, HD)),
        lambda: (len_any, len_ref),
        lambda: (row_any, row_ref),
        lambda: (bi_any, bi_ref),
    )

    def local(n):
        src, dst = pairs[n]()
        return pltpu.make_async_copy(src, dst, loc.at[n])

    for n in (*range(11), 18, 19, 20):
        local(n).start()

    barrier = pltpu.get_barrier_semaphore()

    def greet(dev):
        pl.semaphore_signal(barrier, inc=1, device_id=dev, device_id_type=MESH)

    def greet_z(d, carry):
        greet((zpeer(d), r))
        return carry

    def greet_r(d, carry):
        greet((c, rpeer(d)))
        return carry

    lax.fori_loop(1, NZ, greet_z, 0)
    greet((cpart, r))
    greet((ypart, r))
    lax.fori_loop(1, nresp, greet_r, 0)
    pl.semaphore_wait(barrier, (NZ - 1) + (nresp - 1) + 2)

    ksems = (kk, kx, kzr, kcr)
    vsems = (vv, vx, vzr, vcr)

    def swap(sems):
        ref, x, zr, cr = sems
        return remote(ref.at[c], ref.at[c], x.at[0], x.at[1], (ypart, r))

    def swap_wait(sems):
        ref, x, zr, cr = sems
        got(ref.at[ypart], x.at[1])

    def hop(sems, d, e, far):
        ref, x, zr, cr = sems
        b = zpeer(d) + far * ystep
        to = (zpeer(lax.rem(d - e + NZ, NZ)), r)
        return remote(ref.at[b], ref.at[b], x.at[0], zr.at[e, far], to)

    def hop_wait(sems, d, far):
        ref, x, zr, cr = sems
        got(ref.at[zpeer(d) + far * ystep], zr.at[d, far])

    def share(sems, d, far):
        ref, x, zr, cr = sems
        b = zpeer(d) + far * ystep
        return remote(ref.at[b], ref.at[b], x.at[0], cr.at[d], (cpart, r))

    def share_wait(sems, d):
        ref, x, zr, cr = sems
        got(ref.at[pl.ds(lax.rem(z + d, NZ) * 4, 2)], cr.at[d])

    def begin(sems, far):
        for e in (1, NZ - 1, 2, NZ - 2):
            hop(sems, 0, e, far).start()
        share(sems, 0, far).start()

    def arrived(sems, i):
        d = zoff(i)
        for far in range(2):
            hop_wait(sems, d, far)
            share(sems, d, far).start()

    def relay(sems, d, e):
        for far in range(2):
            hop_wait(sems, d, far)
            hop(sems, d, e, far).start()
        hop(sems, d, NZ // 2, d // (NZ // 2)).start()
        for far in range(2):
            share(sems, d, far).start()

    def drain_gather(sems):
        ref, x, zr, cr = sems
        sent(ref.at[pl.ds(0, 4 * NZ - 1)], x.at[0])

    def sources(p):
        return (cols(sq, p, QW), cols(sdo, p, QW), cols(sk, p, HD), cols(sv, p, HD), dbuf.at[p])

    landings = (rq, rdo, rk, rv, rdel)

    def exchange(d, which):
        p = rpeer(d)
        src = sources(p)
        return [
            remote(src[n], slots(landings[n], r), as_.at[n], ar_.at[n], (c, p))
            for n in which
        ]

    def send_rows(n, carry):
        for cp in exchange(n, range(4)):
            cp.start()
        return carry

    local(0).wait()
    swap(ksems).start()
    begin(ksems, 0)
    local(1).wait()
    swap(vsems).start()
    lax.fori_loop(1, nresp, send_rows, 0)
    swap_wait(ksems)
    begin(ksems, 1)

    lane = lax.broadcasted_iota(jnp.int32, (128, 128), 1)
    subl = lax.broadcasted_iota(jnp.int32, (128, 128), 0)
    diff = lane - subl
    for n in (18, 19, 20):
        local(n).wait()
    my = bi_ref[c]

    def load_queries(q, do, base):
        for h in range(GROUP):
            sl = slice(h * HD, (h + 1) * HD)
            out = slice(base + h * BLK, base + (h + 1) * BLK)
            qh, dh = q[:, sl], do[:, sl]
            qa[out, :] = qh
            doa[out, :] = dh
            qT[:, out] = qh.T
            doT[:, out] = dh.T

    def place_delta(rows, base):
        rows_t = rows.T
        for h in range(GROUP):
            delta[:, base + h * BLK: base + (h + 1) * BLK] = rows_t[h:h + 1, :]

    local(2).wait()
    local(3).wait()
    load_queries(lq, ldo, 0)
    mrun[...] = jnp.full((8, 2 * QW), LOW, F32)
    lrun[...] = jnp.zeros((8, 2 * QW), F32)

    local(4).wait()
    local(5).wait()
    lane16 = lax.broadcasted_iota(jnp.int32, (16, 128), 1)
    for g in range(nresp):
        acc = jnp.zeros((16, 128), F32)
        for h in range(GROUP):
            sl = slice((g * GROUP + h) * HD, (g * GROUP + h + 1) * HD)
            prod = tout[:, sl].astype(F32) * tdo[:, sl].astype(F32)
            acc = jnp.where(lane16 == h, jnp.sum(prod, axis=1, keepdims=True), acc)
        dbuf[g] = acc

    def send_delta(d, carry):
        exchange(d, (4,))[0].start()
        return carry

    lax.fori_loop(1, nresp, send_delta, 0)
    local(11).start()

    def merge(p3, m, mo, sl):
        mrun[:, sl] = m
        lrun[:, sl] = lrun[:, sl] * jnp.exp2((mo - m) * EXP_SCALE) + jnp.sum(p3, axis=0)

    def stats_chunk(i, base, masked):
        zc = lax.rem(z + zoff(i), NZ)
        if masked:
            for b in range(4):
                ahead = (bi_ref[zc * 4 + b] - my) * BLK
                bias[b * BLK:(b + 1) * BLK, :] = jnp.where(diff >= ahead, 0.0, NEG)
        for t in range(QW // QT):
            sl = slice(base + t * QT, base + (t + 1) * QT)
            for b in range(4):
                s = dot(kk[zc * 4 + b], qT[:, sl])
                if masked:
                    s = s + jnp.concatenate([bias[b * BLK:(b + 1) * BLK, :]] * (QT // BLK), axis=1)
                s3 = s.reshape(BLK // 8, 8, QT)
                mo = mrun[:, sl]
                m = jnp.maximum(mo, jnp.max(s3, axis=0))
                p3 = jnp.exp2((s3 - m[None]) * EXP_SCALE)
                prow = pl.ds(pl.multiple_of(i * CK + b * BLK, BLK), BLK)
                pt[prow, sl] = p3.reshape(BLK, QT).astype(BF16)
                mh[i * 4 + b, :, sl] = m
                merge(p3, m, mo, sl)

    def prompt_stats(i, carry):
        @pl.when(i == 1)
        def _():
            relay(ksems, 2, 3)
            relay(ksems, NZ - 2, NZ - 3)
            begin(vsems, 0)
            arrived(ksems, 1)
            arrived(ksems, 2)

        @pl.when(i == 3)
        def _():
            swap_wait(vsems)
            begin(vsems, 1)

        d = zoff(i)
        share_wait(ksems, d)
        stats_chunk(i, 0, True)
        return carry

    lax.fori_loop(0, 5, prompt_stats, 0)

    local(6).wait()
    acc = jnp.zeros((BLK, 128), F32)
    for h in range(GROUP):
        sl = slice(h * HD, (h + 1) * HD)
        prod = lout[:, sl].astype(F32) * ldo[:, sl].astype(F32)
        acc = jnp.where(lane == h, jnp.sum(prod, axis=1, keepdims=True), acc)
    place_delta(acc, 0)

    others = 16 * (nresp - 1)
    for n in range(5):
        got(landings[n].at[pl.ds(0, others), :], ar_.at[n])
    for n in range(7, 12):
        local(n).wait()
    load_queries(rq, rdo, QW)
    place_delta(rdel[...], QW)

    lane1 = lax.broadcasted_iota(jnp.int32, (1, 128), 1)
    startq = jnp.full((1, 128), DEAD, jnp.int32)
    cum = jnp.int32(0)
    for n in range(len_ref.shape[0]):
        count = jnp.where(row_ref[n] == c, len_ref[n], 0)
        startq = jnp.where((lane1 >= cum) & (lane1 < cum + count), cum, startq)
        cum = cum + count
    live = jnp.where(startq < DEAD, 1.0, 0.0)
    own_mask = (subl >= startq) & (diff >= 0)
    for h in range(GROUP):
        sl = slice(QW + h * BLK, QW + (h + 1) * BLK)
        s3 = jnp.where(own_mask, dot(rk[...], qT[:, sl]), NEG).reshape(BLK // 8, 8, BLK)
        mo = mrun[:, sl]
        m = jnp.maximum(mo, jnp.max(s3, axis=0))
        p3 = jnp.exp2((s3 - m[None]) * EXP_SCALE)
        own_pt[:, h * BLK:(h + 1) * BLK] = p3.reshape(BLK, BLK).astype(BF16)
        mh[4 * NZ, :, sl] = m
        merge(p3, m, mo, sl)

    def resp_stats(i, carry):
        stats_chunk(i, QW, False)
        return carry

    lax.fori_loop(0, 5, resp_stats, 0)
    for n in range(5, NZ):
        arrived(ksems, n)

    def late_stats(i, carry):
        @pl.when(i == NZ - 1)
        def _():
            relay(vsems, 2, 3)
            relay(vsems, NZ - 2, NZ - 3)
            arrived(vsems, 1)
            arrived(vsems, 2)

        d = zoff(i)
        share_wait(ksems, d)
        stats_chunk(i, 0, True)
        stats_chunk(i, QW, False)
        return carry

    lax.fori_loop(5, NZ, late_stats, 0)

    peak = jnp.max(mrun[...], axis=0, keepdims=True)
    total = jnp.sum(lrun[...] * jnp.exp2((mrun[...] - peak) * EXP_SCALE), axis=0, keepdims=True)
    inv = jnp.where(total > 0.0, 1.0 / total, 0.0)
    inv = inv * jnp.concatenate([jnp.ones((1, QW), F32)] + [live] * GROUP, axis=1)
    for n in range(4 * NZ):
        mh[n] = jnp.exp2((mh[n] - peak) * EXP_SCALE) * inv
    own_f = jnp.exp2((mh[4 * NZ, :, QW:] - peak[:, QW:]) * EXP_SCALE) * inv[:, QW:]
    dqT[...] = jnp.zeros_like(dqT)

    def back(d, which):
        p = rpeer(d)
        dev = (c, p)
        out = (
            lambda: remote(slots(dqrows, p), cols(dqr, r, QW), bs_.at[0], br_.at[0], dev),
            lambda: remote(slots(dkrows, p), cols(dkr, r, HD), bs_.at[1], br_.at[1], dev),
            lambda: remote(slots(dvrows, p), cols(dvr, r, HD), bs_.at[2], br_.at[2], dev),
        )
        return [out[n]() for n in which]

    rkT = rk[...].T
    for h in range(GROUP):
        sl = slice(QW + h * BLK, QW + (h + 1) * BLK)
        hs = slice(h * BLK, (h + 1) * BLK)
        dp = dot(rv[...], doT[:, sl])
        p3 = own_pt[:, hs].astype(F32).reshape(BLK // 8, 8, BLK) * own_f[:, hs][None]
        p = p3.reshape(BLK, BLK)
        ds = (p * (dp - delta[:, sl])).astype(BF16)
        psc[0:BLK, sl] = p.astype(BF16)
        dssc[0:BLK, sl] = ds
        dqT[:, sl] += dot(rkT, ds)
    dvrows[...] = dot(psc[0:BLK, QW:], doa[QW:, :]).astype(BF16)
    dkrows[...] = (dot(dssc[0:BLK, QW:], qa[QW:, :]) * SCALE).astype(BF16)

    def send_back_kv(d, carry):
        for cp in back(d, (1, 2)):
            cp.start()
        return carry

    lax.fori_loop(1, nresp, send_back_kv, 0)
    local(16).start()
    local(17).start()

    def core_send(j):
        return remote(gpart.at[j, 1 - core], grecv.at[j], gs.at[0], gcr.at[j], (cpart, r))

    def y_send(j):
        return remote(ysb.at[j], yrb.at[j], gs.at[1], gyr.at[j], (ypart, r))

    def z_send(j):
        d = zoff(order(j))
        return remote(zsb.at[j], zrb.at[NZ - d], gs.at[2], gzr.at[0], (zpeer(d), r))

    def after_core(j):
        core_send(j).wait_recv()
        kept[j] = gpart[j, core, ylo] + grecv[j, ylo]
        ysb[j] = (gpart[j, core, 1 - ylo] + grecv[j, 1 - ylo]).astype(BF16)
        y_send(j).start()

    def after_y(j):
        y_send(j).wait_recv()
        zsb[j] = (kept[j] + yrb[j].astype(F32)).astype(BF16)
        z_send(j).start()

    def grads(j, last):
        i = order(j)
        d = zoff(i)
        zc = lax.rem(z + d, NZ)

        if not last:
            @pl.when(j == 1)
            def _():
                for n in range(5, NZ):
                    arrived(vsems, n)

        share_wait(vsems, d)
        vc_rows = vv[pl.ds(zc * 4, 4)].reshape(CK, HD)
        kTc = kk[pl.ds(zc * 4, 4)].reshape(CK, HD).T
        prow = pl.ds(pl.multiple_of(i * CK, CK), CK)
        for t in range(2 * QW // GT):
            sl = slice(t * GT, (t + 1) * GT)
            dp = dot(vc_rows, doT[:, sl])
            f = mh[pl.ds(i * 4, 4), :, sl][:, None]
            p = (pt[prow, sl].astype(F32).reshape(4, BLK // 8, 8, GT) * f).reshape(CK, GT)
            ds = (p * (dp - delta[:, sl])).astype(BF16)
            psc[:, sl] = p.astype(BF16)
            dssc[:, sl] = ds
            dqT[:, sl] += dot(kTc, ds)
        if last:
            after_core(j - 1)
        dk = dot(dssc[...], qa[...])
        dv = dot(psc[...], doa[...])
        for b in range(4):
            gpart[j, b % 2, b // 2, 0] = dk[b * BLK:(b + 1) * BLK, :]
            gpart[j, b % 2, b // 2, 1] = dv[b * BLK:(b + 1) * BLK, :]
        core_send(j).start()
        if last:
            after_y(j - 2)
            return

        @pl.when(j >= 1)
        def _():
            after_core(j - 1)

        @pl.when(j >= 2)
        def _():
            after_y(j - 2)

    def grads_step(j, carry):
        grads(j, False)
        return carry

    lax.fori_loop(0, NZ - 1, grads_step, 0)
    grads(NZ - 1, True)

    for h in range(GROUP):
        dqrows[:, h * HD:(h + 1) * HD] = (dqT[:, QW + h * BLK:QW + (h + 1) * BLK].T * SCALE).astype(BF16)

    def send_back_q(d, carry):
        for cp in back(d, (0,)):
            cp.start()
        return carry

    lax.fori_loop(1, nresp, send_back_q, 0)
    local(15).start()

    after_core(NZ - 1)
    after_y(NZ - 2)
    for h in range(GROUP):
        dqloc[:, h * HD:(h + 1) * HD] = (dqT[:, h * BLK:(h + 1) * BLK].T * SCALE).astype(BF16)
    local(12).start()
    y_send(NZ - 1).wait_recv()
    kept[NZ - 1] = kept[NZ - 1] + yrb[NZ - 1].astype(F32)

    got(zrb.at[pl.ds(0, NZ - 1)], gzr.at[0])
    total_kv = kept[NZ - 1]
    for n in range(1, NZ):
        total_kv = total_kv + zrb[n].astype(F32)
    dkvloc[0] = (total_kv[0] * SCALE).astype(BF16)
    dkvloc[1] = total_kv[1].astype(BF16)
    local(13).start()
    local(14).start()
    drain_gather(ksems)
    drain_gather(vsems)
    for n in range(5):
        sent(landings[n].at[pl.ds(0, others), :], as_.at[n])
    sent(grecv, gs.at[0])
    sent(ysb, gs.at[1])
    sent(zsb.at[pl.ds(0, NZ - 1)], gs.at[2])
    for n, (rows, part) in enumerate(((dqrows, dqr), (dkrows, dkr), (dvrows, dvr))):
        sent(rows.at[pl.ds(0, others), :], bs_.at[n])
        got(part.at[:, pl.ds(0, part.shape[1] * (nresp - 1) // nresp)], br_.at[n])
    for n in range(12, 18):
        local(n).wait()


def settle(*refs):
    n = len(refs) // 2
    for src, dst in zip(refs[:n], refs[n:]):
        dst[...] = src[...]


def solution(mesh):
    nresp = mesh.shape["resp"]
    nctx = mesh.shape["ctx"]

    def body(
        prompt_q, prompt_k, prompt_v, prompt_out, prompt_dout,
        resp_q, resp_k, resp_v, resp_out, resp_dout,
        lengths, resp_row, block_index,
    ):
        shape = jax.ShapeDtypeStruct
        vmem = pl.BlockSpec(memory_space=pltpu.VMEM)
        dma = pltpu.SemaphoreType.DMA
        anywhere = pl.BlockSpec(memory_space=pl.ANY)
        parts = pl.pallas_call(
            functools.partial(kernel, nresp),
            out_shape=(
                shape(prompt_q.shape, BF16),
                shape(prompt_k.shape, BF16),
                shape(prompt_v.shape, BF16),
                shape(resp_q.shape, BF16),
                shape(resp_k.shape, BF16),
                shape(resp_v.shape, BF16),
            ),
            in_specs=[anywhere] * 13,
            out_specs=(anywhere,) * 6,
            scratch_shapes=[
                pltpu.SMEM(lengths.shape, jnp.int32),
                pltpu.SMEM(resp_row.shape, jnp.int32),
                pltpu.SMEM(block_index.shape, jnp.int32),
                pltpu.VMEM((nctx, BLK, HD), BF16),
                pltpu.VMEM((nctx, BLK, HD), BF16),
                pltpu.VMEM((BLK, QW), BF16),
                pltpu.VMEM((BLK, QW), BF16),
                pltpu.VMEM((BLK, QW), BF16),
                pltpu.VMEM(resp_out.shape, BF16),
                pltpu.VMEM(resp_out.shape, BF16),
                pltpu.VMEM((BLK, QW), BF16),
                pltpu.VMEM((BLK, QW), BF16),
                pltpu.VMEM((BLK, HD), BF16),
                pltpu.VMEM((BLK, HD), BF16),
                pltpu.VMEM((BLK, 128), F32),
                pltpu.VMEM((nresp, 16, 128), F32),
                pltpu.VMEM((2 * QW, HD), BF16),
                pltpu.VMEM((2 * QW, HD), BF16),
                pltpu.VMEM((HD, 2 * QW), BF16),
                pltpu.VMEM((HD, 2 * QW), BF16),
                pltpu.VMEM((nctx * BLK, 2 * QW), BF16),
                pltpu.VMEM((BLK, QW), BF16),
                pltpu.VMEM((nctx + 1, 8, 2 * QW), F32),
                pltpu.VMEM((8, 2 * QW), F32),
                pltpu.VMEM((8, 2 * QW), F32),
                pltpu.VMEM((1, 2 * QW), F32),
                pltpu.VMEM((HD, 2 * QW), F32),
                pltpu.VMEM((CK, 2 * QW), BF16),
                pltpu.VMEM((CK, 2 * QW), BF16),
                pltpu.VMEM((CK, BLK), F32),
                pltpu.VMEM((NZ, 2, 2, 2, BLK, HD), F32),
                pltpu.VMEM((NZ, 2, 2, BLK, HD), F32),
                pltpu.VMEM((NZ, 2, BLK, HD), F32),
                pltpu.VMEM((NZ, 2, BLK, HD), BF16),
                pltpu.VMEM((NZ, 2, BLK, HD), BF16),
                pltpu.VMEM((NZ, 2, BLK, HD), BF16),
                pltpu.VMEM((NZ, 2, BLK, HD), BF16),
                pltpu.VMEM((BLK, QW), BF16),
                pltpu.VMEM((BLK, HD), BF16),
                pltpu.VMEM((BLK, HD), BF16),
                pltpu.VMEM((BLK, QW), BF16),
                pltpu.VMEM((2, BLK, HD), BF16),
                dma((2,)), dma((NZ, 2)), dma((NZ,)),
                dma((2,)), dma((NZ, 2)), dma((NZ,)),
                dma((5,)), dma((5,)),
                dma((3,)), dma((NZ,)), dma((NZ,)), dma((1,)),
                dma((3,)), dma((3,)),
                dma((21,)),
            ],
            compiler_params=pltpu.CompilerParams(
                collective_id=0, has_side_effects=True, vmem_limit_bytes=60 * 1024 * 1024
            ),
            name="attn_bwd",
        )(
            lengths, resp_row, block_index,
            prompt_q, prompt_k, prompt_v, prompt_out, prompt_dout,
            resp_q, resp_k, resp_v, resp_out, resp_dout,
        )
        return pl.pallas_call(
            settle,
            out_shape=tuple(shape(part.shape, part.dtype) for part in parts),
            in_specs=[vmem] * 6,
            out_specs=(vmem,) * 6,
            compiler_params=pltpu.CompilerParams(vmem_limit_bytes=60 * 1024 * 1024),
            name="settle",
        )(*parts)

    heads, rows, whole = P("ctx", "resp"), P(("ctx", "resp"), None), P()
    return jax.shard_map(
        body,
        mesh=mesh,
        in_specs=(heads,) * 5 + (rows,) * 5 + (whole,) * 3,
        out_specs=(heads,) * 3 + (rows,) * 3,
        check_vma=False,
    )
```

```python
import functools

import jax
import jax.numpy as jnp
from jax import lax
from jax.experimental import pallas as pl
from jax.experimental.pallas import tpu as pltpu
from jax.sharding import PartitionSpec as P

MESH = pl.DeviceIdType.MESH
F32, BF16 = jnp.float32, jnp.bfloat16
HD = 128
GROUP = 8
BLK = 128
NZ = 8
QW = GROUP * BLK
CK = 4 * BLK
QT = 512
GT = 1024
SCALE = HD ** -0.5
EXP_SCALE = SCALE * 1.4426950408889634
LOW = -1e30
NEG = float("-inf")
DEAD = 1 << 20


def dot(a, b):
    return jnp.dot(a, b, preferred_element_type=F32)


def kernel(
    nresp,
    len_any, row_any, bi_any,
    pq, pk, pv, pout, pdo, sq, sk, sv, sout, sdo,
    dqp, dkp, dvp, dqr, dkr, dvr,
    len_ref, row_ref, bi_ref,
    kk, vv, lq, lout, ldo, tout, tdo, rq, rdo, rk, rv, rdel, dbuf,
    qa, doa, qT, doT, pt, own_pt, mh, mrun, lrun, delta, dqT, psc, dssc, bias,
    gpart, grecv, kept, ysb, yrb, zsb, zrb, dqrows, dkrows, dvrows, dqloc, dkvloc,
    kx, kzr, kcr, vx, vzr, vcr, as_, ar_, gs, gcr, gyr, gzr, bs_, br_, loc,
):
    c = lax.axis_index("ctx")
    r = lax.axis_index("resp")
    z = c // 4
    lane4 = c % 4
    core = c % 2
    ylo = lane4 // 2
    cpart = c + 1 - 2 * core
    ystep = 2 - 4 * ylo
    ypart = c + ystep

    def zpeer(d):
        return lax.rem(z + d, NZ) * 4 + lane4

    def rpeer(d):
        return lax.rem(r + d, nresp)

    def remote(src, dst, ss, rs, dev):
        return pltpu.make_async_remote_copy(
            src_ref=src, dst_ref=dst, send_sem=ss, recv_sem=rs, device_id=dev, device_id_type=MESH
        )

    def got(part, sem):
        remote(part, part, sem, sem, (cpart, r)).wait_recv()

    def sent(part, sem):
        remote(part, part, sem, sem, (cpart, r)).wait_send()

    def zoff(i):
        return jnp.where(i % 2 == 1, (i + 1) // 2, (NZ - i // 2) % NZ)

    def order(j):
        return jnp.where(j < 3, j + 1, jnp.where(j < 6, j + 2, jnp.where(j < 7, 4, 0)))

    def cols(ref, p, w):
        return ref.at[:, pl.ds(pl.multiple_of(p * w, 128), w)]

    def slots(ref, p):
        return ref.at[pl.ds(pl.multiple_of(p * 16, 16), 16), :]

    pairs = (
        lambda: (pk, kk.at[c]),
        lambda: (pv, vv.at[c]),
        lambda: (pq, lq),
        lambda: (pdo, ldo),
        lambda: (sdo, tdo),
        lambda: (sout, tout),
        lambda: (pout, lout),
        lambda: (cols(sq, r, QW), slots(rq, r)),
        lambda: (cols(sdo, r, QW), slots(rdo, r)),
        lambda: (cols(sk, r, HD), slots(rk, r)),
        lambda: (cols(sv, r, HD), slots(rv, r)),
        lambda: (dbuf.at[r], slots(rdel, r)),
        lambda: (dqloc, dqp),
        lambda: (dkvloc.at[0], dkp),
        lambda: (dkvloc.at[1], dvp),
        lambda: (slots(dqrows, r), cols(dqr, r, QW)),
        lambda: (slots(dkrows, r), cols(dkr, r, HD)),
        lambda: (slots(dvrows, r), cols(dvr, r, HD)),
        lambda: (len_any, len_ref),
        lambda: (row_any, row_ref),
        lambda: (bi_any, bi_ref),
    )

    def local(n):
        src, dst = pairs[n]()
        return pltpu.make_async_copy(src, dst, loc.at[n])

    for n in (*range(11), 18, 19, 20):
        local(n).start()

    barrier = pltpu.get_barrier_semaphore()

    def greet(dev):
        pl.semaphore_signal(barrier, inc=1, device_id=dev, device_id_type=MESH)

    def greet_z(d, carry):
        greet((zpeer(d), r))
        return carry

    def greet_r(d, carry):
        greet((c, rpeer(d)))
        return carry

    lax.fori_loop(1, NZ, greet_z, 0)
    greet((cpart, r))
    greet((ypart, r))
    lax.fori_loop(1, nresp, greet_r, 0)
    pl.semaphore_wait(barrier, (NZ - 1) + (nresp - 1) + 2)

    ksems = (kk, kx, kzr, kcr)
    vsems = (vv, vx, vzr, vcr)

    def swap(sems):
        ref, x, zr, cr = sems
        return remote(ref.at[c], ref.at[c], x.at[0], x.at[1], (ypart, r))

    def swap_wait(sems):
        ref, x, zr, cr = sems
        got(ref.at[ypart], x.at[1])

    def hop(sems, d, e, far):
        ref, x, zr, cr = sems
        b = zpeer(d) + far * ystep
        to = (zpeer(lax.rem(d - e + NZ, NZ)), r)
        return remote(ref.at[b], ref.at[b], x.at[0], zr.at[e, far], to)

    def hop_wait(sems, d, far):
        ref, x, zr, cr = sems
        got(ref.at[zpeer(d) + far * ystep], zr.at[d, far])

    def share(sems, d, far):
        ref, x, zr, cr = sems
        b = zpeer(d) + far * ystep
        return remote(ref.at[b], ref.at[b], x.at[0], cr.at[d], (cpart, r))

    def share_wait(sems, d):
        ref, x, zr, cr = sems
        got(ref.at[pl.ds(lax.rem(z + d, NZ) * 4, 2)], cr.at[d])

    def begin(sems, far):
        for e in (1, NZ - 1, 2, NZ - 2):
            hop(sems, 0, e, far).start()
        share(sems, 0, far).start()

    def arrived(sems, i):
        d = zoff(i)
        for far in range(2):
            hop_wait(sems, d, far)
            share(sems, d, far).start()

    def relay(sems, d, e):
        for far in range(2):
            hop_wait(sems, d, far)
            hop(sems, d, e, far).start()
        hop(sems, d, NZ // 2, d // (NZ // 2)).start()
        for far in range(2):
            share(sems, d, far).start()

    def drain_gather(sems):
        ref, x, zr, cr = sems
        sent(ref.at[pl.ds(0, 4 * NZ - 1)], x.at[0])

    def sources(p):
        return (cols(sq, p, QW), cols(sdo, p, QW), cols(sk, p, HD), cols(sv, p, HD), dbuf.at[p])

    landings = (rq, rdo, rk, rv, rdel)

    def exchange(d, which):
        p = rpeer(d)
        src = sources(p)
        return [
            remote(src[n], slots(landings[n], r), as_.at[n], ar_.at[n], (c, p))
            for n in which
        ]

    def send_rows(n, carry):
        for cp in exchange(n, range(4)):
            cp.start()
        return carry

    local(0).wait()
    swap(ksems).start()
    begin(ksems, 0)
    local(1).wait()
    swap(vsems).start()
    swap_wait(ksems)
    begin(ksems, 1)
    lax.fori_loop(1, nresp, send_rows, 0)

    lane = lax.broadcasted_iota(jnp.int32, (128, 128), 1)
    subl = lax.broadcasted_iota(jnp.int32, (128, 128), 0)
    diff = lane - subl
    for n in (18, 19, 20):
        local(n).wait()
    my = bi_ref[c]

    def load_queries(q, do, base):
        for h in range(GROUP):
            sl = slice(h * HD, (h + 1) * HD)
            out = slice(base + h * BLK, base + (h + 1) * BLK)
            qh, dh = q[:, sl], do[:, sl]
            qa[out, :] = qh
            doa[out, :] = dh
            qT[:, out] = qh.T
            doT[:, out] = dh.T

    def place_delta(rows, base):
        rows_t = rows.T
        for h in range(GROUP):
            delta[:, base + h * BLK: base + (h + 1) * BLK] = rows_t[h:h + 1, :]

    local(2).wait()
    local(3).wait()
    load_queries(lq, ldo, 0)
    mrun[...] = jnp.full((8, 2 * QW), LOW, F32)
    lrun[...] = jnp.zeros((8, 2 * QW), F32)

    local(4).wait()
    local(5).wait()
    lane16 = lax.broadcasted_iota(jnp.int32, (16, 128), 1)
    for g in range(nresp):
        acc = jnp.zeros((16, 128), F32)
        for h in range(GROUP):
            sl = slice((g * GROUP + h) * HD, (g * GROUP + h + 1) * HD)
            prod = tout[:, sl].astype(F32) * tdo[:, sl].astype(F32)
            acc = jnp.where(lane16 == h, jnp.sum(prod, axis=1, keepdims=True), acc)
        dbuf[g] = acc

    def send_delta(d, carry):
        exchange(d, (4,))[0].start()
        return carry

    lax.fori_loop(1, nresp, send_delta, 0)
    local(11).start()

    def merge(p3, m, mo, sl):
        mrun[:, sl] = m
        lrun[:, sl] = lrun[:, sl] * jnp.exp2((mo - m) * EXP_SCALE) + jnp.sum(p3, axis=0)

    def stats_chunk(i, base, masked):
        zc = lax.rem(z + zoff(i), NZ)
        if masked:
            for b in range(4):
                ahead = (bi_ref[zc * 4 + b] - my) * BLK
                bias[b * BLK:(b + 1) * BLK, :] = jnp.where(diff >= ahead, 0.0, NEG)
        for t in range(QW // QT):
            sl = slice(base + t * QT, base + (t + 1) * QT)
            for b in range(4):
                s = dot(kk[zc * 4 + b], qT[:, sl])
                if masked:
                    s = s + jnp.concatenate([bias[b * BLK:(b + 1) * BLK, :]] * (QT // BLK), axis=1)
                s3 = s.reshape(BLK // 8, 8, QT)
                mo = mrun[:, sl]
                m = jnp.maximum(mo, jnp.max(s3, axis=0))
                p3 = jnp.exp2((s3 - m[None]) * EXP_SCALE)
                prow = pl.ds(pl.multiple_of(i * CK + b * BLK, BLK), BLK)
                pt[prow, sl] = p3.reshape(BLK, QT).astype(BF16)
                mh[i * 4 + b, :, sl] = m
                merge(p3, m, mo, sl)

    def prompt_stats(i, carry):
        @pl.when(i == 1)
        def _():
            relay(ksems, 2, 3)
            relay(ksems, NZ - 2, NZ - 3)
            begin(vsems, 0)
            arrived(ksems, 1)
            arrived(ksems, 2)

        @pl.when(i == 3)
        def _():
            swap_wait(vsems)
            begin(vsems, 1)

        d = zoff(i)
        share_wait(ksems, d)
        stats_chunk(i, 0, True)
        return carry

    lax.fori_loop(0, 5, prompt_stats, 0)

    local(6).wait()
    acc = jnp.zeros((BLK, 128), F32)
    for h in range(GROUP):
        sl = slice(h * HD, (h + 1) * HD)
        prod = lout[:, sl].astype(F32) * ldo[:, sl].astype(F32)
        acc = jnp.where(lane == h, jnp.sum(prod, axis=1, keepdims=True), acc)
    place_delta(acc, 0)

    others = 16 * (nresp - 1)
    for n in range(5):
        got(landings[n].at[pl.ds(0, others), :], ar_.at[n])
    for n in range(7, 12):
        local(n).wait()
    load_queries(rq, rdo, QW)
    place_delta(rdel[...], QW)

    lane1 = lax.broadcasted_iota(jnp.int32, (1, 128), 1)
    startq = jnp.full((1, 128), DEAD, jnp.int32)
    cum = jnp.int32(0)
    for n in range(len_ref.shape[0]):
        count = jnp.where(row_ref[n] == c, len_ref[n], 0)
        startq = jnp.where((lane1 >= cum) & (lane1 < cum + count), cum, startq)
        cum = cum + count
    live = jnp.where(startq < DEAD, 1.0, 0.0)
    own_mask = (subl >= startq) & (diff >= 0)
    for h in range(GROUP):
        sl = slice(QW + h * BLK, QW + (h + 1) * BLK)
        s3 = jnp.where(own_mask, dot(rk[...], qT[:, sl]), NEG).reshape(BLK // 8, 8, BLK)
        mo = mrun[:, sl]
        m = jnp.maximum(mo, jnp.max(s3, axis=0))
        p3 = jnp.exp2((s3 - m[None]) * EXP_SCALE)
        own_pt[:, h * BLK:(h + 1) * BLK] = p3.reshape(BLK, BLK).astype(BF16)
        mh[4 * NZ, :, sl] = m
        merge(p3, m, mo, sl)

    def resp_stats(i, carry):
        stats_chunk(i, QW, False)
        return carry

    lax.fori_loop(0, 5, resp_stats, 0)
    for n in range(5, NZ):
        arrived(ksems, n)
    relay(vsems, 2, 3)
    relay(vsems, NZ - 2, NZ - 3)

    def late_stats(i, carry):
        @pl.when(i == NZ - 1)
        def _():
            arrived(vsems, 1)
            arrived(vsems, 2)

        d = zoff(i)
        share_wait(ksems, d)
        stats_chunk(i, 0, True)
        stats_chunk(i, QW, False)
        return carry

    lax.fori_loop(5, NZ, late_stats, 0)

    peak = jnp.max(mrun[...], axis=0, keepdims=True)
    total = jnp.sum(lrun[...] * jnp.exp2((mrun[...] - peak) * EXP_SCALE), axis=0, keepdims=True)
    inv = jnp.where(total > 0.0, 1.0 / total, 0.0)
    inv = inv * jnp.concatenate([jnp.ones((1, QW), F32)] + [live] * GROUP, axis=1)
    for n in range(4 * NZ):
        mh[n] = jnp.exp2((mh[n] - peak) * EXP_SCALE) * inv
    own_f = jnp.exp2((mh[4 * NZ, :, QW:] - peak[:, QW:]) * EXP_SCALE) * inv[:, QW:]
    dqT[...] = jnp.zeros_like(dqT)

    def back(d, which):
        p = rpeer(d)
        dev = (c, p)
        out = (
            lambda: remote(slots(dqrows, p), cols(dqr, r, QW), bs_.at[0], br_.at[0], dev),
            lambda: remote(slots(dkrows, p), cols(dkr, r, HD), bs_.at[1], br_.at[1], dev),
            lambda: remote(slots(dvrows, p), cols(dvr, r, HD), bs_.at[2], br_.at[2], dev),
        )
        return [out[n]() for n in which]

    rkT = rk[...].T
    for h in range(GROUP):
        sl = slice(QW + h * BLK, QW + (h + 1) * BLK)
        hs = slice(h * BLK, (h + 1) * BLK)
        dp = dot(rv[...], doT[:, sl])
        p3 = own_pt[:, hs].astype(F32).reshape(BLK // 8, 8, BLK) * own_f[:, hs][None]
        p = p3.reshape(BLK, BLK)
        ds = (p * (dp - delta[:, sl])).astype(BF16)
        psc[0:BLK, sl] = p.astype(BF16)
        dssc[0:BLK, sl] = ds
        dqT[:, sl] += dot(rkT, ds)
    dvrows[...] = dot(psc[0:BLK, QW:], doa[QW:, :]).astype(BF16)
    dkrows[...] = (dot(dssc[0:BLK, QW:], qa[QW:, :]) * SCALE).astype(BF16)

    def send_back_kv(d, carry):
        for cp in back(d, (1, 2)):
            cp.start()
        return carry

    lax.fori_loop(1, nresp, send_back_kv, 0)
    local(16).start()
    local(17).start()

    def core_send(j):
        return remote(gpart.at[j, 1 - core], grecv.at[j], gs.at[0], gcr.at[j], (cpart, r))

    def y_send(j):
        return remote(ysb.at[j], yrb.at[j], gs.at[1], gyr.at[j], (ypart, r))

    def z_send(j):
        d = zoff(order(j))
        return remote(zsb.at[j], zrb.at[NZ - d], gs.at[2], gzr.at[0], (zpeer(d), r))

    def after_core(j):
        core_send(j).wait_recv()
        kept[j] = gpart[j, core, ylo] + grecv[j, ylo]
        ysb[j] = (gpart[j, core, 1 - ylo] + grecv[j, 1 - ylo]).astype(BF16)
        y_send(j).start()

    def after_y(j):
        y_send(j).wait_recv()
        zsb[j] = (kept[j] + yrb[j].astype(F32)).astype(BF16)
        z_send(j).start()

    def grads(j, last):
        i = order(j)
        d = zoff(i)
        zc = lax.rem(z + d, NZ)

        if not last:
            @pl.when(j == 2)
            def _():
                for n in range(5, NZ):
                    arrived(vsems, n)

        share_wait(vsems, d)
        vc_rows = vv[pl.ds(zc * 4, 4)].reshape(CK, HD)
        kTc = kk[pl.ds(zc * 4, 4)].reshape(CK, HD).T
        prow = pl.ds(pl.multiple_of(i * CK, CK), CK)
        for t in range(2 * QW // GT):
            sl = slice(t * GT, (t + 1) * GT)
            dp = dot(vc_rows, doT[:, sl])
            f = mh[pl.ds(i * 4, 4), :, sl][:, None]
            p = (pt[prow, sl].astype(F32).reshape(4, BLK // 8, 8, GT) * f).reshape(CK, GT)
            ds = (p * (dp - delta[:, sl])).astype(BF16)
            psc[:, sl] = p.astype(BF16)
            dssc[:, sl] = ds
            dqT[:, sl] += dot(kTc, ds)
        if last:
            after_core(j - 1)
        dk = dot(dssc[...], qa[...])
        dv = dot(psc[...], doa[...])
        for b in range(4):
            gpart[j, b % 2, b // 2, 0] = dk[b * BLK:(b + 1) * BLK, :]
            gpart[j, b % 2, b // 2, 1] = dv[b * BLK:(b + 1) * BLK, :]
        core_send(j).start()
        if last:
            after_y(j - 2)
            return

        @pl.when(j >= 1)
        def _():
            after_core(j - 1)

        @pl.when(j >= 2)
        def _():
            after_y(j - 2)

    def grads_step(j, carry):
        grads(j, False)
        return carry

    lax.fori_loop(0, NZ - 1, grads_step, 0)
    grads(NZ - 1, True)

    for h in range(GROUP):
        dqrows[:, h * HD:(h + 1) * HD] = (dqT[:, QW + h * BLK:QW + (h + 1) * BLK].T * SCALE).astype(BF16)

    def send_back_q(d, carry):
        for cp in back(d, (0,)):
            cp.start()
        return carry

    lax.fori_loop(1, nresp, send_back_q, 0)
    local(15).start()

    after_core(NZ - 1)
    after_y(NZ - 2)
    for h in range(GROUP):
        dqloc[:, h * HD:(h + 1) * HD] = (dqT[:, h * BLK:(h + 1) * BLK].T * SCALE).astype(BF16)
    local(12).start()
    y_send(NZ - 1).wait_recv()
    kept[NZ - 1] = kept[NZ - 1] + yrb[NZ - 1].astype(F32)

    got(zrb.at[pl.ds(0, NZ - 1)], gzr.at[0])
    total_kv = kept[NZ - 1]
    for n in range(1, NZ):
        total_kv = total_kv + zrb[n].astype(F32)
    dkvloc[0] = (total_kv[0] * SCALE).astype(BF16)
    dkvloc[1] = total_kv[1].astype(BF16)
    local(13).start()
    local(14).start()
    drain_gather(ksems)
    drain_gather(vsems)
    for n in range(5):
        sent(landings[n].at[pl.ds(0, others), :], as_.at[n])
    sent(grecv, gs.at[0])
    sent(ysb, gs.at[1])
    sent(zsb.at[pl.ds(0, NZ - 1)], gs.at[2])
    for n, (rows, part) in enumerate(((dqrows, dqr), (dkrows, dkr), (dvrows, dvr))):
        sent(rows.at[pl.ds(0, others), :], bs_.at[n])
        got(part.at[:, pl.ds(0, part.shape[1] * (nresp - 1) // nresp)], br_.at[n])
    for n in range(12, 18):
        local(n).wait()


def settle(*refs):
    n = len(refs) // 2
    for src, dst in zip(refs[:n], refs[n:]):
        dst[...] = src[...]


def solution(mesh):
    nresp = mesh.shape["resp"]
    nctx = mesh.shape["ctx"]

    def body(
        prompt_q, prompt_k, prompt_v, prompt_out, prompt_dout,
        resp_q, resp_k, resp_v, resp_out, resp_dout,
        lengths, resp_row, block_index,
    ):
        shape = jax.ShapeDtypeStruct
        vmem = pl.BlockSpec(memory_space=pltpu.VMEM)
        dma = pltpu.SemaphoreType.DMA
        anywhere = pl.BlockSpec(memory_space=pl.ANY)
        parts = pl.pallas_call(
            functools.partial(kernel, nresp),
            out_shape=(
                shape(prompt_q.shape, BF16),
                shape(prompt_k.shape, BF16),
                shape(prompt_v.shape, BF16),
                shape(resp_q.shape, BF16),
                shape(resp_k.shape, BF16),
                shape(resp_v.shape, BF16),
            ),
            in_specs=[anywhere] * 13,
            out_specs=(anywhere,) * 6,
            scratch_shapes=[
                pltpu.SMEM(lengths.shape, jnp.int32),
                pltpu.SMEM(resp_row.shape, jnp.int32),
                pltpu.SMEM(block_index.shape, jnp.int32),
                pltpu.VMEM((nctx, BLK, HD), BF16),
                pltpu.VMEM((nctx, BLK, HD), BF16),
                pltpu.VMEM((BLK, QW), BF16),
                pltpu.VMEM((BLK, QW), BF16),
                pltpu.VMEM((BLK, QW), BF16),
                pltpu.VMEM(resp_out.shape, BF16),
                pltpu.VMEM(resp_out.shape, BF16),
                pltpu.VMEM((BLK, QW), BF16),
                pltpu.VMEM((BLK, QW), BF16),
                pltpu.VMEM((BLK, HD), BF16),
                pltpu.VMEM((BLK, HD), BF16),
                pltpu.VMEM((BLK, 128), F32),
                pltpu.VMEM((nresp, 16, 128), F32),
                pltpu.VMEM((2 * QW, HD), BF16),
                pltpu.VMEM((2 * QW, HD), BF16),
                pltpu.VMEM((HD, 2 * QW), BF16),
                pltpu.VMEM((HD, 2 * QW), BF16),
                pltpu.VMEM((nctx * BLK, 2 * QW), BF16),
                pltpu.VMEM((BLK, QW), BF16),
                pltpu.VMEM((nctx + 1, 8, 2 * QW), F32),
                pltpu.VMEM((8, 2 * QW), F32),
                pltpu.VMEM((8, 2 * QW), F32),
                pltpu.VMEM((1, 2 * QW), F32),
                pltpu.VMEM((HD, 2 * QW), F32),
                pltpu.VMEM((CK, 2 * QW), BF16),
                pltpu.VMEM((CK, 2 * QW), BF16),
                pltpu.VMEM((CK, BLK), F32),
                pltpu.VMEM((NZ, 2, 2, 2, BLK, HD), F32),
                pltpu.VMEM((NZ, 2, 2, BLK, HD), F32),
                pltpu.VMEM((NZ, 2, BLK, HD), F32),
                pltpu.VMEM((NZ, 2, BLK, HD), BF16),
                pltpu.VMEM((NZ, 2, BLK, HD), BF16),
                pltpu.VMEM((NZ, 2, BLK, HD), BF16),
                pltpu.VMEM((NZ, 2, BLK, HD), BF16),
                pltpu.VMEM((BLK, QW), BF16),
                pltpu.VMEM((BLK, HD), BF16),
                pltpu.VMEM((BLK, HD), BF16),
                pltpu.VMEM((BLK, QW), BF16),
                pltpu.VMEM((2, BLK, HD), BF16),
                dma((2,)), dma((NZ, 2)), dma((NZ,)),
                dma((2,)), dma((NZ, 2)), dma((NZ,)),
                dma((5,)), dma((5,)),
                dma((3,)), dma((NZ,)), dma((NZ,)), dma((1,)),
                dma((3,)), dma((3,)),
                dma((21,)),
            ],
            compiler_params=pltpu.CompilerParams(
                collective_id=0, has_side_effects=True, vmem_limit_bytes=60 * 1024 * 1024
            ),
            name="attn_bwd",
        )(
            lengths, resp_row, block_index,
            prompt_q, prompt_k, prompt_v, prompt_out, prompt_dout,
            resp_q, resp_k, resp_v, resp_out, resp_dout,
        )
        return pl.pallas_call(
            settle,
            out_shape=tuple(shape(part.shape, part.dtype) for part in parts),
            in_specs=[vmem] * 6,
            out_specs=(vmem,) * 6,
            compiler_params=pltpu.CompilerParams(vmem_limit_bytes=60 * 1024 * 1024),
            name="settle",
        )(*parts)

    heads, rows, whole = P("ctx", "resp"), P(("ctx", "resp"), None), P()
    return jax.shard_map(
        body,
        mesh=mesh,
        in_specs=(heads,) * 5 + (rows,) * 5 + (whole,) * 3,
        out_specs=(heads,) * 3 + (rows,) * 3,
        check_vma=False,
    )
```

```python
import functools

import jax
import jax.numpy as jnp
from jax import lax
from jax.experimental import pallas as pl
from jax.experimental.pallas import tpu as pltpu
from jax.sharding import PartitionSpec as P

MESH = pl.DeviceIdType.MESH
F32, BF16 = jnp.float32, jnp.bfloat16
HD = 128
GROUP = 8
BLK = 128
NZ = 8
QW = GROUP * BLK
CK = 4 * BLK
QT = 512
GT = 1024
SCALE = HD ** -0.5
EXP_SCALE = SCALE * 1.4426950408889634
LOW = -1e30
NEG = float("-inf")
DEAD = 1 << 20


def dot(a, b):
    return jnp.dot(a, b, preferred_element_type=F32)


def kernel(
    nresp,
    len_any, row_any, bi_any,
    pq, pk, pv, pout, pdo, sq, sk, sv, sout, sdo,
    dqp, dkp, dvp, dqr, dkr, dvr,
    len_ref, row_ref, bi_ref,
    kk, vv, lq, lout, ldo, tout, tdo, rq, rdo, rk, rv, rdel, dbuf,
    qa, doa, qT, doT, pt, own_pt, mh, mrun, lrun, delta, dqT, psc, dssc, bias,
    gpart, grecv, kept, ysb, yrb, zsb, zrb, dqrows, dkrows, dvrows, dqloc, dkvloc,
    kx, kzr, kcr, vx, vzr, vcr, as_, ar_, gs, gcr, gyr, gzr, bs_, br_, loc,
):
    c = lax.axis_index("ctx")
    r = lax.axis_index("resp")
    z = c // 4
    lane4 = c % 4
    core = c % 2
    ylo = lane4 // 2
    cpart = c + 1 - 2 * core
    ystep = 2 - 4 * ylo
    ypart = c + ystep

    def zpeer(d):
        return lax.rem(z + d, NZ) * 4 + lane4

    def rpeer(d):
        return lax.rem(r + d, nresp)

    def remote(src, dst, ss, rs, dev):
        return pltpu.make_async_remote_copy(
            src_ref=src, dst_ref=dst, send_sem=ss, recv_sem=rs, device_id=dev, device_id_type=MESH
        )

    def got(part, sem):
        remote(part, part, sem, sem, (cpart, r)).wait_recv()

    def sent(part, sem):
        remote(part, part, sem, sem, (cpart, r)).wait_send()

    def zoff(i):
        return jnp.where(i % 2 == 1, (i + 1) // 2, (NZ - i // 2) % NZ)

    def order(j):
        return jnp.where(j < 3, j + 1, jnp.where(j < 6, j + 2, jnp.where(j < 7, 4, 0)))

    def cols(ref, p, w):
        return ref.at[:, pl.ds(pl.multiple_of(p * w, 128), w)]

    def slots(ref, p):
        return ref.at[pl.ds(pl.multiple_of(p * 16, 16), 16), :]

    pairs = (
        lambda: (pk, kk.at[c]),
        lambda: (pv, vv.at[c]),
        lambda: (pq, lq),
        lambda: (pdo, ldo),
        lambda: (sdo, tdo),
        lambda: (sout, tout),
        lambda: (pout, lout),
        lambda: (cols(sq, r, QW), slots(rq, r)),
        lambda: (cols(sdo, r, QW), slots(rdo, r)),
        lambda: (cols(sk, r, HD), slots(rk, r)),
        lambda: (cols(sv, r, HD), slots(rv, r)),
        lambda: (dbuf.at[r], slots(rdel, r)),
        lambda: (dqloc, dqp),
        lambda: (dkvloc.at[0], dkp),
        lambda: (dkvloc.at[1], dvp),
        lambda: (slots(dqrows, r), cols(dqr, r, QW)),
        lambda: (slots(dkrows, r), cols(dkr, r, HD)),
        lambda: (slots(dvrows, r), cols(dvr, r, HD)),
        lambda: (len_any, len_ref),
        lambda: (row_any, row_ref),
        lambda: (bi_any, bi_ref),
    )

    def local(n):
        src, dst = pairs[n]()
        return pltpu.make_async_copy(src, dst, loc.at[n])

    for n in (*range(11), 18, 19, 20):
        local(n).start()

    barrier = pltpu.get_barrier_semaphore()

    def greet(dev):
        pl.semaphore_signal(barrier, inc=1, device_id=dev, device_id_type=MESH)

    def greet_z(d, carry):
        greet((zpeer(d), r))
        return carry

    def greet_r(d, carry):
        greet((c, rpeer(d)))
        return carry

    lax.fori_loop(1, NZ, greet_z, 0)
    greet((cpart, r))
    greet((ypart, r))
    lax.fori_loop(1, nresp, greet_r, 0)
    pl.semaphore_wait(barrier, (NZ - 1) + (nresp - 1) + 2)

    ksems = (kk, kx, kzr, kcr)
    vsems = (vv, vx, vzr, vcr)

    def swap(sems):
        ref, x, zr, cr = sems
        return remote(ref.at[c], ref.at[c], x.at[0], x.at[1], (ypart, r))

    def swap_wait(sems):
        ref, x, zr, cr = sems
        got(ref.at[ypart], x.at[1])

    def hop(sems, d, e, far):
        ref, x, zr, cr = sems
        b = zpeer(d) + far * ystep
        to = (zpeer(lax.rem(d - e + NZ, NZ)), r)
        return remote(ref.at[b], ref.at[b], x.at[0], zr.at[e, far], to)

    def hop_wait(sems, d, far):
        ref, x, zr, cr = sems
        got(ref.at[zpeer(d) + far * ystep], zr.at[d, far])

    def share(sems, d, far):
        ref, x, zr, cr = sems
        b = zpeer(d) + far * ystep
        return remote(ref.at[b], ref.at[b], x.at[0], cr.at[d], (cpart, r))

    def share_wait(sems, d):
        ref, x, zr, cr = sems
        got(ref.at[pl.ds(lax.rem(z + d, NZ) * 4, 2)], cr.at[d])

    def begin(sems, far):
        for e in (1, NZ - 1, 2, NZ - 2):
            hop(sems, 0, e, far).start()
        share(sems, 0, far).start()

    def arrived(sems, i):
        d = zoff(i)
        for far in range(2):
            hop_wait(sems, d, far)
            share(sems, d, far).start()

    def relay(sems, d, e):
        for far in range(2):
            hop_wait(sems, d, far)
            hop(sems, d, e, far).start()
        hop(sems, d, NZ // 2, d // (NZ // 2)).start()
        for far in range(2):
            share(sems, d, far).start()

    def drain_gather(sems):
        ref, x, zr, cr = sems
        sent(ref.at[pl.ds(0, 4 * NZ - 1)], x.at[0])

    def sources(p):
        return (cols(sq, p, QW), cols(sdo, p, QW), cols(sk, p, HD), cols(sv, p, HD), dbuf.at[p])

    landings = (rq, rdo, rk, rv, rdel)

    def exchange(d, which):
        p = rpeer(d)
        src = sources(p)
        return [
            remote(src[n], slots(landings[n], r), as_.at[n], ar_.at[n], (c, p))
            for n in which
        ]

    def send_rows(n, carry):
        for cp in exchange(n, range(4)):
            cp.start()
        return carry

    local(0).wait()
    swap(ksems).start()
    begin(ksems, 0)
    local(1).wait()
    swap(vsems).start()
    swap_wait(ksems)
    begin(ksems, 1)
    lax.fori_loop(1, nresp, send_rows, 0)

    lane = lax.broadcasted_iota(jnp.int32, (128, 128), 1)
    subl = lax.broadcasted_iota(jnp.int32, (128, 128), 0)
    diff = lane - subl
    for n in (18, 19, 20):
        local(n).wait()
    my = bi_ref[c]

    def load_queries(q, do, base):
        for h in range(GROUP):
            sl = slice(h * HD, (h + 1) * HD)
            out = slice(base + h * BLK, base + (h + 1) * BLK)
            qh, dh = q[:, sl], do[:, sl]
            qa[out, :] = qh
            doa[out, :] = dh
            qT[:, out] = qh.T
            doT[:, out] = dh.T

    def place_delta(rows, base):
        rows_t = rows.T
        for h in range(GROUP):
            delta[:, base + h * BLK: base + (h + 1) * BLK] = rows_t[h:h + 1, :]

    local(2).wait()
    local(3).wait()
    load_queries(lq, ldo, 0)
    mrun[...] = jnp.full((8, 2 * QW), LOW, F32)
    lrun[...] = jnp.zeros((8, 2 * QW), F32)

    local(4).wait()
    local(5).wait()
    lane16 = lax.broadcasted_iota(jnp.int32, (16, 128), 1)
    for g in range(nresp):
        acc = jnp.zeros((16, 128), F32)
        for h in range(GROUP):
            sl = slice((g * GROUP + h) * HD, (g * GROUP + h + 1) * HD)
            prod = tout[:, sl].astype(F32) * tdo[:, sl].astype(F32)
            acc = jnp.where(lane16 == h, jnp.sum(prod, axis=1, keepdims=True), acc)
        dbuf[g] = acc

    def send_delta(d, carry):
        exchange(d, (4,))[0].start()
        return carry

    lax.fori_loop(1, nresp, send_delta, 0)
    local(11).start()

    def merge(p3, m, mo, sl):
        mrun[:, sl] = m
        lrun[:, sl] = lrun[:, sl] * jnp.exp2((mo - m) * EXP_SCALE) + jnp.sum(p3, axis=0)

    def stats_chunk(i, base, masked):
        zc = lax.rem(z + zoff(i), NZ)
        if masked:
            for b in range(4):
                ahead = (bi_ref[zc * 4 + b] - my) * BLK
                bias[b * BLK:(b + 1) * BLK, :] = jnp.where(diff >= ahead, 0.0, NEG)
        for t in range(QW // QT):
            sl = slice(base + t * QT, base + (t + 1) * QT)
            for b in range(4):
                s = dot(kk[zc * 4 + b], qT[:, sl])
                if masked:
                    s = s + jnp.concatenate([bias[b * BLK:(b + 1) * BLK, :]] * (QT // BLK), axis=1)
                s3 = s.reshape(BLK // 8, 8, QT)
                mo = mrun[:, sl]
                m = jnp.maximum(mo, jnp.max(s3, axis=0))
                p3 = jnp.exp2((s3 - m[None]) * EXP_SCALE)
                prow = pl.ds(pl.multiple_of(i * CK + b * BLK, BLK), BLK)
                pt[prow, sl] = p3.reshape(BLK, QT).astype(BF16)
                mh[i * 4 + b, :, sl] = m
                merge(p3, m, mo, sl)

    def prompt_stats(i, carry):
        @pl.when(i == 1)
        def _():
            relay(ksems, 2, 3)
            relay(ksems, NZ - 2, NZ - 3)
            begin(vsems, 0)
            arrived(ksems, 1)
            arrived(ksems, 2)

        @pl.when(i == 3)
        def _():
            swap_wait(vsems)
            begin(vsems, 1)

        d = zoff(i)
        share_wait(ksems, d)
        stats_chunk(i, 0, True)
        return carry

    lax.fori_loop(0, 5, prompt_stats, 0)

    local(6).wait()
    acc = jnp.zeros((BLK, 128), F32)
    for h in range(GROUP):
        sl = slice(h * HD, (h + 1) * HD)
        prod = lout[:, sl].astype(F32) * ldo[:, sl].astype(F32)
        acc = jnp.where(lane == h, jnp.sum(prod, axis=1, keepdims=True), acc)
    place_delta(acc, 0)

    others = 16 * (nresp - 1)
    for n in range(5):
        got(landings[n].at[pl.ds(0, others), :], ar_.at[n])
    for n in range(7, 12):
        local(n).wait()
    load_queries(rq, rdo, QW)
    place_delta(rdel[...], QW)

    lane1 = lax.broadcasted_iota(jnp.int32, (1, 128), 1)
    startq = jnp.full((1, 128), DEAD, jnp.int32)
    cum = jnp.int32(0)
    for n in range(len_ref.shape[0]):
        count = jnp.where(row_ref[n] == c, len_ref[n], 0)
        startq = jnp.where((lane1 >= cum) & (lane1 < cum + count), cum, startq)
        cum = cum + count
    live = jnp.where(startq < DEAD, 1.0, 0.0)
    own_mask = (subl >= startq) & (diff >= 0)
    for h in range(GROUP):
        sl = slice(QW + h * BLK, QW + (h + 1) * BLK)
        s3 = jnp.where(own_mask, dot(rk[...], qT[:, sl]), NEG).reshape(BLK // 8, 8, BLK)
        mo = mrun[:, sl]
        m = jnp.maximum(mo, jnp.max(s3, axis=0))
        p3 = jnp.exp2((s3 - m[None]) * EXP_SCALE)
        own_pt[:, h * BLK:(h + 1) * BLK] = p3.reshape(BLK, BLK).astype(BF16)
        mh[4 * NZ, :, sl] = m
        merge(p3, m, mo, sl)

    def resp_stats(i, carry):
        stats_chunk(i, QW, False)
        return carry

    lax.fori_loop(0, 5, resp_stats, 0)
    for n in range(5, NZ):
        arrived(ksems, n)
    relay(vsems, 2, 3)
    relay(vsems, NZ - 2, NZ - 3)

    def late_stats(i, carry):
        @pl.when(i == NZ - 1)
        def _():
            arrived(vsems, 1)
            arrived(vsems, 2)

        d = zoff(i)
        share_wait(ksems, d)
        stats_chunk(i, 0, True)
        stats_chunk(i, QW, False)
        return carry

    lax.fori_loop(5, NZ, late_stats, 0)

    peak = jnp.max(mrun[...], axis=0, keepdims=True)
    total = jnp.sum(lrun[...] * jnp.exp2((mrun[...] - peak) * EXP_SCALE), axis=0, keepdims=True)
    inv = jnp.where(total > 0.0, 1.0 / total, 0.0)
    inv = inv * jnp.concatenate([jnp.ones((1, QW), F32)] + [live] * GROUP, axis=1)
    for n in range(4 * NZ):
        mh[n] = jnp.exp2((mh[n] - peak) * EXP_SCALE) * inv
    own_f = jnp.exp2((mh[4 * NZ, :, QW:] - peak[:, QW:]) * EXP_SCALE) * inv[:, QW:]
    dqT[...] = jnp.zeros_like(dqT)

    def back(d, which):
        p = rpeer(d)
        dev = (c, p)
        out = (
            lambda: remote(slots(dqrows, p), cols(dqr, r, QW), bs_.at[0], br_.at[0], dev),
            lambda: remote(slots(dkrows, p), cols(dkr, r, HD), bs_.at[1], br_.at[1], dev),
            lambda: remote(slots(dvrows, p), cols(dvr, r, HD), bs_.at[2], br_.at[2], dev),
        )
        return [out[n]() for n in which]

    rkT = rk[...].T
    for h in range(GROUP):
        sl = slice(QW + h * BLK, QW + (h + 1) * BLK)
        hs = slice(h * BLK, (h + 1) * BLK)
        dp = dot(rv[...], doT[:, sl])
        p3 = own_pt[:, hs].astype(F32).reshape(BLK // 8, 8, BLK) * own_f[:, hs][None]
        p = p3.reshape(BLK, BLK)
        ds = (p * (dp - delta[:, sl])).astype(BF16)
        psc[0:BLK, sl] = p.astype(BF16)
        dssc[0:BLK, sl] = ds
        dqT[:, sl] += dot(rkT, ds)
    dvrows[...] = dot(psc[0:BLK, QW:], doa[QW:, :]).astype(BF16)
    dkrows[...] = (dot(dssc[0:BLK, QW:], qa[QW:, :]) * SCALE).astype(BF16)

    def send_back_kv(d, carry):
        for cp in back(d, (1, 2)):
            cp.start()
        return carry

    lax.fori_loop(1, nresp, send_back_kv, 0)
    local(16).start()
    local(17).start()

    def core_send(j):
        return remote(gpart.at[j, 1 - core], grecv.at[j], gs.at[0], gcr.at[j], (cpart, r))

    def y_send(j):
        return remote(ysb.at[j], yrb.at[j], gs.at[1], gyr.at[j], (ypart, r))

    def z_send(j):
        d = zoff(order(j))
        return remote(zsb.at[j], zrb.at[NZ - d], gs.at[2], gzr.at[0], (zpeer(d), r))

    def after_core(j):
        core_send(j).wait_recv()
        kept[j] = gpart[j, core, ylo] + grecv[j, ylo]
        ysb[j] = (gpart[j, core, 1 - ylo] + grecv[j, 1 - ylo]).astype(BF16)
        y_send(j).start()

    def after_y(j):
        y_send(j).wait_recv()
        zsb[j] = (kept[j] + yrb[j].astype(F32)).astype(BF16)
        z_send(j).start()

    def grads(j, last):
        i = order(j)
        d = zoff(i)
        zc = lax.rem(z + d, NZ)

        if not last:
            @pl.when(j == 2)
            def _():
                for n in range(5, NZ):
                    arrived(vsems, n)

        share_wait(vsems, d)
        vc_rows = vv[pl.ds(zc * 4, 4)].reshape(CK, HD)
        kTc = kk[pl.ds(zc * 4, 4)].reshape(CK, HD).T
        prow = pl.ds(pl.multiple_of(i * CK, CK), CK)
        for t in range(2 * QW // GT):
            sl = slice(t * GT, (t + 1) * GT)
            dp = dot(vc_rows, doT[:, sl])
            f = mh[pl.ds(i * 4, 4), :, sl][:, None]
            p = (pt[prow, sl].astype(F32).reshape(4, BLK // 8, 8, GT) * f).reshape(CK, GT)
            ds = (p * (dp - delta[:, sl])).astype(BF16)
            psc[:, sl] = p.astype(BF16)
            dssc[:, sl] = ds
            dqT[:, sl] += dot(kTc, ds)
        if last:
            after_core(j - 1)
            after_y(j - 3)
        dk = dot(dssc[...], qa[...])
        dv = dot(psc[...], doa[...])
        for b in range(4):
            gpart[j, b % 2, b // 2, 0] = dk[b * BLK:(b + 1) * BLK, :]
            gpart[j, b % 2, b // 2, 1] = dv[b * BLK:(b + 1) * BLK, :]
        core_send(j).start()
        if last:
            after_y(j - 2)
            return

        @pl.when(j >= 1)
        def _():
            after_core(j - 1)

        @pl.when(j >= 3)
        def _():
            after_y(j - 3)

    def grads_step(j, carry):
        grads(j, False)
        return carry

    lax.fori_loop(0, NZ - 1, grads_step, 0)
    grads(NZ - 1, True)

    for h in range(GROUP):
        dqrows[:, h * HD:(h + 1) * HD] = (dqT[:, QW + h * BLK:QW + (h + 1) * BLK].T * SCALE).astype(BF16)

    def send_back_q(d, carry):
        for cp in back(d, (0,)):
            cp.start()
        return carry

    lax.fori_loop(1, nresp, send_back_q, 0)
    local(15).start()

    after_core(NZ - 1)
    after_y(NZ - 2)
    for h in range(GROUP):
        dqloc[:, h * HD:(h + 1) * HD] = (dqT[:, h * BLK:(h + 1) * BLK].T * SCALE).astype(BF16)
    local(12).start()
    y_send(NZ - 1).wait_recv()
    kept[NZ - 1] = kept[NZ - 1] + yrb[NZ - 1].astype(F32)

    got(zrb.at[pl.ds(0, NZ - 1)], gzr.at[0])
    total_kv = kept[NZ - 1]
    for n in range(1, NZ):
        total_kv = total_kv + zrb[n].astype(F32)
    dkvloc[0] = (total_kv[0] * SCALE).astype(BF16)
    dkvloc[1] = total_kv[1].astype(BF16)
    local(13).start()
    local(14).start()
    drain_gather(ksems)
    drain_gather(vsems)
    for n in range(5):
        sent(landings[n].at[pl.ds(0, others), :], as_.at[n])
    sent(grecv, gs.at[0])
    sent(ysb, gs.at[1])
    sent(zsb.at[pl.ds(0, NZ - 1)], gs.at[2])
    for n, (rows, part) in enumerate(((dqrows, dqr), (dkrows, dkr), (dvrows, dvr))):
        sent(rows.at[pl.ds(0, others), :], bs_.at[n])
        got(part.at[:, pl.ds(0, part.shape[1] * (nresp - 1) // nresp)], br_.at[n])
    for n in range(12, 18):
        local(n).wait()


def settle(*refs):
    n = len(refs) // 2
    for src, dst in zip(refs[:n], refs[n:]):
        dst[...] = src[...]


def solution(mesh):
    nresp = mesh.shape["resp"]
    nctx = mesh.shape["ctx"]

    def body(
        prompt_q, prompt_k, prompt_v, prompt_out, prompt_dout,
        resp_q, resp_k, resp_v, resp_out, resp_dout,
        lengths, resp_row, block_index,
    ):
        shape = jax.ShapeDtypeStruct
        vmem = pl.BlockSpec(memory_space=pltpu.VMEM)
        dma = pltpu.SemaphoreType.DMA
        anywhere = pl.BlockSpec(memory_space=pl.ANY)
        parts = pl.pallas_call(
            functools.partial(kernel, nresp),
            out_shape=(
                shape(prompt_q.shape, BF16),
                shape(prompt_k.shape, BF16),
                shape(prompt_v.shape, BF16),
                shape(resp_q.shape, BF16),
                shape(resp_k.shape, BF16),
                shape(resp_v.shape, BF16),
            ),
            in_specs=[anywhere] * 13,
            out_specs=(anywhere,) * 6,
            scratch_shapes=[
                pltpu.SMEM(lengths.shape, jnp.int32),
                pltpu.SMEM(resp_row.shape, jnp.int32),
                pltpu.SMEM(block_index.shape, jnp.int32),
                pltpu.VMEM((nctx, BLK, HD), BF16),
                pltpu.VMEM((nctx, BLK, HD), BF16),
                pltpu.VMEM((BLK, QW), BF16),
                pltpu.VMEM((BLK, QW), BF16),
                pltpu.VMEM((BLK, QW), BF16),
                pltpu.VMEM(resp_out.shape, BF16),
                pltpu.VMEM(resp_out.shape, BF16),
                pltpu.VMEM((BLK, QW), BF16),
                pltpu.VMEM((BLK, QW), BF16),
                pltpu.VMEM((BLK, HD), BF16),
                pltpu.VMEM((BLK, HD), BF16),
                pltpu.VMEM((BLK, 128), F32),
                pltpu.VMEM((nresp, 16, 128), F32),
                pltpu.VMEM((2 * QW, HD), BF16),
                pltpu.VMEM((2 * QW, HD), BF16),
                pltpu.VMEM((HD, 2 * QW), BF16),
                pltpu.VMEM((HD, 2 * QW), BF16),
                pltpu.VMEM((nctx * BLK, 2 * QW), BF16),
                pltpu.VMEM((BLK, QW), BF16),
                pltpu.VMEM((nctx + 1, 8, 2 * QW), F32),
                pltpu.VMEM((8, 2 * QW), F32),
                pltpu.VMEM((8, 2 * QW), F32),
                pltpu.VMEM((1, 2 * QW), F32),
                pltpu.VMEM((HD, 2 * QW), F32),
                pltpu.VMEM((CK, 2 * QW), BF16),
                pltpu.VMEM((CK, 2 * QW), BF16),
                pltpu.VMEM((CK, BLK), F32),
                pltpu.VMEM((NZ, 2, 2, 2, BLK, HD), F32),
                pltpu.VMEM((NZ, 2, 2, BLK, HD), F32),
                pltpu.VMEM((NZ, 2, BLK, HD), F32),
                pltpu.VMEM((NZ, 2, BLK, HD), BF16),
                pltpu.VMEM((NZ, 2, BLK, HD), BF16),
                pltpu.VMEM((NZ, 2, BLK, HD), BF16),
                pltpu.VMEM((NZ, 2, BLK, HD), BF16),
                pltpu.VMEM((BLK, QW), BF16),
                pltpu.VMEM((BLK, HD), BF16),
                pltpu.VMEM((BLK, HD), BF16),
                pltpu.VMEM((BLK, QW), BF16),
                pltpu.VMEM((2, BLK, HD), BF16),
                dma((2,)), dma((NZ, 2)), dma((NZ,)),
                dma((2,)), dma((NZ, 2)), dma((NZ,)),
                dma((5,)), dma((5,)),
                dma((3,)), dma((NZ,)), dma((NZ,)), dma((1,)),
                dma((3,)), dma((3,)),
                dma((21,)),
            ],
            compiler_params=pltpu.CompilerParams(
                collective_id=0, has_side_effects=True, vmem_limit_bytes=60 * 1024 * 1024
            ),
            name="attn_bwd",
        )(
            lengths, resp_row, block_index,
            prompt_q, prompt_k, prompt_v, prompt_out, prompt_dout,
            resp_q, resp_k, resp_v, resp_out, resp_dout,
        )
        return pl.pallas_call(
            settle,
            out_shape=tuple(shape(part.shape, part.dtype) for part in parts),
            in_specs=[vmem] * 6,
            out_specs=(vmem,) * 6,
            compiler_params=pltpu.CompilerParams(vmem_limit_bytes=60 * 1024 * 1024),
            name="settle",
        )(*parts)

    heads, rows, whole = P("ctx", "resp"), P(("ctx", "resp"), None), P()
    return jax.shard_map(
        body,
        mesh=mesh,
        in_specs=(heads,) * 5 + (rows,) * 5 + (whole,) * 3,
        out_specs=(heads,) * 3 + (rows,) * 3,
        check_vma=False,
    )
```
